128 devices in a mesh: dp: 2 (over z_hi), seq: 16 (over z_lo, x, core), tensor: 4 (over y).
Axes of the slice: x: 4, y: 4, z: 4 (z_hi: 2, z_lo: 2; z = z_hi * 2 + z_lo), core: 2. Of those that a mesh axis runs over, the one named last changes fastest.
Arguments:
- queries: bfloat16 [8192, 8192], P(('dp', 'seq'), 'tensor'), parts along dimension 0, may hold values from -8 to 8
- keys: bfloat16 [2048, 8192], P(('dp', 'seq'), 'tensor'), parts along dimension 0, may hold values from -4 to 4
- values: bfloat16 [2048, 8192], P(('dp', 'seq'), 'tensor'), parts along dimension 0, may hold values from -6 to 6
- cotangent: bfloat16 [8192, 8192], P(('dp', 'seq'), 'tensor'), parts along dimension 0, may hold values from -6 to 6
- gate: float32 [8192], P('tensor'), may hold values from -1.5 to 1.5
- visible: int32 [64, 4], P(('dp', 'seq')), parts along dimension 0, may hold values from -1 to 15, as said below
Outputs:
- query_grad: bfloat16 [8192, 8192], P(('dp', 'seq'), 'tensor'), parts along dimension 0
- key_grad: bfloat16 [2048, 8192], P(('dp', 'seq'), 'tensor'), parts along dimension 0
- value_grad: bfloat16 [2048, 8192], P(('dp', 'seq'), 'tensor'), parts along dimension 0
- gate_grad: float32 [16384], P(('dp', 'tensor')), parts along dimension 0
The draws below stay inside these ranges and needn't reach their ends.
There are 2 independent parts, one for each index of `dp`. The reference program is written for one: setup_inputs(seed, part) draws one part's arguments, and reference() takes and returns one part's arrays. A program takes and returns all parts, laid end to end along the dimension named above; an argument that names none is the same for every part. Nothing has to cross between parts.
Inputs may be any that keep to these rules, and one draw needn't show every extreme that they name: `visible`: row s lists the images that span s (tokens s * 128 to s * 128 + 127) may see, each at most once. A span on seq index r lists only images below (r + 1), and its slot 0 is image (r + 1) - 1. Unused slots hold -1 and follow the used ones; some span uses all 4 slots.
All inputs are finite; a program needn't handle non-finite values.
Results may differ from the reference program's by a relative error of at most 0.015.
Values may be sent and summed in bfloat16 or wider, within the bound.
A program may use at most 128 MiB of HBM per device.

```python
import jax
import jax.numpy as jnp
from jax import lax

HEADS = 64
HEAD_DIM = 128
LAT = 64
TOK_DEV = 256
IMG_DEV = 1
SPAN = 128
VIS = 4
WIDTH = 8192
TOKENS = 4096
IMAGES = 16
KEYS = 1024
SPANS = 32


def latent_rows(key, corner):
    normal_rows = jnp.clip(jax.random.normal(jax.random.fold_in(key, 31), (KEYS, WIDTH), jnp.float32), -4.0, 4.0)
    mixed = normal_rows
    coin = jax.random.uniform(jax.random.fold_in(key, 33), (IMAGES, 1, WIDTH), jnp.float32)
    signs = jnp.where(coin < 0.5, -corner, corner)
    within = jnp.arange(LAT)[None, :, None]
    leading = jnp.where(within == 0, signs, 0.99 * signs)
    placed = (within < 2) & (corner > 0)
    shaped = jnp.where(placed, leading, mixed.reshape(IMAGES, LAT, WIDTH))
    return shaped.reshape(KEYS, WIDTH)


def draw_keys(key, part):
    drawn_rows = latent_rows(key, 0.0)
    return drawn_rows.astype(jnp.bfloat16)


def draw_queries(key, part):
    key = jax.random.fold_in(key, 5)
    drawn_rows = jnp.clip(jax.random.normal(key, (TOKENS, WIDTH), jnp.float32), -8.0, 8.0)
    return drawn_rows.astype(jnp.bfloat16)


def draw_visible(key, part):
    key = jax.random.fold_in(key, 7)
    span_index = jnp.arange(SPANS, dtype=jnp.int32)
    cycle_index = span_index // (TOK_DEV // SPAN)
    available = (cycle_index + 1) * IMG_DEV
    newest = available - 1
    image_index = jnp.arange(IMAGES, dtype=jnp.int32)
    scores = jax.random.randint(jax.random.fold_in(key, 1), (SPANS, IMAGES), 0, 1 << 20) * IMAGES + image_index[None, :]
    barred = (image_index[None, :] >= available[:, None]) | (image_index[None, :] == newest[:, None])
    scores = jnp.where(barred, 1 << 30, scores)
    ranked = jnp.argsort(scores, axis=1)[:, :VIS - 1].astype(jnp.int32)
    slot_count = jax.random.randint(jax.random.fold_in(key, 2), (SPANS,), 1, VIS + 1)
    slot_count = jnp.minimum(slot_count, available)
    slot_count = jnp.where(span_index == SPANS - 1, VIS, slot_count)
    listed = jnp.concatenate([newest[:, None], ranked], axis=1)
    in_use = jnp.arange(VIS, dtype=jnp.int32)[None, :] < slot_count[:, None]
    return jnp.where(in_use, listed, -1).astype(jnp.int32)


def steps_of(rng, extent, shards, low, top_value):
    def one(axis_at, parts):
        draws = jax.random.uniform(jax.random.fold_in(jax.random.fold_in(rng, 6), axis_at), (parts,), jnp.float32, low / len(shards), top_value / len(shards))
        return jnp.repeat(jnp.exp(draws), extent[axis_at] // parts).reshape((-1,) + (1,) * (len(extent) - axis_at - 1))

    gain = one(*shards[0])
    for cut in shards[1:]:
        gain = gain * one(*cut)
    return gain


def noise(own_key, shape, width, reach, shards=(), held_as=jnp.bfloat16):
    gain = steps_of(own_key, shape, shards, -0.22, 0.18) if shards else 1.0
    array = jax.random.normal(own_key, shape, jnp.float32) * width * gain
    return jnp.minimum(jnp.maximum(array, -reach), reach).astype(held_as)


def setup_inputs(seed: int = 0, part: int = 0) -> dict:
    arg_keys = jax.random.split(jax.random.key(seed), 7)
    part_splits = jax.random.split(jax.random.fold_in(arg_keys[6], part), 7)
    queries = draw_queries(jax.random.fold_in(jax.random.fold_in(arg_keys[6], part), 71), part)
    keys = draw_keys(jax.random.fold_in(jax.random.fold_in(arg_keys[6], part), 71), part)
    values = noise(part_splits[2], (KEYS, WIDTH), 1.0, 6.0, ((0, 16), (1, 4)))
    cotangent = noise(part_splits[3], (TOKENS, WIDTH), 1.0, 6.0, ((0, 16), (1, 4)))
    gate = jnp.clip(jax.random.uniform(arg_keys[4], (WIDTH,), jnp.float32, -1.5, 1.5) * steps_of(arg_keys[4], (WIDTH,), ((0, 4),), -0.4, 0.0), -1.5, 1.5)
    visible = draw_visible(jax.random.fold_in(jax.random.fold_in(arg_keys[6], part), 71), part)
    return {"queries": queries, "keys": keys, "values": values, "cotangent": cotangent, "gate": gate, "visible": visible}


floor_score = -1.0e30


def reference(queries, keys, values, cotangent, gate, visible):
    span_count = TOKENS // SPAN
    scaling = HEAD_DIM ** -0.5
    image_ids = jnp.maximum(visible, 0).astype(jnp.int32)
    key_valid = jnp.repeat(visible >= 0, LAT, axis=1)
    row_index = (image_ids[:, :, None] * LAT + jnp.arange(LAT, dtype=jnp.int32)[None, None, :]).reshape(span_count, VIS * LAT)
    listed_keys = keys[row_index].reshape(span_count, VIS * LAT, HEADS, HEAD_DIM)
    listed_values = values[row_index].reshape(span_count, VIS * LAT, HEADS, HEAD_DIM)
    span_queries = queries.reshape(span_count, SPAN, HEADS, HEAD_DIM)
    tanh_gate = jnp.tanh(gate)
    grad_out = (tanh_gate[None, :] * cotangent.astype(jnp.float32)).astype(jnp.bfloat16)
    span_grads = grad_out.reshape(span_count, SPAN, HEADS, HEAD_DIM)

    def span_work(inputs):
        query_rows, key_rows, value_rows, grad_rows, valid = inputs
        query_wide = query_rows.astype(jnp.float32)
        key_wide = key_rows.astype(jnp.float32)
        value_wide = value_rows.astype(jnp.float32)
        grad_wide = grad_rows.astype(jnp.float32)
        raw = jnp.einsum("qhd,khd->hqk", query_wide, key_wide) * scaling
        allowed = valid[None, None, :]
        scores = jnp.where(allowed, raw, floor_score)
        highest = jnp.max(scores, axis=2, keepdims=True)
        totals = jnp.sum(jnp.where(allowed, jnp.exp(scores - highest), 0.0), axis=2, keepdims=True)
        weights = jnp.where(allowed, jnp.exp(scores - (highest + jnp.log(totals))), 0.0)
        weights_low = weights.astype(jnp.bfloat16)
        attended = jnp.einsum("hqk,khd->qhd", weights_low.astype(jnp.float32), value_wide)
        row_dots = jnp.sum(grad_wide * attended, axis=2)
        weight_grad = jnp.einsum("qhd,khd->hqk", grad_wide, value_wide)
        score_grad = (weights * (weight_grad - row_dots.T[:, :, None])).astype(jnp.bfloat16)
        query_grad = (jnp.einsum("hqk,khd->qhd", score_grad.astype(jnp.float32), key_wide) * scaling).astype(jnp.bfloat16)
        key_grad = jnp.einsum("hqk,qhd->khd", score_grad.astype(jnp.float32), query_wide) * scaling
        value_grad = jnp.einsum("hqk,qhd->khd", weights_low.astype(jnp.float32), grad_wide)
        return query_grad, key_grad, value_grad, attended

    query_grad, key_grad, value_grad, attended = lax.map(span_work, (span_queries, listed_keys, listed_values, span_grads, key_valid))
    flat_out = attended.reshape(TOKENS, WIDTH)
    gate_grad = jnp.sum(cotangent.astype(jnp.float32) * flat_out, axis=0) * (1.0 - tanh_gate * tanh_gate)
    flat_rows = row_index.reshape(-1)
    key_total = jnp.zeros((KEYS, WIDTH), jnp.float32).at[flat_rows].add(key_grad.reshape(-1, WIDTH))
    value_total = jnp.zeros((KEYS, WIDTH), jnp.float32).at[flat_rows].add(value_grad.reshape(-1, WIDTH))
    return (query_grad.reshape(TOKENS, WIDTH), key_total.astype(jnp.bfloat16), value_total.astype(jnp.bfloat16), gate_grad)
```

```python
import functools

import jax
import jax.numpy as jnp
from jax import lax
from jax.experimental import pallas as pl
from jax.experimental.pallas import tpu as pltpu
from jax.sharding import PartitionSpec as P

MESH = pl.DeviceIdType.MESH
D = 128
LAT = 64
SPAN = 128
VIS = 4
CORE_HEADS = 8
N = 1
CHUNKS = CORE_HEADS // N
AHEAD = 2
IMAGES = 16
GATHER2, GATHER3, COMPUTE, BACK2, BACK3, LAST = 1, 2, 3, 5, 7, 9
NEG = -1e30
EXP2_SCALE = D**-0.5 * 1.4426950408889634
F32, BF16 = jnp.float32, jnp.bfloat16

(
    A_R, A_L, A_FR, A_FL, A_Z0, A_ZM, A_ZP, A_HR, A_HL,
    R_R, R_L, R_FR, R_FL, R_Z0, R_ZM, R_ZP, R_HR, R_HL,
) = range(18)
MESSAGES = 18
DQ, OUT_K, OUT_V, IN_K, IN_V = range(5)


def dot(a, b, ca, cb):
    return lax.dot_general(a, b, (((ca,), (cb,)), ((), ())), preferred_element_type=F32)


def kernel(
    q_ref, k_ref, v_ref, ct_ref, gate_hbm, vis_ref,
    qg_ref, kg_ref, vg_ref, gg_ref,
    qw, cw, kv, obuf, rbuf, kvw, sg_ref, low_ref, both_ref, dqs, fin, gpart, gall, gsum, first, gate_ref, vis_s, slot_s,
    ssem, rsem, hsend, hrecv, hout, lsem, lout, lfirst, esend, erecv, elocal, gsend, grecv, glast,
):
    seq = lax.axis_index("seq")
    c, k = lax.div(seq, 2), lax.rem(seq, 2)
    z, x = lax.div(c, 4), lax.rem(c, 4)
    xr, xl = lax.rem(x + 1, 4), lax.rem(x + 3, 4)
    xo = lax.rem(x + 2, 4)
    z0, z1 = z == 0, z == 1

    def at_chip(chip):
        return {"seq": chip * 2 + k}

    right_chip, left_chip, across_chip = z * 4 + xr, z * 4 + xl, (1 - z) * 4 + x
    right, left, across = at_chip(right_chip), at_chip(left_chip), at_chip(across_chip)
    partner = {"seq": c * 2 + (1 - k)}

    def send(idx, g, src, dst, dev):
        return pltpu.make_async_remote_copy(
            src_ref=src, dst_ref=dst, send_sem=ssem.at[idx], recv_sem=rsem.at[g, idx],
            device_id=dev, device_id_type=MESH,
        )

    def blk(buf, g, b):
        return buf.at[g, pl.ds(2 * b, 2)]

    def img(buf, g, b, half):
        return buf.at[g, pl.ds(2 * b + half, 1)]

    hi = z * 4

    def message(idx, g):
        own = blk(kv, g, c)
        if idx == A_R:
            return send(idx, g, own, own, right)
        if idx == A_L:
            return send(idx, g, own, own, left)
        if idx == A_FR:
            b = blk(kv, g, hi + xl)
            return send(idx, g, b, b, right)
        if idx == A_FL:
            b = blk(kv, g, hi + xr)
            return send(idx, g, b, b, left)
        if idx == A_Z0:
            return send(idx, g, own, own, across)
        if idx == A_ZM:
            b = blk(kv, g, xl)
            return send(idx, g, b, b, across)
        if idx == A_ZP:
            b = blk(kv, g, xr)
            return send(idx, g, b, b, across)
        if idx == A_HR:
            b = img(kv, g, xl, 0)
            return send(idx, g, b, b, right)
        if idx == A_HL:
            b = img(kv, g, xr, 1)
            return send(idx, g, b, b, left)
        if idx == R_R:
            return send(idx, g, blk(obuf, g, hi + xl), rbuf.at[g, 0], left)
        if idx == R_L:
            return send(idx, g, blk(obuf, g, hi + xr), rbuf.at[g, 1], right)
        if idx == R_FR:
            return send(idx, g, blk(obuf, g, hi + xo), rbuf.at[g, 2], left)
        if idx == R_FL:
            return send(idx, g, blk(obuf, g, hi + xo), rbuf.at[g, 3], right)
        if idx == R_Z0:
            return send(idx, g, blk(obuf, g, x), rbuf.at[g, 4], across)
        if idx == R_ZM:
            return send(idx, g, blk(obuf, g, xl), rbuf.at[g, 5], across)
        if idx == R_ZP:
            return send(idx, g, blk(obuf, g, xr), rbuf.at[g, 6], across)
        if idx == R_HR:
            return send(idx, g, img(obuf, g, xo, 0), rbuf.at[g, 7, pl.ds(0, 1)], left)
        if idx == R_HL:
            return send(idx, g, img(obuf, g, xo, 1), rbuf.at[g, 7, pl.ds(1, 1)], right)
        raise ValueError(idx)

    def swap(idx, h, src, dst):
        return pltpu.make_async_remote_copy(
            src_ref=src, dst_ref=dst, send_sem=hsend.at[idx], recv_sem=hrecv.at[h, idx - IN_K],
            device_id=partner, device_id_type=MESH,
        )

    def swap_all(idx, src, dst):
        return pltpu.make_async_remote_copy(
            src_ref=src, dst_ref=dst, send_sem=hsend.at[idx], recv_sem=hout.at[idx],
            device_id=partner, device_id_type=MESH,
        )

    def head_message(idx, h):
        g, n = lax.div(h, N), lax.rem(h, N)
        theirs = head_cols(1 - k, h)
        if idx == IN_K:
            return swap(idx, h, k_ref.at[:, theirs], kv.at[g, seq, 0, n])
        return swap(idx, h, v_ref.at[:, theirs], kv.at[g, seq, 1, n])

    def head_got(idx, h, dst):
        swap(idx, h, dst, dst).wait_recv()

    def head_cols(core, h):
        return pl.ds(pl.multiple_of((core * CORE_HEADS + h) * D, D), D)

    def got(idx, g, dst):
        send(idx, g, dst, dst, partner).wait_recv()

    def own_copies(h):
        g, n = lax.div(h, N), lax.rem(h, N)
        mine = head_cols(k, h)
        return (
            pltpu.make_async_copy(k_ref.at[:, mine], kv.at[g, seq, 0, n], lsem.at[h, 0]),
            pltpu.make_async_copy(v_ref.at[:, mine], kv.at[g, seq, 1, n], lsem.at[h, 1]),
        )

    half_width = CORE_HEADS * D
    half_cols = pl.ds(pl.multiple_of(k * half_width, half_width), half_width)
    their_cols = pl.ds(pl.multiple_of((1 - k) * half_width, half_width), half_width)
    my_rows, their_rows = pl.ds(k * 256, 256), pl.ds((1 - k) * 256, 256)

    def result_copies():
        results = ((1, fin.at[k, 0], kg_ref), (2, fin.at[k, 1], vg_ref))
        return [
            pltpu.make_async_copy(src, ref.at[:, half_cols], lout.at[i]) for i, src, ref in results
        ] + [
            swap_all(OUT_K, fin.at[1 - k, 0], kg_ref.at[:, half_cols]),
            swap_all(OUT_V, fin.at[1 - k, 1], vg_ref.at[:, half_cols]),
        ]

    def query_copies():
        return [
            pltpu.make_async_copy(dqs.at[my_rows], qg_ref.at[:, half_cols], lout.at[0]),
            swap_all(DQ, dqs.at[their_rows], qg_ref.at[:, half_cols]),
        ]

    def early(i, src, dst):
        return pltpu.make_async_remote_copy(
            src_ref=src, dst_ref=dst, send_sem=esend.at[i], recv_sem=erecv.at[i],
            device_id=partner, device_id_type=MESH,
        )

    swaps = [
        early(0, vis_ref, vis_s.at[k]),
        early(1, q_ref.at[:, their_cols], qw.at[my_rows]),
        early(2, ct_ref.at[:, their_cols], cw.at[my_rows]),
    ]
    keeps = [
        pltpu.make_async_copy(vis_ref, vis_s.at[k], elocal.at[0]),
        pltpu.make_async_copy(q_ref.at[:, half_cols], qw.at[my_rows], elocal.at[1]),
        pltpu.make_async_copy(ct_ref.at[:, half_cols], cw.at[my_rows], elocal.at[2]),
        pltpu.make_async_copy(gate_hbm, gate_ref, elocal.at[3]),
    ]

    first_cols = head_cols(1 - k, 0)
    first_copies = [
        pltpu.make_async_copy(k_ref.at[:, first_cols], first.at[0, 0, 0], lfirst.at[0]),
        pltpu.make_async_copy(v_ref.at[:, first_cols], first.at[0, 1, 0], lfirst.at[1]),
    ]

    def first_messages(idx, chip):
        mine = kv.at[0, pl.ds(seq, 1)]
        return [
            pltpu.make_async_remote_copy(
                src_ref=src, dst_ref=mine, send_sem=ssem.at[idx], recv_sem=rsem.at[0, idx],
                device_id={"seq": chip * 2 + core}, device_id_type=MESH,
            )
            for src, core in ((mine, k), (first, 1 - k))
        ]

    def send_first():
        for copy in (*own_copies(0), *first_copies):
            copy.wait()

        @pl.when(jnp.logical_or(z0, x < 3))
        def _():
            for copy in first_messages(A_R, right_chip):
                copy.start()

        @pl.when(jnp.logical_or(z0, x == 0))
        def _():
            for copy in first_messages(A_L, left_chip):
                copy.start()

        @pl.when(z0)
        def _():
            for copy in first_messages(A_Z0, across_chip):
                copy.start()

    for copy in first_copies:
        copy.start()
    for h in range(AHEAD):
        for copy in own_copies(h):
            copy.start()

    for copy in keeps:
        copy.start()

    barrier = pltpu.get_barrier_semaphore()
    greeted = [{"seq": chip * 2 + m} for chip in (right_chip, left_chip, across_chip) for m in (0, 1)]
    for device in greeted + [partner]:
        pl.semaphore_signal(barrier, inc=1, device_id=device, device_id_type=MESH)
    pl.semaphore_wait(barrier, 7)

    send_first()

    for h in range(AHEAD):
        head_message(IN_K, h).start()
        head_message(IN_V, h).start()

    for copy in swaps:
        copy.start()

    sg_ref[:, VIS] = jnp.zeros((4, LAT, SPAN), BF16)
    low_ref[:, VIS] = jnp.zeros((4, LAT, SPAN), BF16)

    def prepare():
        for copy in keeps:
            copy.wait()
        for copy in swaps:
            copy.wait()

        @pl.loop(0, IMAGES)
        def _(i):
            for s in range(4):
                slot = jnp.int32(VIS)
                for v in range(VIS):
                    slot = jnp.where(vis_s[s // 2, s % 2, v] == i, v, slot)
                slot_s[s, i] = slot

    def when(cond):
        return pl.when(cond)

    def span_work(h):
        cols = pl.ds(pl.multiple_of(h * D, D), D)
        kvw[...] = kv[h, :, :, 0]
        tanh_gate = jnp.tanh(gate_ref[pl.ds(k * CORE_HEADS + h, 1), :])
        q_all = qw[:, cols]
        ct_all = cw[:, cols]
        go_all = (tanh_gate * ct_all.astype(F32)).astype(BF16)
        both_ref[:, :D] = go_all
        both_ref[:, D:] = ct_all
        spans = range(4)
        listed = [[vis_s[s // 2, s % 2, v] for v in range(VIS)] for s in spans]
        ids = [[jnp.maximum(i, 0) for i in row] for row in listed]
        q = [q_all[s * SPAN : (s + 1) * SPAN] for s in spans]
        go = [go_all[s * SPAN : (s + 1) * SPAN] for s in spans]
        kl = [jnp.concatenate([kvw[i, 0] for i in ids[s]], axis=0) for s in spans]
        vl = [jnp.concatenate([kvw[i, 1] for i in ids[s]], axis=0) for s in spans]
        raw = [dot(kl[s], q[s], 1, 1) for s in spans]
        wg = [dot(vl[s], go[s], 1, 1) for s in spans]
        p, low, sg = [], [], []
        for s in spans:
            rows = [raw[s][:LAT] * EXP2_SCALE]
            for v in range(1, VIS):
                bias = jnp.where(listed[s][v] >= 0, 0.0, NEG).astype(F32)
                rows.append(raw[s][v * LAT : (v + 1) * LAT] * EXP2_SCALE + bias)
            sc = jnp.concatenate(rows, axis=0)
            e = jnp.exp2(sc - jnp.max(sc, axis=0, keepdims=True))
            p.append(e * (1.0 / jnp.sum(e, axis=0, keepdims=True)))
            low.append(p[s].astype(BF16))
        for s in spans:
            dots = jnp.sum(low[s].astype(F32) * wg[s], axis=0, keepdims=True)
            sg.append((p[s] * (wg[s] - dots)).astype(BF16))
        for s in spans:
            low_ref[s, pl.ds(0, VIS)] = low[s].reshape(VIS, LAT, SPAN)
            sg_ref[s, pl.ds(0, VIS)] = sg[s].reshape(VIS, LAT, SPAN)
        dq = [dot(sg[s], kl[s], 0, 0) * (D**-0.5) for s in spans]
        for s in spans:
            dqs[pl.ds(s * SPAN, SPAN), cols] = dq[s].astype(BF16)

    def products(g):
        tanh_gate = jnp.tanh(gate_ref[pl.ds(k * CORE_HEADS + g, 1), :])
        q_all = qw[:, pl.ds(pl.multiple_of(g * D, D), D)]
        both = both_ref[...]

        def images(count):
            left, low_left, vals = [], [], []
            for i in range(count):
                slots = [slot_s[s, i] for s in range(4)]
                left.append(jnp.concatenate([sg_ref[s, slots[s]] for s in range(4)], axis=1))
                low_left.append(jnp.concatenate([low_ref[s, slots[s]] for s in range(4)], axis=1))
                vals.append(jnp.where(i < 2 * (c + 1), kvw[i, 1].astype(F32), 0.0))
            dk = dot(jnp.concatenate(left, axis=0), q_all, 1, 0) * (D**-0.5)
            obuf[g, pl.ds(0, count), 0, 0] = dk.reshape(count, LAT, D).astype(BF16)
            vw = dot(jnp.concatenate(low_left, axis=0), both, 1, 0)
            obuf[g, pl.ds(0, count), 1, 0] = vw[:, :D].reshape(count, LAT, D).astype(BF16)
            vals = jnp.concatenate(vals, axis=0)
            gate_sum = jnp.sum(vals * vw[:, D:], axis=0, keepdims=True)
            gpart[pl.ds(g, 1), :] = gate_sum * (1.0 - tanh_gate * tanh_gate)

        @when(z0)
        def _():
            images(8)

        @when(z1)
        def _():
            images(16)

    def add(g, b, slot):
        rows = pl.ds(2 * b, 2)
        obuf[g, rows] = (obuf[g, rows].astype(F32) + rbuf[g, slot].astype(F32)).astype(BF16)

    def swapped(g):
        other = c * 2 + (1 - k)
        head_got(IN_K, g, kv.at[g, other, 0, 0])
        head_got(IN_V, g, kv.at[g, other, 1, 0])

    def gather1(g):
        for copy in own_copies(g):
            copy.wait()
        swapped(g)

        @when(jnp.logical_or(z0, x < 3))
        def _():
            message(A_R, g).start()

        @when(jnp.logical_or(z0, x == 0))
        def _():
            message(A_L, g).start()

    def gather2(g):
        @when(jnp.logical_or(z0, x > 0))
        def _():
            got(A_R, g, blk(kv, g, hi + xl))

        @when(z0)
        def _():
            message(A_ZM, g).start()
            got(A_L, g, blk(kv, g, hi + xr))
            message(A_ZP, g).start()

    def gather_own(g):
        @when(z0)
        def _():
            message(A_Z0, g).start()

    def gather_forward(g):
        @when(jnp.logical_or(x == 1, jnp.logical_and(z1, x == 2)))
        def _():
            message(A_FR, g).start()

        @when(jnp.logical_and(z0, x == 0))
        def _():
            message(A_FL, g).start()

    def gather3(g):
        @when(z1)
        def _():
            got(A_ZM, g, blk(kv, g, xl))
            message(A_HR, g).start()
            got(A_ZP, g, blk(kv, g, xr))
            message(A_HL, g).start()

    def gather4(g):
        @when(z1)
        def _():
            got(A_Z0, g, blk(kv, g, x))
            got(A_HR, g, img(kv, g, xo, 0))
            got(A_HL, g, img(kv, g, xo, 1))

        @when(jnp.logical_or(x == 2, jnp.logical_and(z1, x == 3)))
        def _():
            got(A_FR, g, blk(kv, g, hi + xo))

        @when(jnp.logical_and(z0, x == 3))
        def _():
            got(A_FL, g, blk(kv, g, xo))

        @when(jnp.logical_and(z1, x == 3))
        def _():
            got(A_L, g, blk(kv, g, 4))

    def back1(g):
        @when(z1)
        def _():
            message(R_HR, g).start()
            message(R_HL, g).start()
            message(R_Z0, g).start()

        @when(jnp.logical_or(x == 2, jnp.logical_and(z1, x == 3)))
        def _():
            message(R_FR, g).start()

        @when(jnp.logical_and(z0, x == 3))
        def _():
            message(R_FL, g).start()

        @when(jnp.logical_and(z1, x == 3))
        def _():
            message(R_L, g).start()

    def back2(g):
        @when(z1)
        def _():
            got(R_HR, g, rbuf.at[g, 7, pl.ds(0, 1)])
            row = 2 * xl
            obuf[g, row] = (obuf[g, row].astype(F32) + rbuf[g, 7, 0].astype(F32)).astype(BF16)
            message(R_ZM, g).start()
            got(R_HL, g, rbuf.at[g, 7, pl.ds(1, 1)])
            row = 2 * xr + 1
            obuf[g, row] = (obuf[g, row].astype(F32) + rbuf[g, 7, 1].astype(F32)).astype(BF16)
            message(R_ZP, g).start()

            @when(jnp.logical_or(x == 1, x == 2))
            def _():
                got(R_FR, g, rbuf.at[g, 2])
                add(g, 4 + xl, 2)

            @when(x > 0)
            def _():
                message(R_R, g).start()

    def back3(g):
        @when(z0)
        def _():
            @when(x == 1)
            def _():
                got(R_FR, g, rbuf.at[g, 2])
                add(g, xl, 2)

            @when(x == 0)
            def _():
                got(R_FL, g, rbuf.at[g, 3])
                add(g, xr, 3)

            got(R_ZM, g, rbuf.at[g, 5])
            add(g, xl, 5)
            message(R_R, g).start()
            got(R_ZP, g, rbuf.at[g, 6])
            add(g, xr, 6)
            message(R_L, g).start()

    def back4(g):
        own = pl.ds(2 * c, 2)

        def finish(slots):
            total = obuf[g, own].astype(F32)
            for slot in slots:
                total += rbuf[g, slot].astype(F32)
            fin[:, :, :, pl.ds(pl.multiple_of(g * D, D), D)] = total[:, :, 0].astype(BF16)

        @when(z0)
        def _():
            got(R_Z0, g, rbuf.at[g, 4])
            got(R_R, g, rbuf.at[g, 0])
            got(R_L, g, rbuf.at[g, 1])
            finish((4, 0, 1))

        @when(z1)
        def _():
            @when(x < 3)
            def _():
                got(R_R, g, rbuf.at[g, 0])

            @when(x == 0)
            def _():
                got(R_L, g, rbuf.at[g, 1])
                finish((0, 1))

            @when(jnp.logical_or(x == 1, x == 2))
            def _():
                finish((0,))

            @when(x == 3)
            def _():
                finish(())

    odd = lax.rem(x, 2)
    pairs = (
        across,
        at_chip(z * 4 + x + 1 - 2 * odd),
        at_chip(z * 4 + lax.rem(x + 3 + 2 * odd, 4)),
    )

    def gate_step(i):
        return pltpu.make_async_remote_copy(
            src_ref=gsum.at[i], dst_ref=gall.at[i], send_sem=gsend.at[i], recv_sem=grecv.at[i],
            device_id=pairs[i], device_id_type=MESH,
        )

    gate_local = pltpu.make_async_copy(gsum.at[3], gg_ref.at[k], glast.at[0])
    gate_remote = pltpu.make_async_remote_copy(
        src_ref=gsum.at[3], dst_ref=gg_ref.at[k], send_sem=glast.at[1], recv_sem=glast.at[2],
        device_id=partner, device_id_type=MESH,
    )

    @pl.loop(0, CHUNKS + LAST)
    def _(t):
        def stage(offset, run, first=0):
            @when(jnp.logical_and(t >= offset + first, t < CHUNKS + offset))
            def _():
                run(t - offset)

        @when(t < CHUNKS - AHEAD)
        def _():
            for copy in own_copies(t + AHEAD):
                copy.start()
            head_message(IN_K, t + AHEAD).start()
            head_message(IN_V, t + AHEAD).start()

        stage(0, gather1, 1)
        stage(GATHER2, gather2)
        stage(0, gather_own, 1)
        stage(GATHER2, gather_forward)
        stage(BACK2, back2)
        stage(BACK3, back3)
        stage(LAST, back4)

        @when(t == COMPUTE - 1)
        def _():
            prepare()
            swapped(0)

        stage(COMPUTE, gather4)
        stage(COMPUTE, span_work)
        stage(GATHER3, gather3)
        stage(COMPUTE, products)
        stage(COMPUTE, back1)

        @when(t == CHUNKS + COMPUTE - 1)
        def _():
            for copy in query_copies():
                copy.start()
            gsum[0] = gpart[...]
            gate_step(0).start()

        for i in range(3):

            @when(t == CHUNKS + COMPUTE + i)
            def _():
                gate_step(i).wait_recv()
                gsum[i + 1] = gsum[i] + gall[i]
                if i < 2:
                    gate_step(i + 1).start()
                else:
                    gate_local.start()
                    gate_remote.start()

    for copy in result_copies():
        copy.start()
    for i in range(3):
        gate_step(i).wait_send()

    def done(idx):
        half = idx in (A_HR, A_HL, R_HR, R_HL)
        sent = kv.at[:, pl.ds(0, 1 if half else 2)]
        pltpu.make_async_remote_copy(
            src_ref=sent, dst_ref=sent, send_sem=ssem.at[idx], recv_sem=rsem.at[0, idx],
            device_id=partner, device_id_type=MESH,
        ).wait_send()

    @when(z0)
    def _():
        for idx in (A_Z0, A_ZM, A_ZP):
            done(idx)

    @when(z1)
    def _():
        for idx in (A_HR, A_HL, R_HR, R_HL, R_Z0, R_ZM, R_ZP):
            done(idx)

    @when(jnp.logical_or(z0, x < 3))
    def _():
        done(A_R)

    @when(jnp.logical_or(z0, x == 0))
    def _():
        done(A_L)

    @when(jnp.logical_or(x == 1, jnp.logical_and(z1, x == 2)))
    def _():
        done(A_FR)

    @when(jnp.logical_and(z0, x == 0))
    def _():
        done(A_FL)

    @when(jnp.logical_or(x == 2, jnp.logical_and(z1, x == 3)))
    def _():
        done(R_FR)

    @when(jnp.logical_and(z0, x == 3))
    def _():
        done(R_FL)

    @when(jnp.logical_or(z0, x == 3))
    def _():
        done(R_L)

    @when(jnp.logical_or(z0, x > 0))
    def _():
        done(R_R)

    swap_all(DQ, dqs.at[their_rows], qg_ref.at[:, their_cols]).wait_send()
    swap_all(OUT_K, fin.at[1 - k, 0], kg_ref.at[:, their_cols]).wait_send()
    swap_all(OUT_V, fin.at[1 - k, 1], vg_ref.at[:, their_cols]).wait_send()
    swap_all(IN_K, k_ref.at[:, their_cols], kg_ref.at[:, their_cols]).wait_send()
    swap_all(IN_V, v_ref.at[:, their_cols], vg_ref.at[:, their_cols]).wait_send()
    for idx, ref in ((DQ, qg_ref), (OUT_K, kg_ref), (OUT_V, vg_ref)):
        swap_all(idx, ref.at[:, their_cols], ref.at[:, their_cols]).wait_recv()
    pltpu.make_async_copy(qg_ref.at[:, half_cols], qg_ref.at[:, half_cols], lout.at[0]).wait()
    pltpu.make_async_copy(kg_ref.at[:, half_cols], kg_ref.at[:, half_cols], lout.at[1]).wait()
    pltpu.make_async_copy(vg_ref.at[:, half_cols], vg_ref.at[:, half_cols], lout.at[2]).wait()

    gate_local.wait()
    gate_remote.wait_send()
    pltpu.make_async_remote_copy(
        src_ref=gsum.at[3], dst_ref=gg_ref.at[1 - k], send_sem=glast.at[1], recv_sem=glast.at[2],
        device_id=partner, device_id_type=MESH,
    ).wait_recv()


def place(a0, a1, a2, a3, b0, b1, b2, b3, m0, m1, m2, m3, sem):
    held = (m0, m1, m2, m3)
    into = [
        pltpu.make_async_copy(a, m, sem.at[0, i]) for i, (a, m) in enumerate(zip((a0, a1, a2, a3), held))
    ]
    out = [
        pltpu.make_async_copy(m, b, sem.at[1, i]) for i, (m, b) in enumerate(zip(held, (b0, b1, b2, b3)))
    ]
    for copy in into:
        copy.start()
    for copy, after in zip(into, out):
        copy.wait()
        after.start()
    for copy in out:
        copy.wait()


def shards(queries, keys, values, cotangent, gate, visible):
    tokens, width = queries.shape
    half = width // 2
    any_spec = pl.BlockSpec(memory_space=pl.ANY)
    hbm_spec = pl.BlockSpec(memory_space=pltpu.HBM)
    dma = pltpu.SemaphoreType.DMA
    out_shape = (
        jax.ShapeDtypeStruct((tokens, width), BF16),
        jax.ShapeDtypeStruct((LAT, width), BF16),
        jax.ShapeDtypeStruct((LAT, width), BF16),
        jax.ShapeDtypeStruct((2, CORE_HEADS, D), F32),
    )
    results = pl.pallas_call(
        kernel,
        out_shape=out_shape,
        in_specs=[hbm_spec] * 6,
        out_specs=(any_spec,) * 4,
        scratch_shapes=[
            pltpu.VMEM((2 * tokens, half), BF16),
            pltpu.VMEM((2 * tokens, half), BF16),
            pltpu.VMEM((CHUNKS, IMAGES, 2, N, LAT, D), BF16),
            pltpu.VMEM((CHUNKS, IMAGES, 2, N, LAT, D), BF16),
            pltpu.VMEM((CHUNKS, 8, 2, 2, N, LAT, D), BF16),
            pltpu.VMEM((IMAGES, 2, LAT, D), BF16),
            pltpu.VMEM((4, VIS + 1, LAT, SPAN), BF16),
            pltpu.VMEM((4, VIS + 1, LAT, SPAN), BF16),
            pltpu.VMEM((2 * tokens, 2 * D), BF16),
            pltpu.VMEM((2 * tokens, half), BF16),
            pltpu.VMEM((2, 2, LAT, half), BF16),
            pltpu.VMEM((CORE_HEADS, D), F32),
            pltpu.VMEM((3, CORE_HEADS, D), F32),
            pltpu.VMEM((4, CORE_HEADS, D), F32),
            pltpu.VMEM((1, 2, N, LAT, D), BF16),
            pltpu.VMEM((2 * CORE_HEADS, D), F32),
            pltpu.SMEM((2, 2, VIS), jnp.int32),
            pltpu.SMEM((4, IMAGES), jnp.int32),
            dma((MESSAGES,)),
            dma((CHUNKS, MESSAGES)),
            dma((5,)),
            dma((CORE_HEADS, 2)),
            dma((3,)),
            dma((CORE_HEADS, 2)),
            dma((3,)),
            dma((2,)),
            dma((3,)),
            dma((3,)),
            dma((4,)),
            dma((3,)),
            dma((3,)),
            dma((3,)),
        ],
        compiler_params=pltpu.CompilerParams(
            collective_id=0, has_side_effects=True, vmem_limit_bytes=63 * 1024 * 1024
        ),
        name="cross_attention_backward",
    )(queries, keys, values, cotangent, gate.reshape(2 * CORE_HEADS, D), visible)
    query_grad, key_grad, value_grad, gate_grad = pl.pallas_call(
        place,
        out_shape=out_shape,
        in_specs=[any_spec] * 4,
        out_specs=(hbm_spec,) * 4,
        scratch_shapes=[pltpu.VMEM(o.shape, o.dtype) for o in out_shape] + [dma((2, 4))],
        compiler_params=pltpu.CompilerParams(vmem_limit_bytes=63 * 1024 * 1024),
        name="place_results",
    )(*results)
    return query_grad, key_grad, value_grad, gate_grad.reshape(width)


def solution(mesh):
    placed = (
        P(("dp", "seq"), "tensor"),
        P(("dp", "seq"), "tensor"),
        P(("dp", "seq"), "tensor"),
        P(("dp", "seq"), "tensor"),
        P("tensor"),
        P(("dp", "seq"), None),
    )
    return jax.shard_map(
        shards,
        mesh=mesh,
        in_specs=placed,
        out_specs=(
            P(("dp", "seq"), "tensor"),
            P(("dp", "seq"), "tensor"),
            P(("dp", "seq"), "tensor"),
            P(("dp", "tensor")),
        ),
        check_vma=False,
    )
```

```python
import functools

import jax
import jax.numpy as jnp
from jax import lax
from jax.experimental import pallas as pl
from jax.experimental.pallas import tpu as pltpu
from jax.sharding import PartitionSpec as P

MESH = pl.DeviceIdType.MESH
D = 128
LAT = 64
SPAN = 128
VIS = 4
CORE_HEADS = 8
N = 1
CHUNKS = CORE_HEADS // N
AHEAD = 2
IMAGES = 16
GATHER2, GATHER3, COMPUTE, BACK2, BACK3, LAST = 1, 2, 3, 5, 7, 9
NEG = -1e30
EXP2_SCALE = D**-0.5 * 1.4426950408889634
F32, BF16 = jnp.float32, jnp.bfloat16

(
    A_R, A_L, A_FR, A_FL, A_Z0, A_ZM, A_ZP, A_HR, A_HL,
    R_R, R_L, R_FR, R_FL, R_Z0, R_ZM, R_ZP, R_HR, R_HL,
) = range(18)
MESSAGES = 18
DQ, OUT_K, OUT_V, IN_K, IN_V = range(5)


def dot(a, b, ca, cb):
    return lax.dot_general(a, b, (((ca,), (cb,)), ((), ())), preferred_element_type=F32)


def kernel(
    q_ref, k_ref, v_ref, ct_ref, gate_hbm, vis_ref,
    qg_ref, kg_ref, vg_ref, gg_ref,
    qw, cw, kv, obuf, rbuf, kvw, sg_ref, low_ref, both_ref, dqs, fin, gpart, gall, gsum, first, gate_ref, vis_s, slot_s,
    ssem, rsem, hsend, hrecv, hout, lsem, lout, lfirst, esend, erecv, elocal, gsend, grecv, glast,
):
    seq = lax.axis_index("seq")
    c, k = lax.div(seq, 2), lax.rem(seq, 2)
    z, x = lax.div(c, 4), lax.rem(c, 4)
    xr, xl = lax.rem(x + 1, 4), lax.rem(x + 3, 4)
    xo = lax.rem(x + 2, 4)
    z0, z1 = z == 0, z == 1

    def at_chip(chip):
        return {"seq": chip * 2 + k}

    right_chip, left_chip, across_chip = z * 4 + xr, z * 4 + xl, (1 - z) * 4 + x
    right, left, across = at_chip(right_chip), at_chip(left_chip), at_chip(across_chip)
    partner = {"seq": c * 2 + (1 - k)}

    def send(idx, g, src, dst, dev):
        return pltpu.make_async_remote_copy(
            src_ref=src, dst_ref=dst, send_sem=ssem.at[idx], recv_sem=rsem.at[g, idx],
            device_id=dev, device_id_type=MESH,
        )

    def blk(buf, g, b):
        return buf.at[g, pl.ds(2 * b, 2)]

    def img(buf, g, b, half):
        return buf.at[g, pl.ds(2 * b + half, 1)]

    hi = z * 4

    def message(idx, g):
        own = blk(kv, g, c)
        if idx == A_R:
            return send(idx, g, own, own, right)
        if idx == A_L:
            return send(idx, g, own, own, left)
        if idx == A_FR:
            b = blk(kv, g, hi + xl)
            return send(idx, g, b, b, right)
        if idx == A_FL:
            b = blk(kv, g, hi + xr)
            return send(idx, g, b, b, left)
        if idx == A_Z0:
            return send(idx, g, own, own, across)
        if idx == A_ZM:
            b = blk(kv, g, xl)
            return send(idx, g, b, b, across)
        if idx == A_ZP:
            b = blk(kv, g, xr)
            return send(idx, g, b, b, across)
        if idx == A_HR:
            b = img(kv, g, xl, 0)
            return send(idx, g, b, b, right)
        if idx == A_HL:
            b = img(kv, g, xr, 1)
            return send(idx, g, b, b, left)
        if idx == R_R:
            return send(idx, g, blk(obuf, g, hi + xl), rbuf.at[g, 0], left)
        if idx == R_L:
            return send(idx, g, blk(obuf, g, hi + xr), rbuf.at[g, 1], right)
        if idx == R_FR:
            return send(idx, g, blk(obuf, g, hi + xo), rbuf.at[g, 2], left)
        if idx == R_FL:
            return send(idx, g, blk(obuf, g, hi + xo), rbuf.at[g, 3], right)
        if idx == R_Z0:
            return send(idx, g, blk(obuf, g, x), rbuf.at[g, 4], across)
        if idx == R_ZM:
            return send(idx, g, blk(obuf, g, xl), rbuf.at[g, 5], across)
        if idx == R_ZP:
            return send(idx, g, blk(obuf, g, xr), rbuf.at[g, 6], across)
        if idx == R_HR:
            return send(idx, g, img(obuf, g, xo, 0), rbuf.at[g, 7, pl.ds(0, 1)], left)
        if idx == R_HL:
            return send(idx, g, img(obuf, g, xo, 1), rbuf.at[g, 7, pl.ds(1, 1)], right)
        raise ValueError(idx)

    def swap(idx, h, src, dst):
        return pltpu.make_async_remote_copy(
            src_ref=src, dst_ref=dst, send_sem=hsend.at[idx], recv_sem=hrecv.at[h, idx - IN_K],
            device_id=partner, device_id_type=MESH,
        )

    def swap_all(idx, src, dst):
        return pltpu.make_async_remote_copy(
            src_ref=src, dst_ref=dst, send_sem=hsend.at[idx], recv_sem=hout.at[idx],
            device_id=partner, device_id_type=MESH,
        )

    def head_message(idx, h):
        g, n = h, 0
        theirs = head_cols(1 - k, h)
        if idx == IN_K:
            return swap(idx, h, k_ref.at[:, theirs], kv.at[g, seq, 0, n])
        return swap(idx, h, v_ref.at[:, theirs], kv.at[g, seq, 1, n])

    def head_got(idx, h, dst):
        swap(idx, h, dst, dst).wait_recv()

    def head_cols(core, h):
        return pl.ds(pl.multiple_of((core * CORE_HEADS + h) * D, D), D)

    def got(idx, g, dst):
        send(idx, g, dst, dst, partner).wait_recv()

    def own_copies(h):
        g, n = h, 0
        mine = head_cols(k, h)
        return (
            pltpu.make_async_copy(k_ref.at[:, mine], kv.at[g, seq, 0, n], lsem.at[h, 0]),
            pltpu.make_async_copy(v_ref.at[:, mine], kv.at[g, seq, 1, n], lsem.at[h, 1]),
        )

    half_width = CORE_HEADS * D
    half_cols = pl.ds(pl.multiple_of(k * half_width, half_width), half_width)
    their_cols = pl.ds(pl.multiple_of((1 - k) * half_width, half_width), half_width)
    my_rows, their_rows = pl.ds(k * 256, 256), pl.ds((1 - k) * 256, 256)

    def result_copies():
        results = ((1, fin.at[k, 0], kg_ref), (2, fin.at[k, 1], vg_ref))
        return [
            pltpu.make_async_copy(src, ref.at[:, half_cols], lout.at[i]) for i, src, ref in results
        ] + [
            swap_all(OUT_K, fin.at[1 - k, 0], kg_ref.at[:, half_cols]),
            swap_all(OUT_V, fin.at[1 - k, 1], vg_ref.at[:, half_cols]),
        ]

    def query_copies():
        return [
            pltpu.make_async_copy(dqs.at[my_rows], qg_ref.at[:, half_cols], lout.at[0]),
            swap_all(DQ, dqs.at[their_rows], qg_ref.at[:, half_cols]),
        ]

    def early(i, src, dst):
        return pltpu.make_async_remote_copy(
            src_ref=src, dst_ref=dst, send_sem=esend.at[i], recv_sem=erecv.at[i],
            device_id=partner, device_id_type=MESH,
        )

    swaps = [
        early(0, vis_ref, vis_s.at[k]),
        early(1, q_ref.at[:, their_cols], qw.at[my_rows]),
        early(2, ct_ref.at[:, their_cols], cw.at[my_rows]),
    ]
    keeps = [
        pltpu.make_async_copy(vis_ref, vis_s.at[k], elocal.at[0]),
        pltpu.make_async_copy(q_ref.at[:, half_cols], qw.at[my_rows], elocal.at[1]),
        pltpu.make_async_copy(ct_ref.at[:, half_cols], cw.at[my_rows], elocal.at[2]),
        pltpu.make_async_copy(gate_hbm, gate_ref, elocal.at[3]),
    ]

    first_cols = head_cols(1 - k, 0)
    first_copies = [
        pltpu.make_async_copy(k_ref.at[:, first_cols], first.at[0, 0, 0], lfirst.at[0]),
        pltpu.make_async_copy(v_ref.at[:, first_cols], first.at[0, 1, 0], lfirst.at[1]),
    ]

    def first_messages(idx, chip):
        mine = kv.at[0, pl.ds(seq, 1)]
        return [
            pltpu.make_async_remote_copy(
                src_ref=src, dst_ref=mine, send_sem=ssem.at[idx], recv_sem=rsem.at[0, idx],
                device_id={"seq": chip * 2 + core}, device_id_type=MESH,
            )
            for src, core in ((mine, k), (first, 1 - k))
        ]

    def send_first():
        for copy in (*own_copies(0), *first_copies):
            copy.wait()

        @pl.when(jnp.logical_or(z0, x < 3))
        def _():
            for copy in first_messages(A_R, right_chip):
                copy.start()

        @pl.when(jnp.logical_or(z0, x == 0))
        def _():
            for copy in first_messages(A_L, left_chip):
                copy.start()

        @pl.when(z0)
        def _():
            for copy in first_messages(A_Z0, across_chip):
                copy.start()

    for copy in first_copies:
        copy.start()
    for h in range(AHEAD):
        for copy in own_copies(h):
            copy.start()

    for copy in keeps:
        copy.start()

    barrier = pltpu.get_barrier_semaphore()
    greeted = [{"seq": chip * 2 + m} for chip in (right_chip, left_chip, across_chip) for m in (0, 1)]
    for device in greeted + [partner]:
        pl.semaphore_signal(barrier, inc=1, device_id=device, device_id_type=MESH)
    pl.semaphore_wait(barrier, 7)

    send_first()

    for h in range(AHEAD):
        head_message(IN_K, h).start()
        head_message(IN_V, h).start()

    for copy in swaps:
        copy.start()

    sg_ref[:, VIS] = jnp.zeros((4, LAT, SPAN), BF16)
    low_ref[:, VIS] = jnp.zeros((4, LAT, SPAN), BF16)

    def prepare():
        for copy in keeps:
            copy.wait()
        for copy in swaps:
            copy.wait()

        @pl.loop(0, IMAGES)
        def _(i):
            for s in range(4):
                slot = jnp.int32(VIS)
                for v in range(VIS):
                    slot = jnp.where(vis_s[s // 2, s % 2, v] == i, v, slot)
                slot_s[s, i] = slot

    def when(cond):
        return pl.when(cond)

    def span_work(h):
        cols = pl.ds(pl.multiple_of(h * D, D), D)
        kvw[...] = kv[h, :, :, 0]
        tanh_gate = jnp.tanh(gate_ref[pl.ds(k * CORE_HEADS + h, 1), :])
        q_all = qw[:, cols]
        ct_all = cw[:, cols]
        go_all = (tanh_gate * ct_all.astype(F32)).astype(BF16)
        both_ref[:, :D] = go_all
        both_ref[:, D:] = ct_all
        spans = range(4)
        listed = [[vis_s[s // 2, s % 2, v] for v in range(VIS)] for s in spans]
        ids = [[jnp.maximum(i, 0) for i in row] for row in listed]
        q = [q_all[s * SPAN : (s + 1) * SPAN] for s in spans]
        go = [go_all[s * SPAN : (s + 1) * SPAN] for s in spans]
        kl = [jnp.concatenate([kvw[i, 0] for i in ids[s]], axis=0) for s in spans]
        vl = [jnp.concatenate([kvw[i, 1] for i in ids[s]], axis=0) for s in spans]
        raw = [dot(kl[s], q[s], 1, 1) for s in spans]
        wg = [dot(vl[s], go[s], 1, 1) for s in spans]
        p, low, sg = [], [], []
        for s in spans:
            rows = [raw[s][:LAT] * EXP2_SCALE]
            for v in range(1, VIS):
                bias = jnp.where(listed[s][v] >= 0, 0.0, NEG).astype(F32)
                rows.append(raw[s][v * LAT : (v + 1) * LAT] * EXP2_SCALE + bias)
            sc = jnp.concatenate(rows, axis=0)
            e = jnp.exp2(sc - jnp.max(sc, axis=0, keepdims=True))
            p.append(e * (1.0 / jnp.sum(e, axis=0, keepdims=True)))
            low.append(p[s].astype(BF16))
        for s in spans:
            dots = jnp.sum(low[s].astype(F32) * wg[s], axis=0, keepdims=True)
            sg.append((p[s] * (wg[s] - dots)).astype(BF16))
        for s in spans:
            low_ref[s, pl.ds(0, VIS)] = low[s].reshape(VIS, LAT, SPAN)
            sg_ref[s, pl.ds(0, VIS)] = sg[s].reshape(VIS, LAT, SPAN)
        dq = [dot(sg[s], kl[s], 0, 0) * (D**-0.5) for s in spans]
        for s in spans:
            dqs[pl.ds(s * SPAN, SPAN), cols] = dq[s].astype(BF16)

    def products(g):
        tanh_gate = jnp.tanh(gate_ref[pl.ds(k * CORE_HEADS + g, 1), :])
        q_all = qw[:, pl.ds(pl.multiple_of(g * D, D), D)]
        both = both_ref[...]

        def images(count):
            left, low_left, vals = [], [], []
            for i in range(count):
                slots = [slot_s[s, i] for s in range(4)]
                left.append(jnp.concatenate([sg_ref[s, slots[s]] for s in range(4)], axis=1))
                low_left.append(jnp.concatenate([low_ref[s, slots[s]] for s in range(4)], axis=1))
                vals.append(jnp.where(i < 2 * (c + 1), kvw[i, 1].astype(F32), 0.0))
            dk = dot(jnp.concatenate(left, axis=0), q_all, 1, 0) * (D**-0.5)
            obuf[g, pl.ds(0, count), 0, 0] = dk.reshape(count, LAT, D).astype(BF16)
            vw = dot(jnp.concatenate(low_left, axis=0), both, 1, 0)
            obuf[g, pl.ds(0, count), 1, 0] = vw[:, :D].reshape(count, LAT, D).astype(BF16)
            vals = jnp.concatenate(vals, axis=0)
            gate_sum = jnp.sum(vals * vw[:, D:], axis=0, keepdims=True)
            gpart[pl.ds(g, 1), :] = gate_sum * (1.0 - tanh_gate * tanh_gate)

        @when(z0)
        def _():
            images(8)

        @when(z1)
        def _():
            images(16)

    def add(g, b, slot):
        rows = pl.ds(2 * b, 2)
        obuf[g, rows] = (obuf[g, rows].astype(F32) + rbuf[g, slot].astype(F32)).astype(BF16)

    def swapped(g):
        other = c * 2 + (1 - k)
        head_got(IN_K, g, kv.at[g, other, 0, 0])
        head_got(IN_V, g, kv.at[g, other, 1, 0])

    def gather1(g):
        for copy in own_copies(g):
            copy.wait()
        swapped(g)

        @when(jnp.logical_or(z0, x < 3))
        def _():
            message(A_R, g).start()

        @when(jnp.logical_or(z0, x == 0))
        def _():
            message(A_L, g).start()

    def gather2(g):
        @when(jnp.logical_or(z0, x > 0))
        def _():
            got(A_R, g, blk(kv, g, hi + xl))

        @when(z0)
        def _():
            message(A_ZM, g).start()
            got(A_L, g, blk(kv, g, hi + xr))
            message(A_ZP, g).start()

    def gather_own(g):
        @when(z0)
        def _():
            message(A_Z0, g).start()

    def gather_forward(g):
        @when(jnp.logical_or(x == 1, jnp.logical_and(z1, x == 2)))
        def _():
            message(A_FR, g).start()

        @when(jnp.logical_and(z0, x == 0))
        def _():
            message(A_FL, g).start()

    def gather3(g):
        @when(z1)
        def _():
            got(A_ZM, g, blk(kv, g, xl))
            message(A_HR, g).start()
            got(A_ZP, g, blk(kv, g, xr))
            message(A_HL, g).start()

    def gather4(g):
        @when(z1)
        def _():
            got(A_Z0, g, blk(kv, g, x))
            got(A_HR, g, img(kv, g, xo, 0))
            got(A_HL, g, img(kv, g, xo, 1))

        @when(jnp.logical_or(x == 2, jnp.logical_and(z1, x == 3)))
        def _():
            got(A_FR, g, blk(kv, g, hi + xo))

        @when(jnp.logical_and(z0, x == 3))
        def _():
            got(A_FL, g, blk(kv, g, xo))

        @when(jnp.logical_and(z1, x == 3))
        def _():
            got(A_L, g, blk(kv, g, 4))

    def back1(g):
        @when(z1)
        def _():
            message(R_HR, g).start()
            message(R_HL, g).start()
            message(R_Z0, g).start()

        @when(jnp.logical_or(x == 2, jnp.logical_and(z1, x == 3)))
        def _():
            message(R_FR, g).start()

        @when(jnp.logical_and(z0, x == 3))
        def _():
            message(R_FL, g).start()

        @when(jnp.logical_and(z1, x == 3))
        def _():
            message(R_L, g).start()

    def back2(g):
        @when(z1)
        def _():
            got(R_HR, g, rbuf.at[g, 7, pl.ds(0, 1)])
            row = 2 * xl
            obuf[g, row] = (obuf[g, row].astype(F32) + rbuf[g, 7, 0].astype(F32)).astype(BF16)
            message(R_ZM, g).start()
            got(R_HL, g, rbuf.at[g, 7, pl.ds(1, 1)])
            row = 2 * xr + 1
            obuf[g, row] = (obuf[g, row].astype(F32) + rbuf[g, 7, 1].astype(F32)).astype(BF16)
            message(R_ZP, g).start()

            @when(jnp.logical_or(x == 1, x == 2))
            def _():
                got(R_FR, g, rbuf.at[g, 2])
                add(g, 4 + xl, 2)

            @when(x > 0)
            def _():
                message(R_R, g).start()

    def back3(g):
        @when(z0)
        def _():
            @when(x == 1)
            def _():
                got(R_FR, g, rbuf.at[g, 2])
                add(g, xl, 2)

            @when(x == 0)
            def _():
                got(R_FL, g, rbuf.at[g, 3])
                add(g, xr, 3)

            got(R_ZM, g, rbuf.at[g, 5])
            add(g, xl, 5)
            message(R_R, g).start()
            got(R_ZP, g, rbuf.at[g, 6])
            add(g, xr, 6)
            message(R_L, g).start()

    def back4(g):
        own = pl.ds(2 * c, 2)

        def finish(slots):
            total = obuf[g, own].astype(F32)
            for slot in slots:
                total += rbuf[g, slot].astype(F32)
            fin[:, :, :, pl.ds(pl.multiple_of(g * D, D), D)] = total[:, :, 0].astype(BF16)

        @when(z0)
        def _():
            got(R_Z0, g, rbuf.at[g, 4])
            got(R_R, g, rbuf.at[g, 0])
            got(R_L, g, rbuf.at[g, 1])
            finish((4, 0, 1))

        @when(z1)
        def _():
            @when(x < 3)
            def _():
                got(R_R, g, rbuf.at[g, 0])

            @when(x == 0)
            def _():
                got(R_L, g, rbuf.at[g, 1])
                finish((0, 1))

            @when(jnp.logical_or(x == 1, x == 2))
            def _():
                finish((0,))

            @when(x == 3)
            def _():
                finish(())

    odd = lax.rem(x, 2)
    pairs = (
        across,
        at_chip(z * 4 + x + 1 - 2 * odd),
        at_chip(z * 4 + lax.rem(x + 3 + 2 * odd, 4)),
    )

    def gate_step(i):
        return pltpu.make_async_remote_copy(
            src_ref=gsum.at[i], dst_ref=gall.at[i], send_sem=gsend.at[i], recv_sem=grecv.at[i],
            device_id=pairs[i], device_id_type=MESH,
        )

    gate_local = pltpu.make_async_copy(gsum.at[3], gg_ref.at[k], glast.at[0])
    gate_remote = pltpu.make_async_remote_copy(
        src_ref=gsum.at[3], dst_ref=gg_ref.at[k], send_sem=glast.at[1], recv_sem=glast.at[2],
        device_id=partner, device_id_type=MESH,
    )

    def iteration(t):
        fixed = isinstance(t, int)

        def stage(offset, run, first=0):
            if fixed:
                if offset + first <= t < CHUNKS + offset:
                    run(t - offset)
                return
            conditions = []
            if offset + first > COMPUTE:
                conditions.append(t >= offset + first)
            if offset < COMPUTE:
                conditions.append(t < CHUNKS + offset)
            if not conditions:
                run(t - offset)
            else:
                pl.when(functools.reduce(jnp.logical_and, conditions))(lambda: run(t - offset))

        def fetch(g):
            for copy in own_copies(g):
                copy.start()
            head_message(IN_K, g).start()
            head_message(IN_V, g).start()

        stage(-AHEAD, lambda g: fetch(g))
        stage(0, gather1, 1)
        stage(GATHER2, gather2)
        stage(0, gather_own, 1)
        stage(GATHER2, gather_forward)
        stage(BACK2, back2)
        stage(BACK3, back3)
        stage(LAST, back4)
        if not fixed:
            gather4(t - COMPUTE)
            span_work(t - COMPUTE)
        stage(GATHER3, gather3)
        if not fixed:
            products(t - COMPUTE)
            back1(t - COMPUTE)

    for t in range(COMPUTE - 1):
        iteration(t)
    prepare()
    iteration(COMPUTE - 1)
    swapped(0)

    @pl.loop(COMPUTE, COMPUTE + CHUNKS)
    def _(t):
        iteration(t)

    for copy in query_copies():
        copy.start()
    gsum[0] = gpart[...]
    gate_step(0).start()
    for i in range(LAST - COMPUTE):
        iteration(COMPUTE + CHUNKS + i)
        if i < 3:
            gate_step(i).wait_recv()
            gsum[i + 1] = gsum[i] + gall[i]
            if i < 2:
                gate_step(i + 1).start()
            else:
                gate_local.start()
                gate_remote.start()

    for copy in result_copies():
        copy.start()
    for i in range(3):
        gate_step(i).wait_send()

    def done(idx):
        half = idx in (A_HR, A_HL, R_HR, R_HL)
        sent = kv.at[:, pl.ds(0, 1 if half else 2)]
        pltpu.make_async_remote_copy(
            src_ref=sent, dst_ref=sent, send_sem=ssem.at[idx], recv_sem=rsem.at[0, idx],
            device_id=partner, device_id_type=MESH,
        ).wait_send()

    @when(z0)
    def _():
        for idx in (A_Z0, A_ZM, A_ZP):
            done(idx)

    @when(z1)
    def _():
        for idx in (A_HR, A_HL, R_HR, R_HL, R_Z0, R_ZM, R_ZP):
            done(idx)

    @when(jnp.logical_or(z0, x < 3))
    def _():
        done(A_R)

    @when(jnp.logical_or(z0, x == 0))
    def _():
        done(A_L)

    @when(jnp.logical_or(x == 1, jnp.logical_and(z1, x == 2)))
    def _():
        done(A_FR)

    @when(jnp.logical_and(z0, x == 0))
    def _():
        done(A_FL)

    @when(jnp.logical_or(x == 2, jnp.logical_and(z1, x == 3)))
    def _():
        done(R_FR)

    @when(jnp.logical_and(z0, x == 3))
    def _():
        done(R_FL)

    @when(jnp.logical_or(z0, x == 3))
    def _():
        done(R_L)

    @when(jnp.logical_or(z0, x > 0))
    def _():
        done(R_R)

    swap_all(DQ, dqs.at[their_rows], qg_ref.at[:, their_cols]).wait_send()
    swap_all(OUT_K, fin.at[1 - k, 0], kg_ref.at[:, their_cols]).wait_send()
    swap_all(OUT_V, fin.at[1 - k, 1], vg_ref.at[:, their_cols]).wait_send()
    swap_all(IN_K, k_ref.at[:, their_cols], kg_ref.at[:, their_cols]).wait_send()
    swap_all(IN_V, v_ref.at[:, their_cols], vg_ref.at[:, their_cols]).wait_send()
    for idx, ref in ((DQ, qg_ref), (OUT_K, kg_ref), (OUT_V, vg_ref)):
        swap_all(idx, ref.at[:, their_cols], ref.at[:, their_cols]).wait_recv()
    pltpu.make_async_copy(qg_ref.at[:, half_cols], qg_ref.at[:, half_cols], lout.at[0]).wait()
    pltpu.make_async_copy(kg_ref.at[:, half_cols], kg_ref.at[:, half_cols], lout.at[1]).wait()
    pltpu.make_async_copy(vg_ref.at[:, half_cols], vg_ref.at[:, half_cols], lout.at[2]).wait()

    gate_local.wait()
    gate_remote.wait_send()
    pltpu.make_async_remote_copy(
        src_ref=gsum.at[3], dst_ref=gg_ref.at[1 - k], send_sem=glast.at[1], recv_sem=glast.at[2],
        device_id=partner, device_id_type=MESH,
    ).wait_recv()


def place(a0, a1, a2, a3, b0, b1, b2, b3, m0, m1, m2, m3, sem):
    held = (m0, m1, m2, m3)
    into = [
        pltpu.make_async_copy(a, m, sem.at[0, i]) for i, (a, m) in enumerate(zip((a0, a1, a2, a3), held))
    ]
    out = [
        pltpu.make_async_copy(m, b, sem.at[1, i]) for i, (m, b) in enumerate(zip(held, (b0, b1, b2, b3)))
    ]
    for copy in into:
        copy.start()
    for copy, after in zip(into, out):
        copy.wait()
        after.start()
    for copy in out:
        copy.wait()


def shards(queries, keys, values, cotangent, gate, visible):
    tokens, width = queries.shape
    half = width // 2
    any_spec = pl.BlockSpec(memory_space=pl.ANY)
    hbm_spec = pl.BlockSpec(memory_space=pltpu.HBM)
    dma = pltpu.SemaphoreType.DMA
    out_shape = (
        jax.ShapeDtypeStruct((tokens, width), BF16),
        jax.ShapeDtypeStruct((LAT, width), BF16),
        jax.ShapeDtypeStruct((LAT, width), BF16),
        jax.ShapeDtypeStruct((2, CORE_HEADS, D), F32),
    )
    results = pl.pallas_call(
        kernel,
        out_shape=out_shape,
        in_specs=[hbm_spec] * 6,
        out_specs=(any_spec,) * 4,
        scratch_shapes=[
            pltpu.VMEM((2 * tokens, half), BF16),
            pltpu.VMEM((2 * tokens, half), BF16),
            pltpu.VMEM((CHUNKS, IMAGES, 2, N, LAT, D), BF16),
            pltpu.VMEM((CHUNKS, IMAGES, 2, N, LAT, D), BF16),
            pltpu.VMEM((CHUNKS, 8, 2, 2, N, LAT, D), BF16),
            pltpu.VMEM((IMAGES, 2, LAT, D), BF16),
            pltpu.VMEM((4, VIS + 1, LAT, SPAN), BF16),
            pltpu.VMEM((4, VIS + 1, LAT, SPAN), BF16),
            pltpu.VMEM((2 * tokens, 2 * D), BF16),
            pltpu.VMEM((2 * tokens, half), BF16),
            pltpu.VMEM((2, 2, LAT, half), BF16),
            pltpu.VMEM((CORE_HEADS, D), F32),
            pltpu.VMEM((3, CORE_HEADS, D), F32),
            pltpu.VMEM((4, CORE_HEADS, D), F32),
            pltpu.VMEM((1, 2, N, LAT, D), BF16),
            pltpu.VMEM((2 * CORE_HEADS, D), F32),
            pltpu.SMEM((2, 2, VIS), jnp.int32),
            pltpu.SMEM((4, IMAGES), jnp.int32),
            dma((MESSAGES,)),
            dma((CHUNKS, MESSAGES)),
            dma((5,)),
            dma((CORE_HEADS, 2)),
            dma((3,)),
            dma((CORE_HEADS, 2)),
            dma((3,)),
            dma((2,)),
            dma((3,)),
            dma((3,)),
            dma((4,)),
            dma((3,)),
            dma((3,)),
            dma((3,)),
        ],
        compiler_params=pltpu.CompilerParams(
            collective_id=0, has_side_effects=True, vmem_limit_bytes=63 * 1024 * 1024
        ),
        name="cross_attention_backward",
    )(queries, keys, values, cotangent, gate.reshape(2 * CORE_HEADS, D), visible)
    query_grad, key_grad, value_grad, gate_grad = pl.pallas_call(
        place,
        out_shape=out_shape,
        in_specs=[any_spec] * 4,
        out_specs=(hbm_spec,) * 4,
        scratch_shapes=[pltpu.VMEM(o.shape, o.dtype) for o in out_shape] + [dma((2, 4))],
        compiler_params=pltpu.CompilerParams(vmem_limit_bytes=63 * 1024 * 1024),
        name="place_results",
    )(*results)
    return query_grad, key_grad, value_grad, gate_grad.reshape(width)


def solution(mesh):
    placed = (
        P(("dp", "seq"), "tensor"),
        P(("dp", "seq"), "tensor"),
        P(("dp", "seq"), "tensor"),
        P(("dp", "seq"), "tensor"),
        P("tensor"),
        P(("dp", "seq"), None),
    )
    return jax.shard_map(
        shards,
        mesh=mesh,
        in_specs=placed,
        out_specs=(
            P(("dp", "seq"), "tensor"),
            P(("dp", "seq"), "tensor"),
            P(("dp", "seq"), "tensor"),
            P(("dp", "tensor")),
        ),
        check_vma=False,
    )
```

```python
import functools

import jax
import jax.numpy as jnp
from jax import lax
from jax.experimental import pallas as pl
from jax.experimental.pallas import tpu as pltpu
from jax.sharding import PartitionSpec as P

MESH = pl.DeviceIdType.MESH
D = 128
LAT = 64
SPAN = 128
VIS = 4
CORE_HEADS = 8
N = 1
CHUNKS = CORE_HEADS // N
AHEAD = 2
IMAGES = 16
GATHER2, GATHER3, COMPUTE, BACK2, BACK3, LAST = 1, 2, 3, 5, 7, 9
NEG = -1e30
EXP2_SCALE = D**-0.5 * 1.4426950408889634
F32, BF16 = jnp.float32, jnp.bfloat16

(
    A_R, A_L, A_FR, A_FL, A_Z0, A_ZM, A_ZP, A_HR, A_HL,
    R_R, R_L, R_FR, R_FL, R_Z0, R_ZM, R_ZP, R_HR, R_HL,
) = range(18)
MESSAGES = 18
DQ, OUT, IN_K, IN_V, IN_Q, IN_C = range(6)


def dot(a, b, ca, cb):
    return lax.dot_general(a, b, (((ca,), (cb,)), ((), ())), preferred_element_type=F32)


def kernel(
    q_ref, k_ref, v_ref, ct_ref, gate_hbm, vis_ref,
    qg_ref, kg_ref, vg_ref, gg_ref,
    qw, cw, kv, obuf, rbuf, kvw, sg_ref, low_ref, both_ref, dqs, fin, gpart, gall, gsum, first, gate_ref, qct, kvt, dq_in, fin_in, gate_in, vis_s, slot_s,
    ssem, rsem, hsend, hrecv, hout, lsem, lout, lfirst, lstage, lland, esend, erecv, elocal, gsend, grecv, glast,
):
    seq = lax.axis_index("seq")
    c, k = lax.div(seq, 2), lax.rem(seq, 2)
    z, x = lax.div(c, 4), lax.rem(c, 4)
    xr, xl = lax.rem(x + 1, 4), lax.rem(x + 3, 4)
    xo = lax.rem(x + 2, 4)
    z0, z1 = z == 0, z == 1

    def at_chip(chip):
        return {"seq": chip * 2 + k}

    right_chip, left_chip, across_chip = z * 4 + xr, z * 4 + xl, (1 - z) * 4 + x
    right, left, across = at_chip(right_chip), at_chip(left_chip), at_chip(across_chip)
    partner = {"seq": c * 2 + (1 - k)}

    def send(idx, g, src, dst, dev):
        return pltpu.make_async_remote_copy(
            src_ref=src, dst_ref=dst, send_sem=ssem.at[idx], recv_sem=rsem.at[g, idx],
            device_id=dev, device_id_type=MESH,
        )

    def blk(buf, g, b):
        return buf.at[g, pl.ds(2 * b, 2)]

    def img(buf, g, b, half):
        return buf.at[g, pl.ds(2 * b + half, 1)]

    hi = z * 4

    def message(idx, g):
        own = blk(kv, g, c)
        if idx == A_R:
            return send(idx, g, own, own, right)
        if idx == A_L:
            return send(idx, g, own, own, left)
        if idx == A_FR:
            b = blk(kv, g, hi + xl)
            return send(idx, g, b, b, right)
        if idx == A_FL:
            b = blk(kv, g, hi + xr)
            return send(idx, g, b, b, left)
        if idx == A_Z0:
            return send(idx, g, own, own, across)
        if idx == A_ZM:
            b = blk(kv, g, xl)
            return send(idx, g, b, b, across)
        if idx == A_ZP:
            b = blk(kv, g, xr)
            return send(idx, g, b, b, across)
        if idx == A_HR:
            b = img(kv, g, xl, 0)
            return send(idx, g, b, b, right)
        if idx == A_HL:
            b = img(kv, g, xr, 1)
            return send(idx, g, b, b, left)
        if idx == R_R:
            return send(idx, g, blk(obuf, g, hi + xl), rbuf.at[g, 0], left)
        if idx == R_L:
            return send(idx, g, blk(obuf, g, hi + xr), rbuf.at[g, 1], right)
        if idx == R_FR:
            return send(idx, g, blk(obuf, g, hi + xo), rbuf.at[g, 2], left)
        if idx == R_FL:
            return send(idx, g, blk(obuf, g, hi + xo), rbuf.at[g, 3], right)
        if idx == R_Z0:
            return send(idx, g, blk(obuf, g, x), rbuf.at[g, 4], across)
        if idx == R_ZM:
            return send(idx, g, blk(obuf, g, xl), rbuf.at[g, 5], across)
        if idx == R_ZP:
            return send(idx, g, blk(obuf, g, xr), rbuf.at[g, 6], across)
        if idx == R_HR:
            return send(idx, g, img(obuf, g, xo, 0), rbuf.at[g, 7, pl.ds(0, 1)], left)
        if idx == R_HL:
            return send(idx, g, img(obuf, g, xo, 1), rbuf.at[g, 7, pl.ds(1, 1)], right)
        raise ValueError(idx)

    def swap(idx, h, src, dst):
        return pltpu.make_async_remote_copy(
            src_ref=src, dst_ref=dst, send_sem=hsend.at[idx], recv_sem=hrecv.at[h, idx - IN_K],
            device_id=partner, device_id_type=MESH,
        )

    def swap_all(idx, src, dst):
        return pltpu.make_async_remote_copy(
            src_ref=src, dst_ref=dst, send_sem=hsend.at[idx], recv_sem=hout.at[idx],
            device_id=partner, device_id_type=MESH,
        )

    def head_message(idx, h):
        g, n = h, 0
        theirs = head_cols(0, h)
        if idx == DQ:
            return swap_all(DQ, dqs.at[their_rows, theirs], dq_in.at[:, theirs])
        if idx == OUT:
            return swap_all(OUT, fin.at[1 - k, :, :, theirs], fin_in.at[:, :, theirs])
        if idx == IN_Q:
            return swap(idx, h, qct.at[0, :, theirs], qw.at[my_rows, theirs])
        if idx == IN_C:
            return swap(idx, h, qct.at[1, :, theirs], cw.at[my_rows, theirs])
        return swap(idx, h, kvt.at[idx - IN_K, :, theirs], kv.at[g, seq, idx - IN_K, n])

    def head_got(idx, h, dst):
        swap(idx, h, dst, dst).wait_recv()

    def head_cols(core, h):
        return pl.ds(pl.multiple_of((core * CORE_HEADS + h) * D, D), D)

    def got(idx, g, dst):
        send(idx, g, dst, dst, partner).wait_recv()

    def own_copies(h):
        g, n = h, 0
        mine = head_cols(k, h)
        return (
            pltpu.make_async_copy(k_ref.at[:, mine], kv.at[g, seq, 0, n], lsem.at[h, 0]),
            pltpu.make_async_copy(v_ref.at[:, mine], kv.at[g, seq, 1, n], lsem.at[h, 1]),
        )

    half_width = CORE_HEADS * D
    half_cols = pl.ds(pl.multiple_of(k * half_width, half_width), half_width)
    their_cols = pl.ds(pl.multiple_of((1 - k) * half_width, half_width), half_width)
    my_rows, their_rows = pl.ds(k * 256, 256), pl.ds((1 - k) * 256, 256)

    def result_copies():
        results = ((1, fin.at[k, 0], kg_ref), (2, fin.at[k, 1], vg_ref))
        return [
            pltpu.make_async_copy(src, ref.at[:, half_cols], lout.at[i]) for i, src, ref in results
        ]

    def query_copy():
        return pltpu.make_async_copy(dqs.at[my_rows], qg_ref.at[:, half_cols], lout.at[0])

    def early(i, src, dst):
        return pltpu.make_async_remote_copy(
            src_ref=src, dst_ref=dst, send_sem=esend.at[i], recv_sem=erecv.at[i],
            device_id=partner, device_id_type=MESH,
        )

    swaps = [
        early(0, vis_ref, vis_s.at[k]),
    ]
    theirs_staged = [
        pltpu.make_async_copy(k_ref.at[:, their_cols], kvt.at[0], lstage.at[0]),
        pltpu.make_async_copy(v_ref.at[:, their_cols], kvt.at[1], lstage.at[1]),
        pltpu.make_async_copy(q_ref.at[:, their_cols], qct.at[0], lstage.at[2]),
        pltpu.make_async_copy(ct_ref.at[:, their_cols], qct.at[1], lstage.at[3]),
    ]
    keeps = [
        pltpu.make_async_copy(vis_ref, vis_s.at[k], elocal.at[0]),
        pltpu.make_async_copy(q_ref.at[:, half_cols], qw.at[my_rows], elocal.at[1]),
        pltpu.make_async_copy(ct_ref.at[:, half_cols], cw.at[my_rows], elocal.at[2]),
        pltpu.make_async_copy(gate_hbm, gate_ref, elocal.at[3]),
    ]

    first_cols = head_cols(1 - k, 0)
    first_copies = [
        pltpu.make_async_copy(k_ref.at[:, first_cols], first.at[0, 0, 0], lfirst.at[0]),
        pltpu.make_async_copy(v_ref.at[:, first_cols], first.at[0, 1, 0], lfirst.at[1]),
    ]

    def first_messages(idx, chip):
        mine = kv.at[0, pl.ds(seq, 1)]
        return [
            pltpu.make_async_remote_copy(
                src_ref=src, dst_ref=mine, send_sem=ssem.at[idx], recv_sem=rsem.at[0, idx],
                device_id={"seq": chip * 2 + core}, device_id_type=MESH,
            )
            for src, core in ((mine, k), (first, 1 - k))
        ]

    def send_first():
        for copy in (*own_copies(0), *first_copies):
            copy.wait()

        @pl.when(jnp.logical_or(z0, x < 3))
        def _():
            for copy in first_messages(A_R, right_chip):
                copy.start()

        @pl.when(jnp.logical_or(z0, x == 0))
        def _():
            for copy in first_messages(A_L, left_chip):
                copy.start()

        @pl.when(z0)
        def _():
            for copy in first_messages(A_Z0, across_chip):
                copy.start()

    for copy in first_copies:
        copy.start()
    for h in range(AHEAD):
        for copy in own_copies(h):
            copy.start()

    for copy in theirs_staged + keeps:
        copy.start()

    barrier = pltpu.get_barrier_semaphore()
    greeted = [{"seq": chip * 2 + m} for chip in (right_chip, left_chip, across_chip) for m in (0, 1)]
    for device in greeted + [partner]:
        pl.semaphore_signal(barrier, inc=1, device_id=device, device_id_type=MESH)
    pl.semaphore_wait(barrier, 7)

    send_first()

    for copy in theirs_staged:
        copy.wait()
    for h in range(AHEAD):
        for idx in (IN_K, IN_V, IN_Q, IN_C):
            head_message(idx, h).start()

    for copy in swaps:
        copy.start()

    sg_ref[:, VIS] = jnp.zeros((4, LAT, SPAN), BF16)
    low_ref[:, VIS] = jnp.zeros((4, LAT, SPAN), BF16)

    def prepare():
        for copy in keeps:
            copy.wait()
        for copy in swaps:
            copy.wait()

        @pl.loop(0, IMAGES)
        def _(i):
            for s in range(4):
                slot = jnp.int32(VIS)
                for v in range(VIS):
                    slot = jnp.where(vis_s[s // 2, s % 2, v] == i, v, slot)
                slot_s[s, i] = slot

    def when(cond):
        return pl.when(cond)

    def span_work(h):
        cols = pl.ds(pl.multiple_of(h * D, D), D)
        kvw[...] = kv[h, :, :, 0]
        tanh_gate = jnp.tanh(gate_ref[pl.ds(k * CORE_HEADS + h, 1), :])
        q_all = qw[:, cols]
        ct_all = cw[:, cols]
        go_all = (tanh_gate * ct_all.astype(F32)).astype(BF16)
        both_ref[:, :D] = go_all
        both_ref[:, D:] = ct_all
        spans = range(4)
        listed = [[vis_s[s // 2, s % 2, v] for v in range(VIS)] for s in spans]
        ids = [[jnp.maximum(i, 0) for i in row] for row in listed]
        q = [q_all[s * SPAN : (s + 1) * SPAN] for s in spans]
        go = [go_all[s * SPAN : (s + 1) * SPAN] for s in spans]
        kl = [jnp.concatenate([kvw[i, 0] for i in ids[s]], axis=0) for s in spans]
        vl = [jnp.concatenate([kvw[i, 1] for i in ids[s]], axis=0) for s in spans]
        raw = [dot(kl[s], q[s], 1, 1) for s in spans]
        wg = [dot(vl[s], go[s], 1, 1) for s in spans]
        p, low, sg = [], [], []
        for s in spans:
            rows = [raw[s][:LAT] * EXP2_SCALE]
            for v in range(1, VIS):
                bias = jnp.where(listed[s][v] >= 0, 0.0, NEG).astype(F32)
                rows.append(raw[s][v * LAT : (v + 1) * LAT] * EXP2_SCALE + bias)
            sc = jnp.concatenate(rows, axis=0)
            e = jnp.exp2(sc - jnp.max(sc, axis=0, keepdims=True))
            p.append(e * (1.0 / jnp.sum(e, axis=0, keepdims=True)))
            low.append(p[s].astype(BF16))
        for s in spans:
            dots = jnp.sum(low[s].astype(F32) * wg[s], axis=0, keepdims=True)
            sg.append((p[s] * (wg[s] - dots)).astype(BF16))
        for s in spans:
            low_ref[s, pl.ds(0, VIS)] = low[s].reshape(VIS, LAT, SPAN)
            sg_ref[s, pl.ds(0, VIS)] = sg[s].reshape(VIS, LAT, SPAN)
        dq = [dot(sg[s], kl[s], 0, 0) * (D**-0.5) for s in spans]
        for s in spans:
            dqs[pl.ds(s * SPAN, SPAN), cols] = dq[s].astype(BF16)

    def products(g):
        tanh_gate = jnp.tanh(gate_ref[pl.ds(k * CORE_HEADS + g, 1), :])
        q_all = qw[:, pl.ds(pl.multiple_of(g * D, D), D)]
        both = both_ref[...]

        def images(count):
            left, low_left, vals = [], [], []
            for i in range(count):
                slots = [slot_s[s, i] for s in range(4)]
                left.append(jnp.concatenate([sg_ref[s, slots[s]] for s in range(4)], axis=1))
                low_left.append(jnp.concatenate([low_ref[s, slots[s]] for s in range(4)], axis=1))
                vals.append(jnp.where(i < 2 * (c + 1), kvw[i, 1].astype(F32), 0.0))
            dk = dot(jnp.concatenate(left, axis=0), q_all, 1, 0) * (D**-0.5)
            obuf[g, pl.ds(0, count), 0, 0] = dk.reshape(count, LAT, D).astype(BF16)
            vw = dot(jnp.concatenate(low_left, axis=0), both, 1, 0)
            obuf[g, pl.ds(0, count), 1, 0] = vw[:, :D].reshape(count, LAT, D).astype(BF16)
            vals = jnp.concatenate(vals, axis=0)
            gate_sum = jnp.sum(vals * vw[:, D:], axis=0, keepdims=True)
            gpart[pl.ds(g, 1), :] = gate_sum * (1.0 - tanh_gate * tanh_gate)

        @when(z0)
        def _():
            images(8)

        @when(z1)
        def _():
            images(16)

    def add(g, b, slot):
        rows = pl.ds(2 * b, 2)
        obuf[g, rows] = (obuf[g, rows].astype(F32) + rbuf[g, slot].astype(F32)).astype(BF16)

    def swapped(g):
        other = c * 2 + (1 - k)
        head_got(IN_K, g, kv.at[g, other, 0, 0])
        head_got(IN_V, g, kv.at[g, other, 1, 0])

    def swapped_queries(g):
        theirs = head_cols(0, g)
        head_got(IN_Q, g, qw.at[their_rows, theirs])
        head_got(IN_C, g, cw.at[their_rows, theirs])

    def gather1(g):
        for copy in own_copies(g):
            copy.wait()
        swapped(g)

        @when(jnp.logical_or(z0, x < 3))
        def _():
            message(A_R, g).start()

        @when(jnp.logical_or(z0, x == 0))
        def _():
            message(A_L, g).start()

    def gather2(g):
        @when(jnp.logical_or(z0, x > 0))
        def _():
            got(A_R, g, blk(kv, g, hi + xl))

        @when(z0)
        def _():
            message(A_ZM, g).start()
            got(A_L, g, blk(kv, g, hi + xr))
            message(A_ZP, g).start()

    def gather_own(g):
        @when(z0)
        def _():
            message(A_Z0, g).start()

    def gather_forward(g):
        @when(jnp.logical_or(x == 1, jnp.logical_and(z1, x == 2)))
        def _():
            message(A_FR, g).start()

        @when(jnp.logical_and(z0, x == 0))
        def _():
            message(A_FL, g).start()

    def gather3(g):
        @when(z1)
        def _():
            got(A_ZM, g, blk(kv, g, xl))
            message(A_HR, g).start()
            got(A_ZP, g, blk(kv, g, xr))
            message(A_HL, g).start()

    def gather4(g):
        @when(z1)
        def _():
            got(A_Z0, g, blk(kv, g, x))
            got(A_HR, g, img(kv, g, xo, 0))
            got(A_HL, g, img(kv, g, xo, 1))

        @when(jnp.logical_or(x == 2, jnp.logical_and(z1, x == 3)))
        def _():
            got(A_FR, g, blk(kv, g, hi + xo))

        @when(jnp.logical_and(z0, x == 3))
        def _():
            got(A_FL, g, blk(kv, g, xo))

        @when(jnp.logical_and(z1, x == 3))
        def _():
            got(A_L, g, blk(kv, g, 4))

    def back1(g):
        @when(z1)
        def _():
            message(R_HR, g).start()
            message(R_HL, g).start()
            message(R_Z0, g).start()

        @when(jnp.logical_or(x == 2, jnp.logical_and(z1, x == 3)))
        def _():
            message(R_FR, g).start()

        @when(jnp.logical_and(z0, x == 3))
        def _():
            message(R_FL, g).start()

        @when(jnp.logical_and(z1, x == 3))
        def _():
            message(R_L, g).start()

    def back2(g):
        @when(z1)
        def _():
            got(R_HR, g, rbuf.at[g, 7, pl.ds(0, 1)])
            row = 2 * xl
            obuf[g, row] = (obuf[g, row].astype(F32) + rbuf[g, 7, 0].astype(F32)).astype(BF16)
            message(R_ZM, g).start()
            got(R_HL, g, rbuf.at[g, 7, pl.ds(1, 1)])
            row = 2 * xr + 1
            obuf[g, row] = (obuf[g, row].astype(F32) + rbuf[g, 7, 1].astype(F32)).astype(BF16)
            message(R_ZP, g).start()

            @when(jnp.logical_or(x == 1, x == 2))
            def _():
                got(R_FR, g, rbuf.at[g, 2])
                add(g, 4 + xl, 2)

            @when(x > 0)
            def _():
                message(R_R, g).start()

    def back3(g):
        @when(z0)
        def _():
            @when(x == 1)
            def _():
                got(R_FR, g, rbuf.at[g, 2])
                add(g, xl, 2)

            @when(x == 0)
            def _():
                got(R_FL, g, rbuf.at[g, 3])
                add(g, xr, 3)

            got(R_ZM, g, rbuf.at[g, 5])
            add(g, xl, 5)
            message(R_R, g).start()
            got(R_ZP, g, rbuf.at[g, 6])
            add(g, xr, 6)
            message(R_L, g).start()

    def back4(g):
        own = pl.ds(2 * c, 2)

        def finish(slots):
            total = obuf[g, own].astype(F32)
            for slot in slots:
                total += rbuf[g, slot].astype(F32)
            fin[:, :, :, pl.ds(pl.multiple_of(g * D, D), D)] = total[:, :, 0].astype(BF16)

        @when(z0)
        def _():
            got(R_Z0, g, rbuf.at[g, 4])
            got(R_R, g, rbuf.at[g, 0])
            got(R_L, g, rbuf.at[g, 1])
            finish((4, 0, 1))

        @when(z1)
        def _():
            @when(x < 3)
            def _():
                got(R_R, g, rbuf.at[g, 0])

            @when(x == 0)
            def _():
                got(R_L, g, rbuf.at[g, 1])
                finish((0, 1))

            @when(jnp.logical_or(x == 1, x == 2))
            def _():
                finish((0,))

            @when(x == 3)
            def _():
                finish(())

        head_message(OUT, g).start()

    odd = lax.rem(x, 2)
    pairs = (
        across,
        at_chip(z * 4 + x + 1 - 2 * odd),
        at_chip(z * 4 + lax.rem(x + 3 + 2 * odd, 4)),
    )

    def gate_step(i):
        return pltpu.make_async_remote_copy(
            src_ref=gsum.at[i], dst_ref=gall.at[i], send_sem=gsend.at[i], recv_sem=grecv.at[i],
            device_id=pairs[i], device_id_type=MESH,
        )

    gate_local = pltpu.make_async_copy(gsum.at[3], gg_ref.at[k], glast.at[0])
    gate_remote = pltpu.make_async_remote_copy(
        src_ref=gsum.at[3], dst_ref=gate_in, send_sem=glast.at[1], recv_sem=glast.at[2],
        device_id=partner, device_id_type=MESH,
    )
    landed = [
        pltpu.make_async_copy(dq_in, qg_ref.at[:, their_cols], lland.at[0]),
        pltpu.make_async_copy(fin_in.at[0], kg_ref.at[:, their_cols], lland.at[1]),
        pltpu.make_async_copy(fin_in.at[1], vg_ref.at[:, their_cols], lland.at[2]),
        pltpu.make_async_copy(gate_in, gg_ref.at[1 - k], lland.at[3]),
    ]

    def iteration(t):
        fixed = isinstance(t, int)

        def stage(offset, run, first=0):
            if fixed:
                if offset + first <= t < CHUNKS + offset:
                    run(t - offset)
                return
            conditions = []
            if offset + first > COMPUTE:
                conditions.append(t >= offset + first)
            if offset < COMPUTE:
                conditions.append(t < CHUNKS + offset)
            if not conditions:
                run(t - offset)
            else:
                pl.when(functools.reduce(jnp.logical_and, conditions))(lambda: run(t - offset))

        def fetch(g):
            for copy in own_copies(g):
                copy.start()
            for idx in (IN_K, IN_V, IN_Q, IN_C):
                head_message(idx, g).start()

        stage(-AHEAD, lambda g: fetch(g))
        stage(0, gather1, 1)
        stage(GATHER2, gather2)
        stage(0, gather_own, 1)
        stage(GATHER2, gather_forward)
        stage(BACK2, back2)
        stage(BACK3, back3)
        stage(LAST, back4)
        if not fixed:
            gather4(t - COMPUTE)
            swapped_queries(t - COMPUTE)
            span_work(t - COMPUTE)
        stage(GATHER3, gather3)
        if not fixed:
            head_message(DQ, t - COMPUTE).start()
            products(t - COMPUTE)
            back1(t - COMPUTE)

    for t in range(COMPUTE - 1):
        iteration(t)
    prepare()
    iteration(COMPUTE - 1)
    swapped(0)

    @pl.loop(COMPUTE, COMPUTE + CHUNKS)
    def _(t):
        iteration(t)

    query_copy().start()
    gsum[0] = gpart[...]
    gate_step(0).start()
    for i in range(LAST - COMPUTE):
        iteration(COMPUTE + CHUNKS + i)
        if i < 3:
            gate_step(i).wait_recv()
            gsum[i + 1] = gsum[i] + gall[i]
            if i < 2:
                gate_step(i + 1).start()
            else:
                gate_local.start()
                gate_remote.start()

    for copy in result_copies():
        copy.start()
    swap_all(DQ, dqs.at[their_rows], dq_in).wait_recv()
    landed[0].start()
    gate_remote.wait_recv()
    landed[3].start()
    swap_all(OUT, fin.at[1 - k], fin_in).wait_recv()
    landed[1].start()
    landed[2].start()

    for i in range(3):
        gate_step(i).wait_send()

    def done(idx):
        half = idx in (A_HR, A_HL, R_HR, R_HL)
        sent = kv.at[:, pl.ds(0, 1 if half else 2)]
        pltpu.make_async_remote_copy(
            src_ref=sent, dst_ref=sent, send_sem=ssem.at[idx], recv_sem=rsem.at[0, idx],
            device_id=partner, device_id_type=MESH,
        ).wait_send()

    @when(z0)
    def _():
        for idx in (A_Z0, A_ZM, A_ZP):
            done(idx)

    @when(z1)
    def _():
        for idx in (A_HR, A_HL, R_HR, R_HL, R_Z0, R_ZM, R_ZP):
            done(idx)

    @when(jnp.logical_or(z0, x < 3))
    def _():
        done(A_R)

    @when(jnp.logical_or(z0, x == 0))
    def _():
        done(A_L)

    @when(jnp.logical_or(x == 1, jnp.logical_and(z1, x == 2)))
    def _():
        done(A_FR)

    @when(jnp.logical_and(z0, x == 0))
    def _():
        done(A_FL)

    @when(jnp.logical_or(x == 2, jnp.logical_and(z1, x == 3)))
    def _():
        done(R_FR)

    @when(jnp.logical_and(z0, x == 3))
    def _():
        done(R_FL)

    @when(jnp.logical_or(z0, x == 3))
    def _():
        done(R_L)

    @when(jnp.logical_or(z0, x > 0))
    def _():
        done(R_R)

    swap_all(DQ, dqs.at[their_rows], dq_in).wait_send()
    swap_all(OUT, fin.at[1 - k], fin_in).wait_send()
    for idx, sent in ((IN_K, kvt.at[0]), (IN_V, kvt.at[1]), (IN_Q, qct.at[0]), (IN_C, qct.at[1])):
        pltpu.make_async_remote_copy(
            src_ref=sent, dst_ref=sent, send_sem=hsend.at[idx], recv_sem=hout.at[0],
            device_id=partner, device_id_type=MESH,
        ).wait_send()
    for copy in landed:
        copy.wait()
    pltpu.make_async_copy(qg_ref.at[:, half_cols], qg_ref.at[:, half_cols], lout.at[0]).wait()
    pltpu.make_async_copy(kg_ref.at[:, half_cols], kg_ref.at[:, half_cols], lout.at[1]).wait()
    pltpu.make_async_copy(vg_ref.at[:, half_cols], vg_ref.at[:, half_cols], lout.at[2]).wait()

    gate_local.wait()
    gate_remote.wait_send()


def place(a0, a1, a2, a3, b0, b1, b2, b3, m0, m1, m2, m3, sem):
    held = (m0, m1, m2, m3)
    into = [
        pltpu.make_async_copy(a, m, sem.at[0, i]) for i, (a, m) in enumerate(zip((a0, a1, a2, a3), held))
    ]
    out = [
        pltpu.make_async_copy(m, b, sem.at[1, i]) for i, (m, b) in enumerate(zip(held, (b0, b1, b2, b3)))
    ]
    for copy in into:
        copy.start()
    for copy, after in zip(into, out):
        copy.wait()
        after.start()
    for copy in out:
        copy.wait()


def shards(queries, keys, values, cotangent, gate, visible):
    tokens, width = queries.shape
    half = width // 2
    any_spec = pl.BlockSpec(memory_space=pl.ANY)
    hbm_spec = pl.BlockSpec(memory_space=pltpu.HBM)
    dma = pltpu.SemaphoreType.DMA
    out_shape = (
        jax.ShapeDtypeStruct((tokens, width), BF16),
        jax.ShapeDtypeStruct((LAT, width), BF16),
        jax.ShapeDtypeStruct((LAT, width), BF16),
        jax.ShapeDtypeStruct((2, CORE_HEADS, D), F32),
    )
    results = pl.pallas_call(
        kernel,
        out_shape=out_shape,
        in_specs=[hbm_spec] * 6,
        out_specs=(any_spec,) * 4,
        scratch_shapes=[
            pltpu.VMEM((2 * tokens, half), BF16),
            pltpu.VMEM((2 * tokens, half), BF16),
            pltpu.VMEM((CHUNKS, IMAGES, 2, N, LAT, D), BF16),
            pltpu.VMEM((CHUNKS, IMAGES, 2, N, LAT, D), BF16),
            pltpu.VMEM((CHUNKS, 8, 2, 2, N, LAT, D), BF16),
            pltpu.VMEM((IMAGES, 2, LAT, D), BF16),
            pltpu.VMEM((4, VIS + 1, LAT, SPAN), BF16),
            pltpu.VMEM((4, VIS + 1, LAT, SPAN), BF16),
            pltpu.VMEM((2 * tokens, 2 * D), BF16),
            pltpu.VMEM((2 * tokens, half), BF16),
            pltpu.VMEM((2, 2, LAT, half), BF16),
            pltpu.VMEM((CORE_HEADS, D), F32),
            pltpu.VMEM((3, CORE_HEADS, D), F32),
            pltpu.VMEM((4, CORE_HEADS, D), F32),
            pltpu.VMEM((1, 2, N, LAT, D), BF16),
            pltpu.VMEM((2 * CORE_HEADS, D), F32),
            pltpu.VMEM((2, tokens, half), BF16),
            pltpu.VMEM((2, LAT, half), BF16),
            pltpu.VMEM((tokens, half), BF16),
            pltpu.VMEM((2, LAT, half), BF16),
            pltpu.VMEM((CORE_HEADS, D), F32),
            pltpu.SMEM((2, 2, VIS), jnp.int32),
            pltpu.SMEM((4, IMAGES), jnp.int32),
            dma((MESSAGES,)),
            dma((CHUNKS, MESSAGES)),
            dma((6,)),
            dma((CORE_HEADS, 4)),
            dma((2,)),
            dma((CORE_HEADS, 2)),
            dma((3,)),
            dma((2,)),
            dma((4,)),
            dma((4,)),
            dma((3,)),
            dma((3,)),
            dma((4,)),
            dma((3,)),
            dma((3,)),
            dma((3,)),
        ],
        compiler_params=pltpu.CompilerParams(
            collective_id=0, has_side_effects=True, vmem_limit_bytes=63 * 1024 * 1024
        ),
        name="cross_attention_backward",
    )(queries, keys, values, cotangent, gate.reshape(2 * CORE_HEADS, D), visible)
    query_grad, key_grad, value_grad, gate_grad = pl.pallas_call(
        place,
        out_shape=out_shape,
        in_specs=[any_spec] * 4,
        out_specs=(hbm_spec,) * 4,
        scratch_shapes=[pltpu.VMEM(o.shape, o.dtype) for o in out_shape] + [dma((2, 4))],
        compiler_params=pltpu.CompilerParams(vmem_limit_bytes=63 * 1024 * 1024),
        name="place_results",
    )(*results)
    return query_grad, key_grad, value_grad, gate_grad.reshape(width)


def solution(mesh):
    placed = (
        P(("dp", "seq"), "tensor"),
        P(("dp", "seq"), "tensor"),
        P(("dp", "seq"), "tensor"),
        P(("dp", "seq"), "tensor"),
        P("tensor"),
        P(("dp", "seq"), None),
    )
    return jax.shard_map(
        shards,
        mesh=mesh,
        in_specs=placed,
        out_specs=(
            P(("dp", "seq"), "tensor"),
            P(("dp", "seq"), "tensor"),
            P(("dp", "seq"), "tensor"),
            P(("dp", "tensor")),
        ),
        check_vma=False,
    )
```

```python
import functools

import jax
import jax.numpy as jnp
from jax import lax
from jax.experimental import pallas as pl
from jax.experimental.pallas import tpu as pltpu
from jax.sharding import PartitionSpec as P

MESH = pl.DeviceIdType.MESH
D = 128
LAT = 64
SPAN = 128
VIS = 4
CORE_HEADS = 8
N = 1
CHUNKS = CORE_HEADS // N
AHEAD = 6
EARLY = 6
IMAGES = 16
GATHER2, GATHER3, COMPUTE, BACK2, BACK3, LAST = 1, 2, 3, 5, 7, 9
NEG = -1e30
EXP2_SCALE = D**-0.5 * 1.4426950408889634
F32, BF16 = jnp.float32, jnp.bfloat16

(
    A_R, A_L, A_FR, A_FL, A_Z0, A_ZM, A_ZP, A_HR, A_HL,
    R_R, R_L, R_FR, R_FL, R_Z0, R_ZM, R_ZP, R_HR, R_HL,
) = range(18)
MESSAGES = 18
DQ, OUT, IN_K, IN_V, IN_Q, IN_C = range(6)


def dot(a, b, ca, cb):
    return lax.dot_general(a, b, (((ca,), (cb,)), ((), ())), preferred_element_type=F32)


def kernel(
    q_ref, k_ref, v_ref, ct_ref, gate_hbm, vis_ref,
    qg_ref, kg_ref, vg_ref, gg_ref,
    qw, cw, kv, obuf, rbuf, kvw, sg_ref, low_ref, both_ref, q_turned, go_turned, dqs, fin, gpart, gall, gsum, first, gate_ref, qct, kvt, dq_in, fin_in, gate_in, vis_s, slot_s,
    ssem, rsem, hsend, hrecv, hout, lsem, lout, lfirst, lstage, lland, esend, erecv, elocal, gsend, grecv, glast,
):
    seq = lax.axis_index("seq")
    c, k = lax.div(seq, 2), lax.rem(seq, 2)
    z, x = lax.div(c, 4), lax.rem(c, 4)
    xr, xl = lax.rem(x + 1, 4), lax.rem(x + 3, 4)
    xo = lax.rem(x + 2, 4)
    z0, z1 = z == 0, z == 1

    def at_chip(chip):
        return {"seq": chip * 2 + k}

    right_chip, left_chip, across_chip = z * 4 + xr, z * 4 + xl, (1 - z) * 4 + x
    right, left, across = at_chip(right_chip), at_chip(left_chip), at_chip(across_chip)
    partner = {"seq": c * 2 + (1 - k)}

    def send(idx, g, src, dst, dev):
        return pltpu.make_async_remote_copy(
            src_ref=src, dst_ref=dst, send_sem=ssem.at[idx], recv_sem=rsem.at[g, idx],
            device_id=dev, device_id_type=MESH,
        )

    def blk(buf, g, b):
        return buf.at[g, pl.ds(2 * b, 2)]

    def img(buf, g, b, half):
        return buf.at[g, pl.ds(2 * b + half, 1)]

    hi = z * 4

    def message(idx, g):
        own = blk(kv, g, c)
        if idx == A_R:
            return send(idx, g, own, own, right)
        if idx == A_L:
            return send(idx, g, own, own, left)
        if idx == A_FR:
            b = blk(kv, g, hi + xl)
            return send(idx, g, b, b, right)
        if idx == A_FL:
            b = blk(kv, g, hi + xr)
            return send(idx, g, b, b, left)
        if idx == A_Z0:
            return send(idx, g, own, own, across)
        if idx == A_ZM:
            b = blk(kv, g, xl)
            return send(idx, g, b, b, across)
        if idx == A_ZP:
            b = blk(kv, g, xr)
            return send(idx, g, b, b, across)
        if idx == A_HR:
            b = img(kv, g, xl, 0)
            return send(idx, g, b, b, right)
        if idx == A_HL:
            b = img(kv, g, xr, 1)
            return send(idx, g, b, b, left)
        if idx == R_R:
            return send(idx, g, blk(obuf, g, hi + xl), rbuf.at[g, 0], left)
        if idx == R_L:
            return send(idx, g, blk(obuf, g, hi + xr), rbuf.at[g, 1], right)
        if idx == R_FR:
            return send(idx, g, blk(obuf, g, hi + xo), rbuf.at[g, 2], left)
        if idx == R_FL:
            return send(idx, g, blk(obuf, g, hi + xo), rbuf.at[g, 3], right)
        if idx == R_Z0:
            return send(idx, g, blk(obuf, g, x), rbuf.at[g, 4], across)
        if idx == R_ZM:
            return send(idx, g, blk(obuf, g, xl), rbuf.at[g, 5], across)
        if idx == R_ZP:
            return send(idx, g, blk(obuf, g, xr), rbuf.at[g, 6], across)
        if idx == R_HR:
            return send(idx, g, img(obuf, g, xo, 0), rbuf.at[g, 7, pl.ds(0, 1)], left)
        if idx == R_HL:
            return send(idx, g, img(obuf, g, xo, 1), rbuf.at[g, 7, pl.ds(1, 1)], right)
        raise ValueError(idx)

    def swap(idx, h, src, dst):
        return pltpu.make_async_remote_copy(
            src_ref=src, dst_ref=dst, send_sem=hsend.at[idx], recv_sem=hrecv.at[h, idx - IN_K],
            device_id=partner, device_id_type=MESH,
        )

    def swap_all(idx, src, dst):
        return pltpu.make_async_remote_copy(
            src_ref=src, dst_ref=dst, send_sem=hsend.at[idx], recv_sem=hout.at[idx],
            device_id=partner, device_id_type=MESH,
        )

    def head_message(idx, h):
        g, n = h, 0
        theirs = head_cols(0, h)
        if idx == DQ:
            return swap_all(DQ, dqs.at[their_rows, theirs], dq_in.at[:, theirs])
        if idx == OUT:
            return swap_all(OUT, fin.at[1 - k, :, :, theirs], fin_in.at[:, :, theirs])
        if idx == IN_Q:
            return swap(idx, h, qct.at[0, :, theirs], qw.at[my_rows, theirs])
        if idx == IN_C:
            return swap(idx, h, qct.at[1, :, theirs], cw.at[my_rows, theirs])
        return swap(idx, h, kvt.at[idx - IN_K, :, theirs], kv.at[g, seq, idx - IN_K, n])

    def head_got(idx, h, dst):
        swap(idx, h, dst, dst).wait_recv()

    def head_cols(core, h):
        return pl.ds(pl.multiple_of((core * CORE_HEADS + h) * D, D), D)

    def got(idx, g, dst):
        send(idx, g, dst, dst, partner).wait_recv()

    def own_copies(h):
        g, n = h, 0
        mine = head_cols(k, h)
        return (
            pltpu.make_async_copy(k_ref.at[:, mine], kv.at[g, seq, 0, n], lsem.at[h, 0]),
            pltpu.make_async_copy(v_ref.at[:, mine], kv.at[g, seq, 1, n], lsem.at[h, 1]),
        )

    half_width = CORE_HEADS * D
    half_cols = pl.ds(pl.multiple_of(k * half_width, half_width), half_width)
    their_cols = pl.ds(pl.multiple_of((1 - k) * half_width, half_width), half_width)
    my_rows, their_rows = pl.ds(k * 256, 256), pl.ds((1 - k) * 256, 256)

    def result_copies():
        results = ((1, fin.at[k, 0], kg_ref), (2, fin.at[k, 1], vg_ref))
        return [
            pltpu.make_async_copy(src, ref.at[:, half_cols], lout.at[i]) for i, src, ref in results
        ]

    def query_copy():
        return pltpu.make_async_copy(dqs.at[my_rows], qg_ref.at[:, half_cols], lout.at[0])

    def early(i, src, dst):
        return pltpu.make_async_remote_copy(
            src_ref=src, dst_ref=dst, send_sem=esend.at[i], recv_sem=erecv.at[i],
            device_id=partner, device_id_type=MESH,
        )

    swaps = [
        early(0, vis_ref, vis_s.at[k]),
    ]
    theirs_staged = [
        pltpu.make_async_copy(k_ref.at[:, their_cols], kvt.at[0], lstage.at[0]),
        pltpu.make_async_copy(v_ref.at[:, their_cols], kvt.at[1], lstage.at[1]),
        pltpu.make_async_copy(q_ref.at[:, their_cols], qct.at[0], lstage.at[2]),
        pltpu.make_async_copy(ct_ref.at[:, their_cols], qct.at[1], lstage.at[3]),
    ]
    keeps = [
        pltpu.make_async_copy(vis_ref, vis_s.at[k], elocal.at[0]),
        pltpu.make_async_copy(q_ref.at[:, half_cols], qw.at[my_rows], elocal.at[1]),
        pltpu.make_async_copy(ct_ref.at[:, half_cols], cw.at[my_rows], elocal.at[2]),
        pltpu.make_async_copy(gate_hbm, gate_ref, elocal.at[3]),
    ]

    first_cols = head_cols(1 - k, 0)
    first_copies = [
        pltpu.make_async_copy(k_ref.at[:, first_cols], first.at[0, 0, 0], lfirst.at[0]),
        pltpu.make_async_copy(v_ref.at[:, first_cols], first.at[0, 1, 0], lfirst.at[1]),
    ]

    def first_messages(idx, chip):
        mine = kv.at[0, pl.ds(seq, 1)]
        return [
            pltpu.make_async_remote_copy(
                src_ref=src, dst_ref=mine, send_sem=ssem.at[idx], recv_sem=rsem.at[0, idx],
                device_id={"seq": chip * 2 + core}, device_id_type=MESH,
            )
            for src, core in ((mine, k), (first, 1 - k))
        ]

    def send_first():
        for copy in (*own_copies(0), *first_copies):
            copy.wait()

        @pl.when(jnp.logical_or(z0, x < 3))
        def _():
            for copy in first_messages(A_R, right_chip):
                copy.start()

        @pl.when(jnp.logical_or(z0, x == 0))
        def _():
            for copy in first_messages(A_L, left_chip):
                copy.start()

        @pl.when(z0)
        def _():
            for copy in first_messages(A_Z0, across_chip):
                copy.start()

    for copy in first_copies:
        copy.start()
    for h in range(AHEAD):
        for copy in own_copies(h):
            copy.start()

    for copy in theirs_staged + keeps:
        copy.start()

    barrier = pltpu.get_barrier_semaphore()
    greeted = [{"seq": chip * 2 + m} for chip in (right_chip, left_chip, across_chip) for m in (0, 1)]
    for device in greeted + [partner]:
        pl.semaphore_signal(barrier, inc=1, device_id=device, device_id_type=MESH)
    pl.semaphore_wait(barrier, 7)

    send_first()

    for copy in theirs_staged:
        copy.wait()
    for h in range(AHEAD):
        for idx in (IN_K, IN_V, IN_Q, IN_C):
            head_message(idx, h).start()

    for copy in swaps:
        copy.start()

    sg_ref[:, VIS] = jnp.zeros((4, LAT, SPAN), BF16)
    low_ref[:, VIS] = jnp.zeros((4, LAT, SPAN), BF16)

    def prepare():
        for copy in keeps:
            copy.wait()
        for copy in swaps:
            copy.wait()

        @pl.loop(0, IMAGES)
        def _(i):
            for s in range(4):
                slot = jnp.int32(VIS)
                for v in range(VIS):
                    slot = jnp.where(vis_s[s // 2, s % 2, v] == i, v, slot)
                slot_s[s, i] = slot

    def when(cond):
        return pl.when(cond)

    def text_work(h):
        swapped_queries(h)
        cols = pl.ds(h * D if isinstance(h, int) else pl.multiple_of(h * D, D), D)
        tanh_gate = jnp.tanh(gate_ref[pl.ds(k * CORE_HEADS + h, 1), :])
        ct_all = cw[:, cols]
        go_all = (tanh_gate * ct_all.astype(F32)).astype(BF16)
        both_ref[h, :, :D] = go_all
        both_ref[h, :, D:] = ct_all
        for s in range(4):
            rows = pl.ds(s * SPAN, SPAN)
            q_turned[h, s] = qw[rows, cols].T
            go_turned[h, s] = go_all[s * SPAN : (s + 1) * SPAN].T

    def span_work(h):
        cols = pl.ds(pl.multiple_of(h * D, D), D)
        kvw[...] = kv[h, :, :, 0]
        spans = range(4)
        listed = [[vis_s[s // 2, s % 2, v] for v in range(VIS)] for s in spans]
        ids = [[jnp.maximum(i, 0) for i in row] for row in listed]
        kl = [jnp.concatenate([kvw[i, 0] for i in ids[s]], axis=0) for s in spans]
        vl = [jnp.concatenate([kvw[i, 1] for i in ids[s]], axis=0) for s in spans]
        raw = [dot(kl[s], q_turned[h, s], 1, 0) for s in spans]
        wg = [dot(vl[s], go_turned[h, s], 1, 0) for s in spans]
        p, low, sg = [], [], []
        for s in spans:
            rows = [raw[s][:LAT] * EXP2_SCALE]
            for v in range(1, VIS):
                bias = jnp.where(listed[s][v] >= 0, 0.0, NEG).astype(F32)
                rows.append(raw[s][v * LAT : (v + 1) * LAT] * EXP2_SCALE + bias)
            sc = jnp.concatenate(rows, axis=0)
            e = jnp.exp2(sc - jnp.max(sc, axis=0, keepdims=True))
            p.append(e * (1.0 / jnp.sum(e, axis=0, keepdims=True)))
            low.append(p[s].astype(BF16))
        for s in spans:
            dots = jnp.sum(low[s].astype(F32) * wg[s], axis=0, keepdims=True)
            sg.append((p[s] * (wg[s] - dots)).astype(BF16))
        for s in spans:
            low_ref[s, pl.ds(0, VIS)] = low[s].reshape(VIS, LAT, SPAN)
            sg_ref[s, pl.ds(0, VIS)] = sg[s].reshape(VIS, LAT, SPAN)
        dq = [dot(sg[s], kl[s], 0, 0) * (D**-0.5) for s in spans]
        for s in spans:
            dqs[pl.ds(s * SPAN, SPAN), cols] = dq[s].astype(BF16)

    def products(g):
        tanh_gate = jnp.tanh(gate_ref[pl.ds(k * CORE_HEADS + g, 1), :])
        q_all = qw[:, pl.ds(pl.multiple_of(g * D, D), D)]
        both = both_ref[g]

        def images(count):
            left, low_left, vals = [], [], []
            for i in range(count):
                slots = [slot_s[s, i] for s in range(4)]
                left.append(jnp.concatenate([sg_ref[s, slots[s]] for s in range(4)], axis=1))
                low_left.append(jnp.concatenate([low_ref[s, slots[s]] for s in range(4)], axis=1))
                vals.append(jnp.where(i < 2 * (c + 1), kvw[i, 1].astype(F32), 0.0))
            dk = dot(jnp.concatenate(left, axis=0), q_all, 1, 0) * (D**-0.5)
            obuf[g, pl.ds(0, count), 0, 0] = dk.reshape(count, LAT, D).astype(BF16)
            vw = dot(jnp.concatenate(low_left, axis=0), both, 1, 0)
            obuf[g, pl.ds(0, count), 1, 0] = vw[:, :D].reshape(count, LAT, D).astype(BF16)
            vals = jnp.concatenate(vals, axis=0)
            gate_sum = jnp.sum(vals * vw[:, D:], axis=0, keepdims=True)
            gpart[pl.ds(g, 1), :] = gate_sum * (1.0 - tanh_gate * tanh_gate)

        @when(z0)
        def _():
            images(8)

        @when(z1)
        def _():
            images(16)

    def add(g, b, slot):
        rows = pl.ds(2 * b, 2)
        obuf[g, rows] = (obuf[g, rows].astype(F32) + rbuf[g, slot].astype(F32)).astype(BF16)

    def swapped(g):
        other = c * 2 + (1 - k)
        head_got(IN_K, g, kv.at[g, other, 0, 0])
        head_got(IN_V, g, kv.at[g, other, 1, 0])

    def swapped_queries(g):
        theirs = head_cols(0, g)
        head_got(IN_Q, g, qw.at[their_rows, theirs])
        head_got(IN_C, g, cw.at[their_rows, theirs])

    def gather1(g):
        for copy in own_copies(g):
            copy.wait()
        swapped(g)

        @when(jnp.logical_or(z0, x < 3))
        def _():
            message(A_R, g).start()

        @when(jnp.logical_or(z0, x == 0))
        def _():
            message(A_L, g).start()

    def gather2(g):
        @when(jnp.logical_or(z0, x > 0))
        def _():
            got(A_R, g, blk(kv, g, hi + xl))

        @when(z0)
        def _():
            message(A_ZM, g).start()
            got(A_L, g, blk(kv, g, hi + xr))
            message(A_ZP, g).start()

    def gather_own(g):
        @when(z0)
        def _():
            message(A_Z0, g).start()

    def gather_forward(g):
        @when(jnp.logical_or(x == 1, jnp.logical_and(z1, x == 2)))
        def _():
            message(A_FR, g).start()

        @when(jnp.logical_and(z0, x == 0))
        def _():
            message(A_FL, g).start()

    def gather3(g):
        @when(z1)
        def _():
            got(A_ZM, g, blk(kv, g, xl))
            message(A_HR, g).start()
            got(A_ZP, g, blk(kv, g, xr))
            message(A_HL, g).start()

    def gather4(g):
        @when(z1)
        def _():
            got(A_Z0, g, blk(kv, g, x))
            got(A_HR, g, img(kv, g, xo, 0))
            got(A_HL, g, img(kv, g, xo, 1))

        @when(jnp.logical_or(x == 2, jnp.logical_and(z1, x == 3)))
        def _():
            got(A_FR, g, blk(kv, g, hi + xo))

        @when(jnp.logical_and(z0, x == 3))
        def _():
            got(A_FL, g, blk(kv, g, xo))

        @when(jnp.logical_and(z1, x == 3))
        def _():
            got(A_L, g, blk(kv, g, 4))

    def back1(g):
        @when(z1)
        def _():
            message(R_HR, g).start()
            message(R_HL, g).start()
            message(R_Z0, g).start()

        @when(jnp.logical_or(x == 2, jnp.logical_and(z1, x == 3)))
        def _():
            message(R_FR, g).start()

        @when(jnp.logical_and(z0, x == 3))
        def _():
            message(R_FL, g).start()

        @when(jnp.logical_and(z1, x == 3))
        def _():
            message(R_L, g).start()

    def back2(g):
        @when(z1)
        def _():
            got(R_HR, g, rbuf.at[g, 7, pl.ds(0, 1)])
            row = 2 * xl
            obuf[g, row] = (obuf[g, row].astype(F32) + rbuf[g, 7, 0].astype(F32)).astype(BF16)
            message(R_ZM, g).start()
            got(R_HL, g, rbuf.at[g, 7, pl.ds(1, 1)])
            row = 2 * xr + 1
            obuf[g, row] = (obuf[g, row].astype(F32) + rbuf[g, 7, 1].astype(F32)).astype(BF16)
            message(R_ZP, g).start()

            @when(jnp.logical_or(x == 1, x == 2))
            def _():
                got(R_FR, g, rbuf.at[g, 2])
                add(g, 4 + xl, 2)

            @when(x > 0)
            def _():
                message(R_R, g).start()

    def back3(g):
        @when(z0)
        def _():
            @when(x == 1)
            def _():
                got(R_FR, g, rbuf.at[g, 2])
                add(g, xl, 2)

            @when(x == 0)
            def _():
                got(R_FL, g, rbuf.at[g, 3])
                add(g, xr, 3)

            got(R_ZM, g, rbuf.at[g, 5])
            add(g, xl, 5)
            message(R_R, g).start()
            got(R_ZP, g, rbuf.at[g, 6])
            add(g, xr, 6)
            message(R_L, g).start()

    def back4(g):
        own = pl.ds(2 * c, 2)

        def finish(slots):
            total = obuf[g, own].astype(F32)
            for slot in slots:
                total += rbuf[g, slot].astype(F32)
            fin[:, :, :, pl.ds(pl.multiple_of(g * D, D), D)] = total[:, :, 0].astype(BF16)

        @when(z0)
        def _():
            got(R_Z0, g, rbuf.at[g, 4])
            got(R_R, g, rbuf.at[g, 0])
            got(R_L, g, rbuf.at[g, 1])
            finish((4, 0, 1))

        @when(z1)
        def _():
            @when(x < 3)
            def _():
                got(R_R, g, rbuf.at[g, 0])

            @when(x == 0)
            def _():
                got(R_L, g, rbuf.at[g, 1])
                finish((0, 1))

            @when(jnp.logical_or(x == 1, x == 2))
            def _():
                finish((0,))

            @when(x == 3)
            def _():
                finish(())

        head_message(OUT, g).start()

    odd = lax.rem(x, 2)
    pairs = (
        across,
        at_chip(z * 4 + x + 1 - 2 * odd),
        at_chip(z * 4 + lax.rem(x + 3 + 2 * odd, 4)),
    )

    def gate_step(i):
        return pltpu.make_async_remote_copy(
            src_ref=gsum.at[i], dst_ref=gall.at[i], send_sem=gsend.at[i], recv_sem=grecv.at[i],
            device_id=pairs[i], device_id_type=MESH,
        )

    gate_local = pltpu.make_async_copy(gsum.at[3], gg_ref.at[k], glast.at[0])
    gate_remote = pltpu.make_async_remote_copy(
        src_ref=gsum.at[3], dst_ref=gate_in, send_sem=glast.at[1], recv_sem=glast.at[2],
        device_id=partner, device_id_type=MESH,
    )
    landed = [
        pltpu.make_async_copy(dq_in, qg_ref.at[:, their_cols], lland.at[0]),
        pltpu.make_async_copy(fin_in.at[0], kg_ref.at[:, their_cols], lland.at[1]),
        pltpu.make_async_copy(fin_in.at[1], vg_ref.at[:, their_cols], lland.at[2]),
        pltpu.make_async_copy(gate_in, gg_ref.at[1 - k], lland.at[3]),
    ]

    def iteration(t):
        fixed = isinstance(t, int)

        def stage(offset, run, first=0):
            if fixed:
                if offset + first <= t < CHUNKS + offset:
                    run(t - offset)
                return
            conditions = []
            if offset + first > COMPUTE:
                conditions.append(t >= offset + first)
            if offset < COMPUTE:
                conditions.append(t < CHUNKS + offset)
            if not conditions:
                run(t - offset)
            else:
                pl.when(functools.reduce(jnp.logical_and, conditions))(lambda: run(t - offset))

        def fetch(g):
            for copy in own_copies(g):
                copy.start()
            for idx in (IN_K, IN_V, IN_Q, IN_C):
                head_message(idx, g).start()

        stage(-AHEAD, lambda g: fetch(g))
        stage(0, gather1, 1)
        stage(GATHER2, gather2)
        stage(0, gather_own, 1)
        stage(GATHER2, gather_forward)
        stage(BACK2, back2)
        stage(BACK3, back3)
        stage(LAST, back4)
        if not fixed:
            pl.when(t - COMPUTE < CHUNKS - EARLY)(lambda: text_work(t - COMPUTE + EARLY))
            gather4(t - COMPUTE)
            span_work(t - COMPUTE)
        stage(GATHER3, gather3)
        if not fixed:
            head_message(DQ, t - COMPUTE).start()
            products(t - COMPUTE)
            back1(t - COMPUTE)

    iteration(0)
    prepare()
    text_work(0)
    iteration(1)
    for h in range(1, EARLY - 2):
        text_work(h)
    iteration(2)
    for h in range(EARLY - 2, EARLY):
        text_work(h)
    swapped(0)

    @pl.loop(COMPUTE, COMPUTE + CHUNKS)
    def _(t):
        iteration(t)

    query_copy().start()
    gsum[0] = gpart[...]
    gate_step(0).start()
    for i in range(LAST - COMPUTE):
        iteration(COMPUTE + CHUNKS + i)
        if i < 3:
            gate_step(i).wait_recv()
            gsum[i + 1] = gsum[i] + gall[i]
            if i < 2:
                gate_step(i + 1).start()
            else:
                gate_local.start()
                gate_remote.start()

    for copy in result_copies():
        copy.start()
    swap_all(DQ, dqs.at[their_rows], dq_in).wait_recv()
    landed[0].start()
    gate_remote.wait_recv()
    landed[3].start()
    swap_all(OUT, fin.at[1 - k], fin_in).wait_recv()
    landed[1].start()
    landed[2].start()

    for i in range(3):
        gate_step(i).wait_send()

    def done(idx):
        half = idx in (A_HR, A_HL, R_HR, R_HL)
        sent = kv.at[:, pl.ds(0, 1 if half else 2)]
        pltpu.make_async_remote_copy(
            src_ref=sent, dst_ref=sent, send_sem=ssem.at[idx], recv_sem=rsem.at[0, idx],
            device_id=partner, device_id_type=MESH,
        ).wait_send()

    @when(z0)
    def _():
        for idx in (A_Z0, A_ZM, A_ZP):
            done(idx)

    @when(z1)
    def _():
        for idx in (A_HR, A_HL, R_HR, R_HL, R_Z0, R_ZM, R_ZP):
            done(idx)

    @when(jnp.logical_or(z0, x < 3))
    def _():
        done(A_R)

    @when(jnp.logical_or(z0, x == 0))
    def _():
        done(A_L)

    @when(jnp.logical_or(x == 1, jnp.logical_and(z1, x == 2)))
    def _():
        done(A_FR)

    @when(jnp.logical_and(z0, x == 0))
    def _():
        done(A_FL)

    @when(jnp.logical_or(x == 2, jnp.logical_and(z1, x == 3)))
    def _():
        done(R_FR)

    @when(jnp.logical_and(z0, x == 3))
    def _():
        done(R_FL)

    @when(jnp.logical_or(z0, x == 3))
    def _():
        done(R_L)

    @when(jnp.logical_or(z0, x > 0))
    def _():
        done(R_R)

    swap_all(DQ, dqs.at[their_rows], dq_in).wait_send()
    swap_all(OUT, fin.at[1 - k], fin_in).wait_send()
    for idx, sent in ((IN_K, kvt.at[0]), (IN_V, kvt.at[1]), (IN_Q, qct.at[0]), (IN_C, qct.at[1])):
        pltpu.make_async_remote_copy(
            src_ref=sent, dst_ref=sent, send_sem=hsend.at[idx], recv_sem=hout.at[0],
            device_id=partner, device_id_type=MESH,
        ).wait_send()
    for copy in landed:
        copy.wait()
    pltpu.make_async_copy(qg_ref.at[:, half_cols], qg_ref.at[:, half_cols], lout.at[0]).wait()
    pltpu.make_async_copy(kg_ref.at[:, half_cols], kg_ref.at[:, half_cols], lout.at[1]).wait()
    pltpu.make_async_copy(vg_ref.at[:, half_cols], vg_ref.at[:, half_cols], lout.at[2]).wait()

    gate_local.wait()
    gate_remote.wait_send()


def place(a0, a1, a2, a3, b0, b1, b2, b3, m0, m1, m2, m3, sem):
    held = (m0, m1, m2, m3)
    into = [
        pltpu.make_async_copy(a, m, sem.at[0, i]) for i, (a, m) in enumerate(zip((a0, a1, a2, a3), held))
    ]
    out = [
        pltpu.make_async_copy(m, b, sem.at[1, i]) for i, (m, b) in enumerate(zip(held, (b0, b1, b2, b3)))
    ]
    for copy in into:
        copy.start()
    for copy, after in zip(into, out):
        copy.wait()
        after.start()
    for copy in out:
        copy.wait()


def shards(queries, keys, values, cotangent, gate, visible):
    tokens, width = queries.shape
    half = width // 2
    any_spec = pl.BlockSpec(memory_space=pl.ANY)
    hbm_spec = pl.BlockSpec(memory_space=pltpu.HBM)
    dma = pltpu.SemaphoreType.DMA
    out_shape = (
        jax.ShapeDtypeStruct((tokens, width), BF16),
        jax.ShapeDtypeStruct((LAT, width), BF16),
        jax.ShapeDtypeStruct((LAT, width), BF16),
        jax.ShapeDtypeStruct((2, CORE_HEADS, D), F32),
    )
    results = pl.pallas_call(
        kernel,
        out_shape=out_shape,
        in_specs=[hbm_spec] * 6,
        out_specs=(any_spec,) * 4,
        scratch_shapes=[
            pltpu.VMEM((2 * tokens, half), BF16),
            pltpu.VMEM((2 * tokens, half), BF16),
            pltpu.VMEM((CHUNKS, IMAGES, 2, N, LAT, D), BF16),
            pltpu.VMEM((CHUNKS, IMAGES, 2, N, LAT, D), BF16),
            pltpu.VMEM((CHUNKS, 8, 2, 2, N, LAT, D), BF16),
            pltpu.VMEM((IMAGES, 2, LAT, D), BF16),
            pltpu.VMEM((4, VIS + 1, LAT, SPAN), BF16),
            pltpu.VMEM((4, VIS + 1, LAT, SPAN), BF16),
            pltpu.VMEM((CORE_HEADS, 2 * tokens, 2 * D), BF16),
            pltpu.VMEM((CORE_HEADS, 4, D, SPAN), BF16),
            pltpu.VMEM((CORE_HEADS, 4, D, SPAN), BF16),
            pltpu.VMEM((2 * tokens, half), BF16),
            pltpu.VMEM((2, 2, LAT, half), BF16),
            pltpu.VMEM((CORE_HEADS, D), F32),
            pltpu.VMEM((3, CORE_HEADS, D), F32),
            pltpu.VMEM((4, CORE_HEADS, D), F32),
            pltpu.VMEM((1, 2, N, LAT, D), BF16),
            pltpu.VMEM((2 * CORE_HEADS, D), F32),
            pltpu.VMEM((2, tokens, half), BF16),
            pltpu.VMEM((2, LAT, half), BF16),
            pltpu.VMEM((tokens, half), BF16),
            pltpu.VMEM((2, LAT, half), BF16),
            pltpu.VMEM((CORE_HEADS, D), F32),
            pltpu.SMEM((2, 2, VIS), jnp.int32),
            pltpu.SMEM((4, IMAGES), jnp.int32),
            dma((MESSAGES,)),
            dma((CHUNKS, MESSAGES)),
            dma((6,)),
            dma((CORE_HEADS, 4)),
            dma((2,)),
            dma((CORE_HEADS, 2)),
            dma((3,)),
            dma((2,)),
            dma((4,)),
            dma((4,)),
            dma((3,)),
            dma((3,)),
            dma((4,)),
            dma((3,)),
            dma((3,)),
            dma((3,)),
        ],
        compiler_params=pltpu.CompilerParams(
            collective_id=0, has_side_effects=True, vmem_limit_bytes=63 * 1024 * 1024
        ),
        name="cross_attention_backward",
    )(queries, keys, values, cotangent, gate.reshape(2 * CORE_HEADS, D), visible)
    query_grad, key_grad, value_grad, gate_grad = pl.pallas_call(
        place,
        out_shape=out_shape,
        in_specs=[any_spec] * 4,
        out_specs=(hbm_spec,) * 4,
        scratch_shapes=[pltpu.VMEM(o.shape, o.dtype) for o in out_shape] + [dma((2, 4))],
        compiler_params=pltpu.CompilerParams(vmem_limit_bytes=63 * 1024 * 1024),
        name="place_results",
    )(*results)
    return query_grad, key_grad, value_grad, gate_grad.reshape(width)


def solution(mesh):
    placed = (
        P(("dp", "seq"), "tensor"),
        P(("dp", "seq"), "tensor"),
        P(("dp", "seq"), "tensor"),
        P(("dp", "seq"), "tensor"),
        P("tensor"),
        P(("dp", "seq"), None),
    )
    return jax.shard_map(
        shards,
        mesh=mesh,
        in_specs=placed,
        out_specs=(
            P(("dp", "seq"), "tensor"),
            P(("dp", "seq"), "tensor"),
            P(("dp", "seq"), "tensor"),
            P(("dp", "tensor")),
        ),
        check_vma=False,
    )
```

```python
import functools

import jax
import jax.numpy as jnp
from jax import lax
from jax.experimental import pallas as pl
from jax.experimental.pallas import tpu as pltpu
from jax.sharding import PartitionSpec as P

MESH = pl.DeviceIdType.MESH
D = 128
LAT = 64
SPAN = 128
VIS = 4
CORE_HEADS = 8
N = 1
CHUNKS = CORE_HEADS // N
AHEAD = 2
IMAGES = 16
GATHER2, GATHER3, COMPUTE, BACK2, BACK3, LAST = 1, 2, 3, 5, 7, 9
NEG = -1e30
EXP2_SCALE = D**-0.5 * 1.4426950408889634
F32, BF16 = jnp.float32, jnp.bfloat16

(
    A_R, A_L, A_FR, A_FL, A_Z0, A_ZM, A_ZP, A_HR, A_HL,
    R_R, R_L, R_L2, R_FR, R_Z0, R_ZM, R_ZP, R_HR, R_HL, R_HO,
) = range(19)
MESSAGES = 19
HALVES = (A_HR, A_HL, R_L, R_L2, R_ZP, R_HR, R_HL, R_HO)
DQ, OUT, IN_K, IN_V, IN_Q, IN_C = range(6)


def dot(a, b, ca, cb):
    return lax.dot_general(a, b, (((ca,), (cb,)), ((), ())), preferred_element_type=F32)


def kernel(
    q_ref, k_ref, v_ref, ct_ref, gate_hbm, vis_ref,
    qg_ref, kg_ref, vg_ref, gg_ref,
    qw, cw, kv, obuf, rbuf, kvw, sg_ref, low_ref, both_ref, dqs, fin, gpart, gall, gsum, first, gate_ref, qct, kvt, dq_in, fin_in, gate_in, vis_s, slot_s,
    ssem, rsem, hsend, hrecv, hout, lsem, lout, lfirst, lstage, lland, esend, erecv, elocal, gsend, grecv, glast,
):
    seq = lax.axis_index("seq")
    c, k = lax.div(seq, 2), lax.rem(seq, 2)
    z, x = lax.div(c, 4), lax.rem(c, 4)
    xr, xl = lax.rem(x + 1, 4), lax.rem(x + 3, 4)
    xo = lax.rem(x + 2, 4)
    z0, z1 = z == 0, z == 1

    def at_chip(chip):
        return {"seq": chip * 2 + k}

    right_chip, left_chip, across_chip = z * 4 + xr, z * 4 + xl, (1 - z) * 4 + x
    right, left, across = at_chip(right_chip), at_chip(left_chip), at_chip(across_chip)
    partner = {"seq": c * 2 + (1 - k)}

    def send(idx, g, src, dst, dev):
        return pltpu.make_async_remote_copy(
            src_ref=src, dst_ref=dst, send_sem=ssem.at[idx], recv_sem=rsem.at[g, idx],
            device_id=dev, device_id_type=MESH,
        )

    def blk(buf, g, b):
        return buf.at[g, pl.ds(2 * b, 2)]

    def img(buf, g, b, half):
        return buf.at[g, pl.ds(2 * b + half, 1)]

    def rhalf(g, slot, half):
        return rbuf.at[g, slot, pl.ds(half, 1)]

    hi = z * 4

    def message(idx, g):
        own = blk(kv, g, c)
        if idx == A_R:
            return send(idx, g, own, own, right)
        if idx == A_L:
            return send(idx, g, own, own, left)
        if idx == A_FR:
            b = blk(kv, g, hi + xl)
            return send(idx, g, b, b, right)
        if idx == A_FL:
            b = blk(kv, g, hi + xr)
            return send(idx, g, b, b, left)
        if idx == A_Z0:
            return send(idx, g, own, own, across)
        if idx == A_ZM:
            b = blk(kv, g, xl)
            return send(idx, g, b, b, across)
        if idx == A_ZP:
            b = blk(kv, g, xr)
            return send(idx, g, b, b, across)
        if idx == A_HR:
            b = img(kv, g, xl, 0)
            return send(idx, g, b, b, right)
        if idx == A_HL:
            b = img(kv, g, xr, 1)
            return send(idx, g, b, b, left)
        if idx == R_R:
            return send(idx, g, blk(obuf, g, hi + xl), rbuf.at[g, 0], left)
        if idx == R_L:
            return send(idx, g, img(obuf, g, hi + xr, 0), rhalf(g, 1, 0), right)
        if idx == R_L2:
            return send(idx, g, img(obuf, g, hi + xr, 1), rhalf(g, 1, 1), right)
        if idx == R_FR:
            return send(idx, g, blk(obuf, g, hi + xo), rbuf.at[g, 2], left)
        if idx == R_Z0:
            return send(idx, g, blk(obuf, g, x), rbuf.at[g, 4], across)
        if idx == R_ZM:
            return send(idx, g, blk(obuf, g, xl), rbuf.at[g, 5], across)
        if idx == R_ZP:
            return send(idx, g, img(obuf, g, xr, 0), rhalf(g, 6, 0), across)
        if idx == R_HR:
            return send(idx, g, img(obuf, g, xo, 1), rhalf(g, 3, 1), left)
        if idx == R_HL:
            return send(idx, g, img(obuf, g, xo, 0), rhalf(g, 3, 0), right)
        if idx == R_HO:
            return send(idx, g, img(obuf, g, xr, 1), rhalf(g, 6, 1), right)
        raise ValueError(idx)

    def swap(idx, h, src, dst):
        return pltpu.make_async_remote_copy(
            src_ref=src, dst_ref=dst, send_sem=hsend.at[idx], recv_sem=hrecv.at[h, idx - IN_K],
            device_id=partner, device_id_type=MESH,
        )

    def swap_all(idx, src, dst):
        return pltpu.make_async_remote_copy(
            src_ref=src, dst_ref=dst, send_sem=hsend.at[idx], recv_sem=hout.at[idx],
            device_id=partner, device_id_type=MESH,
        )

    def head_message(idx, h):
        g, n = h, 0
        theirs = head_cols(0, h)
        if idx == DQ:
            return swap_all(DQ, dqs.at[their_rows, theirs], dq_in.at[:, theirs])
        if idx == OUT:
            return swap_all(OUT, fin.at[1 - k, :, :, theirs], fin_in.at[:, :, theirs])
        if idx == IN_Q:
            return swap(idx, h, qct.at[0, :, theirs], qw.at[my_rows, theirs])
        if idx == IN_C:
            return swap(idx, h, qct.at[1, :, theirs], cw.at[my_rows, theirs])
        return swap(idx, h, kvt.at[idx - IN_K, :, theirs], kv.at[g, seq, idx - IN_K, n])

    def head_got(idx, h, dst):
        swap(idx, h, dst, dst).wait_recv()

    def head_cols(core, h):
        return pl.ds(pl.multiple_of((core * CORE_HEADS + h) * D, D), D)

    def got(idx, g, dst):
        send(idx, g, dst, dst, partner).wait_recv()

    def own_copies(h):
        g, n = h, 0
        mine = head_cols(k, h)
        return (
            pltpu.make_async_copy(k_ref.at[:, mine], kv.at[g, seq, 0, n], lsem.at[h, 0]),
            pltpu.make_async_copy(v_ref.at[:, mine], kv.at[g, seq, 1, n], lsem.at[h, 1]),
        )

    half_width = CORE_HEADS * D
    half_cols = pl.ds(pl.multiple_of(k * half_width, half_width), half_width)
    their_cols = pl.ds(pl.multiple_of((1 - k) * half_width, half_width), half_width)
    my_rows, their_rows = pl.ds(k * 256, 256), pl.ds((1 - k) * 256, 256)

    def result_copies():
        results = ((1, fin.at[k, 0], kg_ref), (2, fin.at[k, 1], vg_ref))
        return [
            pltpu.make_async_copy(src, ref.at[:, half_cols], lout.at[i]) for i, src, ref in results
        ]

    def query_copy():
        return pltpu.make_async_copy(dqs.at[my_rows], qg_ref.at[:, half_cols], lout.at[0])

    def early(i, src, dst):
        return pltpu.make_async_remote_copy(
            src_ref=src, dst_ref=dst, send_sem=esend.at[i], recv_sem=erecv.at[i],
            device_id=partner, device_id_type=MESH,
        )

    swaps = [
        early(0, vis_ref, vis_s.at[k]),
    ]
    theirs_staged = [
        pltpu.make_async_copy(k_ref.at[:, their_cols], kvt.at[0], lstage.at[0]),
        pltpu.make_async_copy(v_ref.at[:, their_cols], kvt.at[1], lstage.at[1]),
        pltpu.make_async_copy(q_ref.at[:, their_cols], qct.at[0], lstage.at[2]),
        pltpu.make_async_copy(ct_ref.at[:, their_cols], qct.at[1], lstage.at[3]),
    ]
    keeps = [
        pltpu.make_async_copy(vis_ref, vis_s.at[k], elocal.at[0]),
        pltpu.make_async_copy(q_ref.at[:, half_cols], qw.at[my_rows], elocal.at[1]),
        pltpu.make_async_copy(ct_ref.at[:, half_cols], cw.at[my_rows], elocal.at[2]),
        pltpu.make_async_copy(gate_hbm, gate_ref, elocal.at[3]),
    ]

    first_cols = head_cols(1 - k, 0)
    first_copies = [
        pltpu.make_async_copy(k_ref.at[:, first_cols], first.at[0, 0, 0], lfirst.at[0]),
        pltpu.make_async_copy(v_ref.at[:, first_cols], first.at[0, 1, 0], lfirst.at[1]),
    ]

    def first_messages(idx, chip):
        mine = kv.at[0, pl.ds(seq, 1)]
        return [
            pltpu.make_async_remote_copy(
                src_ref=src, dst_ref=mine, send_sem=ssem.at[idx], recv_sem=rsem.at[0, idx],
                device_id={"seq": chip * 2 + core}, device_id_type=MESH,
            )
            for src, core in ((mine, k), (first, 1 - k))
        ]

    def send_first():
        for copy in (*own_copies(0), *first_copies):
            copy.wait()

        @pl.when(jnp.logical_or(z0, x < 3))
        def _():
            for copy in first_messages(A_R, right_chip):
                copy.start()

        @pl.when(jnp.logical_or(z0, x == 0))
        def _():
            for copy in first_messages(A_L, left_chip):
                copy.start()

        @pl.when(z0)
        def _():
            for copy in first_messages(A_Z0, across_chip):
                copy.start()

    for copy in first_copies:
        copy.start()
    for h in range(AHEAD):
        for copy in own_copies(h):
            copy.start()

    for copy in theirs_staged + keeps:
        copy.start()

    barrier = pltpu.get_barrier_semaphore()
    greeted = [{"seq": chip * 2 + m} for chip in (right_chip, left_chip, across_chip) for m in (0, 1)]
    for device in greeted + [partner]:
        pl.semaphore_signal(barrier, inc=1, device_id=device, device_id_type=MESH)
    pl.semaphore_wait(barrier, 7)

    send_first()

    for copy in theirs_staged:
        copy.wait()
    for h in range(AHEAD):
        for idx in (IN_K, IN_V, IN_Q, IN_C):
            head_message(idx, h).start()

    for copy in swaps:
        copy.start()

    sg_ref[:, VIS] = jnp.zeros((4, LAT, SPAN), BF16)
    low_ref[:, VIS] = jnp.zeros((4, LAT, SPAN), BF16)

    def prepare():
        for copy in keeps:
            copy.wait()
        for copy in swaps:
            copy.wait()

        @pl.loop(0, IMAGES)
        def _(i):
            for s in range(4):
                slot = jnp.int32(VIS)
                for v in range(VIS):
                    slot = jnp.where(vis_s[s // 2, s % 2, v] == i, v, slot)
                slot_s[s, i] = slot

    def when(cond):
        return pl.when(cond)

    def span_work(h):
        cols = pl.ds(pl.multiple_of(h * D, D), D)
        kvw[...] = kv[h, :, :, 0]
        tanh_gate = jnp.tanh(gate_ref[pl.ds(k * CORE_HEADS + h, 1), :])
        q_all = qw[:, cols]
        ct_all = cw[:, cols]
        go_all = (tanh_gate * ct_all.astype(F32)).astype(BF16)
        both_ref[:, :D] = go_all
        both_ref[:, D:] = ct_all
        spans = range(4)
        listed = [[vis_s[s // 2, s % 2, v] for v in range(VIS)] for s in spans]
        ids = [[jnp.maximum(i, 0) for i in row] for row in listed]
        q = [q_all[s * SPAN : (s + 1) * SPAN] for s in spans]
        go = [go_all[s * SPAN : (s + 1) * SPAN] for s in spans]
        kl = [jnp.concatenate([kvw[i, 0] for i in ids[s]], axis=0) for s in spans]
        vl = [jnp.concatenate([kvw[i, 1] for i in ids[s]], axis=0) for s in spans]
        raw = [dot(kl[s], q[s], 1, 1) for s in spans]
        wg = [dot(vl[s], go[s], 1, 1) for s in spans]
        p, low, sg = [], [], []
        for s in spans:
            rows = [raw[s][:LAT] * EXP2_SCALE]
            for v in range(1, VIS):
                bias = jnp.where(listed[s][v] >= 0, 0.0, NEG).astype(F32)
                rows.append(raw[s][v * LAT : (v + 1) * LAT] * EXP2_SCALE + bias)
            sc = jnp.concatenate(rows, axis=0)
            e = jnp.exp2(sc - jnp.max(sc, axis=0, keepdims=True))
            p.append(e * (1.0 / jnp.sum(e, axis=0, keepdims=True)))
            low.append(p[s].astype(BF16))
        for s in spans:
            dots = jnp.sum(low[s].astype(F32) * wg[s], axis=0, keepdims=True)
            sg.append((p[s] * (wg[s] - dots)).astype(BF16))
        for s in spans:
            low_ref[s, pl.ds(0, VIS)] = low[s].reshape(VIS, LAT, SPAN)
            sg_ref[s, pl.ds(0, VIS)] = sg[s].reshape(VIS, LAT, SPAN)
        dq = [dot(sg[s], kl[s], 0, 0) * (D**-0.5) for s in spans]
        for s in spans:
            dqs[pl.ds(s * SPAN, SPAN), cols] = dq[s].astype(BF16)

    def products(g):
        tanh_gate = jnp.tanh(gate_ref[pl.ds(k * CORE_HEADS + g, 1), :])
        q_all = qw[:, pl.ds(pl.multiple_of(g * D, D), D)]
        both = both_ref[...]

        def images(count):
            left, low_left, vals = [], [], []
            for i in range(count):
                slots = [slot_s[s, i] for s in range(4)]
                left.append(jnp.concatenate([sg_ref[s, slots[s]] for s in range(4)], axis=1))
                low_left.append(jnp.concatenate([low_ref[s, slots[s]] for s in range(4)], axis=1))
                vals.append(jnp.where(i < 2 * (c + 1), kvw[i, 1].astype(F32), 0.0))
            dk = dot(jnp.concatenate(left, axis=0), q_all, 1, 0) * (D**-0.5)
            obuf[g, pl.ds(0, count), 0, 0] = dk.reshape(count, LAT, D).astype(BF16)
            vw = dot(jnp.concatenate(low_left, axis=0), both, 1, 0)
            obuf[g, pl.ds(0, count), 1, 0] = vw[:, :D].reshape(count, LAT, D).astype(BF16)
            vals = jnp.concatenate(vals, axis=0)
            gate_sum = jnp.sum(vals * vw[:, D:], axis=0, keepdims=True)
            gpart[pl.ds(g, 1), :] = gate_sum * (1.0 - tanh_gate * tanh_gate)

        @when(z0)
        def _():
            images(8)

        @when(z1)
        def _():
            images(16)

    def add(g, b, slot):
        rows = pl.ds(2 * b, 2)
        obuf[g, rows] = (obuf[g, rows].astype(F32) + rbuf[g, slot].astype(F32)).astype(BF16)

    def swapped(g):
        other = c * 2 + (1 - k)
        head_got(IN_K, g, kv.at[g, other, 0, 0])
        head_got(IN_V, g, kv.at[g, other, 1, 0])

    def swapped_queries(g):
        theirs = head_cols(0, g)
        head_got(IN_Q, g, qw.at[their_rows, theirs])
        head_got(IN_C, g, cw.at[their_rows, theirs])

    def gather1(g):
        for copy in own_copies(g):
            copy.wait()
        swapped(g)

        @when(jnp.logical_or(z0, x < 3))
        def _():
            message(A_R, g).start()

        @when(jnp.logical_or(z0, x == 0))
        def _():
            message(A_L, g).start()

    def gather2(g):
        @when(jnp.logical_or(z0, x > 0))
        def _():
            got(A_R, g, blk(kv, g, hi + xl))

        @when(z0)
        def _():
            message(A_ZM, g).start()
            got(A_L, g, blk(kv, g, hi + xr))
            message(A_ZP, g).start()

    def gather_own(g):
        @when(z0)
        def _():
            message(A_Z0, g).start()

    def gather_forward(g):
        @when(jnp.logical_or(x == 1, jnp.logical_and(z1, x == 2)))
        def _():
            message(A_FR, g).start()

        @when(jnp.logical_and(z0, x == 0))
        def _():
            message(A_FL, g).start()

    def gather3(g):
        @when(z1)
        def _():
            got(A_ZM, g, blk(kv, g, xl))
            message(A_HR, g).start()
            got(A_ZP, g, blk(kv, g, xr))
            message(A_HL, g).start()

    def gather4(g):
        @when(z1)
        def _():
            got(A_Z0, g, blk(kv, g, x))
            got(A_HR, g, img(kv, g, xo, 0))
            got(A_HL, g, img(kv, g, xo, 1))

        @when(jnp.logical_or(x == 2, jnp.logical_and(z1, x == 3)))
        def _():
            got(A_FR, g, blk(kv, g, hi + xo))

        @when(jnp.logical_and(z0, x == 3))
        def _():
            got(A_FL, g, blk(kv, g, xo))

        @when(jnp.logical_and(z1, x == 3))
        def _():
            got(A_L, g, blk(kv, g, 4))

    def add_half(g, b, slot, half):
        row = 2 * b + half
        obuf[g, row] = (obuf[g, row].astype(F32) + rbuf[g, slot, half].astype(F32)).astype(BF16)

    middle = jnp.logical_or(x == 1, x == 2)

    def back1(g):
        @when(z1)
        def _():
            message(R_HO, g).start()
            message(R_HR, g).start()
            message(R_HL, g).start()

        @when(x >= 2)
        def _():
            message(R_FR, g).start()

        @when(x == 3)
        def _():
            message(R_L2, g).start()

        @when(jnp.logical_and(z1, x == 3))
        def _():
            message(R_L, g).start()

    def back2(g):
        @when(z1)
        def _():
            got(R_HR, g, rhalf(g, 3, 1))
            add_half(g, xl, 3, 1)
            message(R_ZM, g).start()
            got(R_HL, g, rhalf(g, 3, 0))
            add_half(g, xr, 3, 0)
            message(R_ZP, g).start()
            got(R_HO, g, rhalf(g, 6, 1))
            add_half(g, x, 6, 1)
            message(R_Z0, g).start()

            @when(middle)
            def _():
                got(R_FR, g, rbuf.at[g, 2])
                add(g, 4 + xl, 2)

            @when(x > 0)
            def _():
                message(R_R, g).start()

    def back3(g):
        @when(z0)
        def _():
            @when(middle)
            def _():
                got(R_FR, g, rbuf.at[g, 2])
                add(g, xl, 2)

            got(R_ZM, g, rbuf.at[g, 5])
            add(g, xl, 5)
            message(R_R, g).start()
            got(R_ZP, g, rhalf(g, 6, 0))
            add_half(g, xr, 6, 0)
            message(R_L, g).start()

    def back4(g):
        def finish(*whole):
            total = obuf[g, pl.ds(2 * c, 2)].astype(F32)
            for slot in whole:
                total += rbuf[g, slot].astype(F32)
            fin[:, :, :, pl.ds(pl.multiple_of(g * D, D), D)] = total[:, :, 0].astype(BF16)

        @when(z0)
        def _():
            got(R_Z0, g, rbuf.at[g, 4])
            got(R_R, g, rbuf.at[g, 0])
            got(R_L, g, rhalf(g, 1, 0))

            @when(x > 0)
            def _():
                add_half(g, c, 1, 0)
                finish(4, 0)

            @when(x == 0)
            def _():
                got(R_L2, g, rhalf(g, 1, 1))
                finish(4, 0, 1)

        @when(z1)
        def _():
            @when(x < 3)
            def _():
                got(R_R, g, rbuf.at[g, 0])

            @when(x == 0)
            def _():
                got(R_L, g, rhalf(g, 1, 0))
                got(R_L2, g, rhalf(g, 1, 1))
                finish(0, 1)

            @when(middle)
            def _():
                finish(0)

            @when(x == 3)
            def _():
                finish()

        head_message(OUT, g).start()

    odd = lax.rem(x, 2)
    pairs = (
        across,
        at_chip(z * 4 + x + 1 - 2 * odd),
        at_chip(z * 4 + lax.rem(x + 3 + 2 * odd, 4)),
    )

    def gate_step(i):
        return pltpu.make_async_remote_copy(
            src_ref=gsum.at[i], dst_ref=gall.at[i], send_sem=gsend.at[i], recv_sem=grecv.at[i],
            device_id=pairs[i], device_id_type=MESH,
        )

    gate_local = pltpu.make_async_copy(gsum.at[3], gg_ref.at[k], glast.at[0])
    gate_remote = pltpu.make_async_remote_copy(
        src_ref=gsum.at[3], dst_ref=gate_in, send_sem=glast.at[1], recv_sem=glast.at[2],
        device_id=partner, device_id_type=MESH,
    )
    landed = [
        pltpu.make_async_copy(dq_in, qg_ref.at[:, their_cols], lland.at[0]),
        pltpu.make_async_copy(fin_in.at[0], kg_ref.at[:, their_cols], lland.at[1]),
        pltpu.make_async_copy(fin_in.at[1], vg_ref.at[:, their_cols], lland.at[2]),
        pltpu.make_async_copy(gate_in, gg_ref.at[1 - k], lland.at[3]),
    ]

    def iteration(t):
        fixed = isinstance(t, int)

        def stage(offset, run, first=0):
            if fixed:
                if offset + first <= t < CHUNKS + offset:
                    run(t - offset)
                return
            conditions = []
            if offset + first > COMPUTE:
                conditions.append(t >= offset + first)
            if offset < COMPUTE:
                conditions.append(t < CHUNKS + offset)
            if not conditions:
                run(t - offset)
            else:
                pl.when(functools.reduce(jnp.logical_and, conditions))(lambda: run(t - offset))

        def fetch(g):
            for copy in own_copies(g):
                copy.start()
            for idx in (IN_K, IN_V, IN_Q, IN_C):
                head_message(idx, g).start()

        stage(-AHEAD, lambda g: fetch(g))
        stage(0, gather1, 1)
        stage(GATHER2, gather2)
        stage(0, gather_own, 1)
        stage(GATHER2, gather_forward)
        stage(BACK2, back2)
        stage(BACK3, back3)
        stage(LAST, back4)
        if not fixed:
            gather4(t - COMPUTE)
            swapped_queries(t - COMPUTE)
            span_work(t - COMPUTE)
        stage(GATHER3, gather3)
        if not fixed:
            head_message(DQ, t - COMPUTE).start()
            products(t - COMPUTE)
            back1(t - COMPUTE)

    for t in range(COMPUTE - 1):
        iteration(t)
    prepare()
    iteration(COMPUTE - 1)
    swapped(0)

    @pl.loop(COMPUTE, COMPUTE + CHUNKS)
    def _(t):
        iteration(t)

    query_copy().start()
    gsum[0] = gpart[...]
    gate_step(0).start()
    for i in range(LAST - COMPUTE):
        iteration(COMPUTE + CHUNKS + i)
        if i < 3:
            gate_step(i).wait_recv()
            gsum[i + 1] = gsum[i] + gall[i]
            if i < 2:
                gate_step(i + 1).start()
            else:
                gate_local.start()
                gate_remote.start()

    for copy in result_copies():
        copy.start()
    swap_all(DQ, dqs.at[their_rows], dq_in).wait_recv()
    landed[0].start()
    gate_remote.wait_recv()
    landed[3].start()
    swap_all(OUT, fin.at[1 - k], fin_in).wait_recv()
    landed[1].start()
    landed[2].start()

    for i in range(3):
        gate_step(i).wait_send()

    def done(*kinds):
        for idx in kinds:
            sent = kv.at[:, pl.ds(0, 1 if idx in HALVES else 2)]
            pltpu.make_async_remote_copy(
                src_ref=sent, dst_ref=sent, send_sem=ssem.at[idx], recv_sem=rsem.at[0, idx],
                device_id=partner, device_id_type=MESH,
            ).wait_send()

    @when(z0)
    def _():
        done(A_Z0, A_ZM, A_ZP)

    @when(z1)
    def _():
        done(A_HR, A_HL, R_HR, R_HL, R_HO, R_Z0, R_ZM, R_ZP)

    @when(jnp.logical_or(z0, x < 3))
    def _():
        done(A_R)

    @when(jnp.logical_or(z0, x == 0))
    def _():
        done(A_L)

    @when(jnp.logical_or(x == 1, jnp.logical_and(z1, x == 2)))
    def _():
        done(A_FR)

    @when(jnp.logical_and(z0, x == 0))
    def _():
        done(A_FL)

    @when(x >= 2)
    def _():
        done(R_FR)

    @when(x == 3)
    def _():
        done(R_L2)

    @when(jnp.logical_or(z0, x == 3))
    def _():
        done(R_L)

    @when(jnp.logical_or(z0, x > 0))
    def _():
        done(R_R)

    swap_all(DQ, dqs.at[their_rows], dq_in).wait_send()
    swap_all(OUT, fin.at[1 - k], fin_in).wait_send()
    for idx, sent in ((IN_K, kvt.at[0]), (IN_V, kvt.at[1]), (IN_Q, qct.at[0]), (IN_C, qct.at[1])):
        pltpu.make_async_remote_copy(
            src_ref=sent, dst_ref=sent, send_sem=hsend.at[idx], recv_sem=hout.at[0],
            device_id=partner, device_id_type=MESH,
        ).wait_send()
    for copy in landed:
        copy.wait()
    pltpu.make_async_copy(qg_ref.at[:, half_cols], qg_ref.at[:, half_cols], lout.at[0]).wait()
    pltpu.make_async_copy(kg_ref.at[:, half_cols], kg_ref.at[:, half_cols], lout.at[1]).wait()
    pltpu.make_async_copy(vg_ref.at[:, half_cols], vg_ref.at[:, half_cols], lout.at[2]).wait()

    gate_local.wait()
    gate_remote.wait_send()


def place(a0, a1, a2, a3, b0, b1, b2, b3, m0, m1, m2, m3, sem):
    held = (m0, m1, m2, m3)
    into = [
        pltpu.make_async_copy(a, m, sem.at[0, i]) for i, (a, m) in enumerate(zip((a0, a1, a2, a3), held))
    ]
    out = [
        pltpu.make_async_copy(m, b, sem.at[1, i]) for i, (m, b) in enumerate(zip(held, (b0, b1, b2, b3)))
    ]
    for copy in into:
        copy.start()
    for copy, after in zip(into, out):
        copy.wait()
        after.start()
    for copy in out:
        copy.wait()


def shards(queries, keys, values, cotangent, gate, visible):
    tokens, width = queries.shape
    half = width // 2
    any_spec = pl.BlockSpec(memory_space=pl.ANY)
    hbm_spec = pl.BlockSpec(memory_space=pltpu.HBM)
    dma = pltpu.SemaphoreType.DMA
    out_shape = (
        jax.ShapeDtypeStruct((tokens, width), BF16),
        jax.ShapeDtypeStruct((LAT, width), BF16),
        jax.ShapeDtypeStruct((LAT, width), BF16),
        jax.ShapeDtypeStruct((2, CORE_HEADS, D), F32),
    )
    results = pl.pallas_call(
        kernel,
        out_shape=out_shape,
        in_specs=[hbm_spec] * 6,
        out_specs=(any_spec,) * 4,
        scratch_shapes=[
            pltpu.VMEM((2 * tokens, half), BF16),
            pltpu.VMEM((2 * tokens, half), BF16),
            pltpu.VMEM((CHUNKS, IMAGES, 2, N, LAT, D), BF16),
            pltpu.VMEM((CHUNKS, IMAGES, 2, N, LAT, D), BF16),
            pltpu.VMEM((CHUNKS, 7, 2, 2, N, LAT, D), BF16),
            pltpu.VMEM((IMAGES, 2, LAT, D), BF16),
            pltpu.VMEM((4, VIS + 1, LAT, SPAN), BF16),
            pltpu.VMEM((4, VIS + 1, LAT, SPAN), BF16),
            pltpu.VMEM((2 * tokens, 2 * D), BF16),
            pltpu.VMEM((2 * tokens, half), BF16),
            pltpu.VMEM((2, 2, LAT, half), BF16),
            pltpu.VMEM((CORE_HEADS, D), F32),
            pltpu.VMEM((3, CORE_HEADS, D), F32),
            pltpu.VMEM((4, CORE_HEADS, D), F32),
            pltpu.VMEM((1, 2, N, LAT, D), BF16),
            pltpu.VMEM((2 * CORE_HEADS, D), F32),
            pltpu.VMEM((2, tokens, half), BF16),
            pltpu.VMEM((2, LAT, half), BF16),
            pltpu.VMEM((tokens, half), BF16),
            pltpu.VMEM((2, LAT, half), BF16),
            pltpu.VMEM((CORE_HEADS, D), F32),
            pltpu.SMEM((2, 2, VIS), jnp.int32),
            pltpu.SMEM((4, IMAGES), jnp.int32),
            dma((MESSAGES,)),
            dma((CHUNKS, MESSAGES)),
            dma((6,)),
            dma((CORE_HEADS, 4)),
            dma((2,)),
            dma((CORE_HEADS, 2)),
            dma((3,)),
            dma((2,)),
            dma((4,)),
            dma((4,)),
            dma((3,)),
            dma((3,)),
            dma((4,)),
            dma((3,)),
            dma((3,)),
            dma((3,)),
        ],
        compiler_params=pltpu.CompilerParams(
            collective_id=0, has_side_effects=True, vmem_limit_bytes=63 * 1024 * 1024
        ),
        name="cross_attention_backward",
    )(queries, keys, values, cotangent, gate.reshape(2 * CORE_HEADS, D), visible)
    query_grad, key_grad, value_grad, gate_grad = pl.pallas_call(
        place,
        out_shape=out_shape,
        in_specs=[any_spec] * 4,
        out_specs=(hbm_spec,) * 4,
        scratch_shapes=[pltpu.VMEM(o.shape, o.dtype) for o in out_shape] + [dma((2, 4))],
        compiler_params=pltpu.CompilerParams(vmem_limit_bytes=63 * 1024 * 1024),
        name="place_results",
    )(*results)
    return query_grad, key_grad, value_grad, gate_grad.reshape(width)


def solution(mesh):
    placed = (
        P(("dp", "seq"), "tensor"),
        P(("dp", "seq"), "tensor"),
        P(("dp", "seq"), "tensor"),
        P(("dp", "seq"), "tensor"),
        P("tensor"),
        P(("dp", "seq"), None),
    )
    return jax.shard_map(
        shards,
        mesh=mesh,
        in_specs=placed,
        out_specs=(
            P(("dp", "seq"), "tensor"),
            P(("dp", "seq"), "tensor"),
            P(("dp", "seq"), "tensor"),
            P(("dp", "tensor")),
        ),
        check_vma=False,
    )
```

```python
import functools

import jax
import jax.numpy as jnp
from jax import lax
from jax.experimental import pallas as pl
from jax.experimental.pallas import tpu as pltpu
from jax.sharding import PartitionSpec as P

MESH = pl.DeviceIdType.MESH
D = 128
LAT = 64
SPAN = 128
VIS = 4
CORE_HEADS = 8
N = 1
CHUNKS = CORE_HEADS // N
AHEAD = 2
IMAGES = 16
GATHER2, GATHER3, COMPUTE, BACK2, BACK3, LAST = 1, 2, 3, 5, 7, 9
NEG = -1e30
EXP2_SCALE = D**-0.5 * 1.4426950408889634
F32, BF16 = jnp.float32, jnp.bfloat16

(
    A_R, A_L, A_FR, A_FL, A_Z0, A_ZM, A_ZP, A_HR, A_HL,
    R_R, R_L, R_L2, R_FR, R_Z0, R_ZM, R_ZP, R_HR, R_HL, R_HO,
) = range(19)
MESSAGES = 19
HALVES = (A_HR, A_HL, R_L, R_L2, R_ZP, R_HR, R_HL, R_HO)
DQ, OUT, IN_K, IN_V, IN_Q, IN_C = range(6)


def dot(a, b, ca, cb):
    return lax.dot_general(a, b, (((ca,), (cb,)), ((), ())), preferred_element_type=F32)


def kernel(
    q_ref, k_ref, v_ref, ct_ref, gate_hbm, vis_ref,
    qg_ref, kg_ref, vg_ref, gg_ref,
    qw, cw, kv, obuf, rbuf, kvw, sg_ref, low_ref, both_ref, dqs, fin, gpart, gall, gsum, first, gate_ref, qct, kvt, dq_in, fin_in, gate_in, vis_s, slot_s,
    ssem, rsem, hsend, hrecv, hout, lsem, lout, lfirst, lstage, lland, esend, erecv, elocal, gsend, grecv, glast,
):
    seq = lax.axis_index("seq")
    c, k = lax.div(seq, 2), lax.rem(seq, 2)
    z, x = lax.div(c, 4), lax.rem(c, 4)
    xr, xl = lax.rem(x + 1, 4), lax.rem(x + 3, 4)
    xo = lax.rem(x + 2, 4)
    z0, z1 = z == 0, z == 1

    def at_chip(chip):
        return {"seq": chip * 2 + k}

    right_chip, left_chip, across_chip = z * 4 + xr, z * 4 + xl, (1 - z) * 4 + x
    right, left, across = at_chip(right_chip), at_chip(left_chip), at_chip(across_chip)
    partner = {"seq": c * 2 + (1 - k)}

    def send(idx, g, src, dst, dev):
        return pltpu.make_async_remote_copy(
            src_ref=src, dst_ref=dst, send_sem=ssem.at[idx], recv_sem=rsem.at[g, idx],
            device_id=dev, device_id_type=MESH,
        )

    def blk(buf, g, b):
        return buf.at[g, pl.ds(2 * b, 2)]

    def img(buf, g, b, half):
        return buf.at[g, pl.ds(2 * b + half, 1)]

    def rhalf(g, slot, half):
        return rbuf.at[g, slot, pl.ds(half, 1)]

    hi = z * 4

    def message(idx, g):
        own = blk(kv, g, c)
        if idx == A_R:
            return send(idx, g, own, own, right)
        if idx == A_L:
            return send(idx, g, own, own, left)
        if idx == A_FR:
            b = blk(kv, g, hi + xl)
            return send(idx, g, b, b, right)
        if idx == A_FL:
            b = blk(kv, g, hi + xr)
            return send(idx, g, b, b, left)
        if idx == A_Z0:
            return send(idx, g, own, own, across)
        if idx == A_ZM:
            b = blk(kv, g, xl)
            return send(idx, g, b, b, across)
        if idx == A_ZP:
            b = blk(kv, g, xr)
            return send(idx, g, b, b, across)
        if idx == A_HR:
            b = img(kv, g, xl, 0)
            return send(idx, g, b, b, right)
        if idx == A_HL:
            b = img(kv, g, xr, 1)
            return send(idx, g, b, b, left)
        if idx == R_R:
            return send(idx, g, blk(obuf, g, hi + xl), rbuf.at[g, 0], left)
        if idx == R_L:
            return send(idx, g, img(obuf, g, hi + xr, 0), rhalf(g, 1, 0), right)
        if idx == R_L2:
            return send(idx, g, img(obuf, g, hi + xr, 1), rhalf(g, 1, 1), right)
        if idx == R_FR:
            return send(idx, g, blk(obuf, g, hi + xo), rbuf.at[g, 2], left)
        if idx == R_Z0:
            return send(idx, g, blk(obuf, g, x), rbuf.at[g, 4], across)
        if idx == R_ZM:
            return send(idx, g, blk(obuf, g, xl), rbuf.at[g, 5], across)
        if idx == R_ZP:
            return send(idx, g, img(obuf, g, xr, 0), rhalf(g, 6, 0), across)
        if idx == R_HR:
            return send(idx, g, img(obuf, g, xo, 1), rhalf(g, 3, 1), left)
        if idx == R_HL:
            return send(idx, g, img(obuf, g, xo, 0), rhalf(g, 3, 0), right)
        if idx == R_HO:
            return send(idx, g, img(obuf, g, xr, 1), rhalf(g, 6, 1), right)
        raise ValueError(idx)

    def swap(idx, h, src, dst):
        return pltpu.make_async_remote_copy(
            src_ref=src, dst_ref=dst, send_sem=hsend.at[idx], recv_sem=hrecv.at[h, idx - IN_K],
            device_id=partner, device_id_type=MESH,
        )

    def swap_all(idx, src, dst):
        return pltpu.make_async_remote_copy(
            src_ref=src, dst_ref=dst, send_sem=hsend.at[idx], recv_sem=hout.at[idx],
            device_id=partner, device_id_type=MESH,
        )

    def head_message(idx, h):
        g, n = h, 0
        theirs = head_cols(0, h)
        if idx == DQ:
            return swap_all(DQ, dqs.at[their_rows, theirs], dq_in.at[:, theirs])
        if idx == OUT:
            return swap_all(OUT, fin.at[1 - k, :, :, theirs], fin_in.at[:, :, theirs])
        if idx == IN_Q:
            return swap(idx, h, qct.at[0, :, theirs], qw.at[my_rows, theirs])
        if idx == IN_C:
            return swap(idx, h, qct.at[1, :, theirs], cw.at[my_rows, theirs])
        return swap(idx, h, kvt.at[idx - IN_K, :, theirs], kv.at[g, seq, idx - IN_K, n])

    def head_got(idx, h, dst):
        swap(idx, h, dst, dst).wait_recv()

    def head_cols(core, h):
        return pl.ds(pl.multiple_of((core * CORE_HEADS + h) * D, D), D)

    def got(idx, g, dst):
        send(idx, g, dst, dst, partner).wait_recv()

    def own_copies(h):
        g, n = h, 0
        mine = head_cols(k, h)
        return (
            pltpu.make_async_copy(k_ref.at[:, mine], kv.at[g, seq, 0, n], lsem.at[h, 0]),
            pltpu.make_async_copy(v_ref.at[:, mine], kv.at[g, seq, 1, n], lsem.at[h, 1]),
        )

    half_width = CORE_HEADS * D
    half_cols = pl.ds(pl.multiple_of(k * half_width, half_width), half_width)
    their_cols = pl.ds(pl.multiple_of((1 - k) * half_width, half_width), half_width)
    my_rows, their_rows = pl.ds(k * 256, 256), pl.ds((1 - k) * 256, 256)

    def result_copies():
        results = ((1, fin.at[k, 0], kg_ref), (2, fin.at[k, 1], vg_ref))
        return [
            pltpu.make_async_copy(src, ref.at[:, half_cols], lout.at[i]) for i, src, ref in results
        ]

    def query_copy():
        return pltpu.make_async_copy(dqs.at[my_rows], qg_ref.at[:, half_cols], lout.at[0])

    def early(i, src, dst):
        return pltpu.make_async_remote_copy(
            src_ref=src, dst_ref=dst, send_sem=esend.at[i], recv_sem=erecv.at[i],
            device_id=partner, device_id_type=MESH,
        )

    swaps = [
        early(0, vis_ref, vis_s.at[k]),
    ]
    theirs_staged = [
        pltpu.make_async_copy(k_ref.at[:, their_cols], kvt.at[0], lstage.at[0]),
        pltpu.make_async_copy(v_ref.at[:, their_cols], kvt.at[1], lstage.at[1]),
        pltpu.make_async_copy(q_ref.at[:, their_cols], qct.at[0], lstage.at[2]),
        pltpu.make_async_copy(ct_ref.at[:, their_cols], qct.at[1], lstage.at[3]),
    ]
    keeps = [
        pltpu.make_async_copy(vis_ref, vis_s.at[k], elocal.at[0]),
        pltpu.make_async_copy(q_ref.at[:, half_cols], qw.at[my_rows], elocal.at[1]),
        pltpu.make_async_copy(ct_ref.at[:, half_cols], cw.at[my_rows], elocal.at[2]),
        pltpu.make_async_copy(gate_hbm, gate_ref, elocal.at[3]),
    ]

    first_cols = head_cols(1 - k, 0)
    first_copies = [
        pltpu.make_async_copy(k_ref.at[:, first_cols], first.at[0, 0, 0], lfirst.at[0]),
        pltpu.make_async_copy(v_ref.at[:, first_cols], first.at[0, 1, 0], lfirst.at[1]),
    ]

    def first_messages(idx, chip):
        mine = kv.at[0, pl.ds(seq, 1)]
        return [
            pltpu.make_async_remote_copy(
                src_ref=src, dst_ref=mine, send_sem=ssem.at[idx], recv_sem=rsem.at[0, idx],
                device_id={"seq": chip * 2 + core}, device_id_type=MESH,
            )
            for src, core in ((mine, k), (first, 1 - k))
        ]

    def send_first():
        for copy in (*own_copies(0), *first_copies):
            copy.wait()

        @pl.when(jnp.logical_or(z0, x < 3))
        def _():
            for copy in first_messages(A_R, right_chip):
                copy.start()

        @pl.when(jnp.logical_or(z0, x == 0))
        def _():
            for copy in first_messages(A_L, left_chip):
                copy.start()

        @pl.when(z0)
        def _():
            for copy in first_messages(A_Z0, across_chip):
                copy.start()

    for copy in first_copies:
        copy.start()
    for h in range(AHEAD):
        for copy in own_copies(h):
            copy.start()

    for copy in theirs_staged + keeps:
        copy.start()

    barrier = pltpu.get_barrier_semaphore()
    greeted = [{"seq": chip * 2 + m} for chip in (right_chip, left_chip, across_chip) for m in (0, 1)]
    for device in greeted + [partner]:
        pl.semaphore_signal(barrier, inc=1, device_id=device, device_id_type=MESH)
    pl.semaphore_wait(barrier, 7)

    send_first()

    for copy in theirs_staged:
        copy.wait()
    for h in range(AHEAD):
        for idx in (IN_K, IN_V, IN_Q, IN_C):
            head_message(idx, h).start()

    for copy in swaps:
        copy.start()

    sg_ref[:, VIS] = jnp.zeros((4, LAT, SPAN), BF16)
    low_ref[:, VIS] = jnp.zeros((4, LAT, SPAN), BF16)

    def prepare():
        for copy in keeps:
            copy.wait()
        for copy in swaps:
            copy.wait()

        @pl.loop(0, IMAGES)
        def _(i):
            for s in range(4):
                slot = jnp.int32(VIS)
                for v in range(VIS):
                    slot = jnp.where(vis_s[s // 2, s % 2, v] == i, v, slot)
                slot_s[s, i] = slot

    def when(cond):
        return pl.when(cond)

    def span_work(h):
        cols = pl.ds(pl.multiple_of(h * D, D), D)
        kvw[...] = kv[h, :, :, 0]
        tanh_gate = jnp.tanh(gate_ref[pl.ds(k * CORE_HEADS + h, 1), :])
        q_all = qw[:, cols]
        ct_all = cw[:, cols]
        go_all = (tanh_gate * ct_all.astype(F32)).astype(BF16)
        both_ref[:, :D] = go_all
        both_ref[:, D:] = ct_all
        spans = range(4)
        listed = [[vis_s[s // 2, s % 2, v] for v in range(VIS)] for s in spans]
        ids = [[jnp.maximum(i, 0) for i in row] for row in listed]
        q = [q_all[s * SPAN : (s + 1) * SPAN] for s in spans]
        go = [go_all[s * SPAN : (s + 1) * SPAN] for s in spans]
        kl = [jnp.concatenate([kvw[i, 0] for i in ids[s]], axis=0) for s in spans]
        vl = [jnp.concatenate([kvw[i, 1] for i in ids[s]], axis=0) for s in spans]
        raw = [dot(kl[s], q[s], 1, 1) for s in spans]
        wg = [dot(vl[s], go[s], 1, 1) for s in spans]
        p, low, sg = [], [], []
        for s in spans:
            rows = [raw[s][:LAT] * EXP2_SCALE]
            for v in range(1, VIS):
                bias = jnp.where(listed[s][v] >= 0, 0.0, NEG).astype(F32)
                rows.append(raw[s][v * LAT : (v + 1) * LAT] * EXP2_SCALE + bias)
            sc = jnp.concatenate(rows, axis=0)
            e = jnp.exp2(sc - jnp.max(sc, axis=0, keepdims=True))
            p.append(e * (1.0 / jnp.sum(e, axis=0, keepdims=True)))
            low.append(p[s].astype(BF16))
        for s in spans:
            dots = jnp.sum(low[s].astype(F32) * wg[s], axis=0, keepdims=True)
            sg.append((p[s] * (wg[s] - dots)).astype(BF16))
        for s in spans:
            low_ref[s, pl.ds(0, VIS)] = low[s].reshape(VIS, LAT, SPAN)
            sg_ref[s, pl.ds(0, VIS)] = sg[s].reshape(VIS, LAT, SPAN)
        dq = [dot(sg[s], kl[s], 0, 0) * (D**-0.5) for s in spans]
        for s in spans:
            dqs[pl.ds(s * SPAN, SPAN), cols] = dq[s].astype(BF16)

    def products(g):
        tanh_gate = jnp.tanh(gate_ref[pl.ds(k * CORE_HEADS + g, 1), :])
        q_all = qw[:, pl.ds(pl.multiple_of(g * D, D), D)]
        both = both_ref[...]

        def images(count):
            left, low_left, vals = [], [], []
            for i in range(count):
                slots = [slot_s[s, i] for s in range(4)]
                left.append(jnp.concatenate([sg_ref[s, slots[s]] for s in range(4)], axis=1))
                low_left.append(jnp.concatenate([low_ref[s, slots[s]] for s in range(4)], axis=1))
                vals.append(jnp.where(i < 2 * (c + 1), kvw[i, 1].astype(F32), 0.0))
            dk = dot(jnp.concatenate(left, axis=0), q_all, 1, 0) * (D**-0.5)
            obuf[g, pl.ds(0, count), 0, 0] = dk.reshape(count, LAT, D).astype(BF16)
            vw = dot(jnp.concatenate(low_left, axis=0), both, 1, 0)
            obuf[g, pl.ds(0, count), 1, 0] = vw[:, :D].reshape(count, LAT, D).astype(BF16)
            vals = jnp.concatenate(vals, axis=0)
            gate_sum = jnp.sum(vals * vw[:, D:], axis=0, keepdims=True)
            gpart[pl.ds(g, 1), :] = gate_sum * (1.0 - tanh_gate * tanh_gate)

        @when(z0)
        def _():
            images(8)

        @when(z1)
        def _():
            images(16)

    def add(g, b, slot):
        rows = pl.ds(2 * b, 2)
        obuf[g, rows] = (obuf[g, rows].astype(F32) + rbuf[g, slot].astype(F32)).astype(BF16)

    def swapped(g):
        other = c * 2 + (1 - k)
        head_got(IN_K, g, kv.at[g, other, 0, 0])
        head_got(IN_V, g, kv.at[g, other, 1, 0])

    def swapped_queries(g):
        theirs = head_cols(0, g)
        head_got(IN_Q, g, qw.at[their_rows, theirs])
        head_got(IN_C, g, cw.at[their_rows, theirs])

    def gather1(g):
        for copy in own_copies(g):
            copy.wait()
        swapped(g)

        @when(jnp.logical_or(z0, x < 3))
        def _():
            message(A_R, g).start()

        @when(jnp.logical_or(z0, x == 0))
        def _():
            message(A_L, g).start()

    def gather2(g):
        @when(jnp.logical_or(z0, x > 0))
        def _():
            got(A_R, g, blk(kv, g, hi + xl))

        @when(z0)
        def _():
            message(A_ZM, g).start()
            got(A_L, g, blk(kv, g, hi + xr))
            message(A_ZP, g).start()

    def gather_own(g):
        @when(z0)
        def _():
            message(A_Z0, g).start()

    def gather_forward(g):
        @when(jnp.logical_or(x == 1, jnp.logical_and(z1, x == 2)))
        def _():
            message(A_FR, g).start()

        @when(jnp.logical_and(z0, x == 0))
        def _():
            message(A_FL, g).start()

    def gather3(g):
        @when(z1)
        def _():
            got(A_ZM, g, blk(kv, g, xl))
            message(A_HR, g).start()
            got(A_ZP, g, blk(kv, g, xr))
            message(A_HL, g).start()

    def gather4(g):
        @when(z1)
        def _():
            got(A_Z0, g, blk(kv, g, x))
            got(A_HR, g, img(kv, g, xo, 0))
            got(A_HL, g, img(kv, g, xo, 1))

        @when(jnp.logical_or(x == 2, jnp.logical_and(z1, x == 3)))
        def _():
            got(A_FR, g, blk(kv, g, hi + xo))

        @when(jnp.logical_and(z0, x == 3))
        def _():
            got(A_FL, g, blk(kv, g, xo))

        @when(jnp.logical_and(z1, x == 3))
        def _():
            got(A_L, g, blk(kv, g, 4))

    def add_half(g, b, slot, half):
        row = 2 * b + half
        obuf[g, row] = (obuf[g, row].astype(F32) + rbuf[g, slot, half].astype(F32)).astype(BF16)

    middle = jnp.logical_or(x == 1, x == 2)

    def back1(g):
        @when(z1)
        def _():
            message(R_HO, g).start()
            message(R_HR, g).start()
            message(R_HL, g).start()

        @when(x >= 2)
        def _():
            message(R_FR, g).start()

        @when(x == 3)
        def _():
            message(R_L2, g).start()

        @when(jnp.logical_and(z1, x == 3))
        def _():
            message(R_L, g).start()

    def back2(g):
        @when(z1)
        def _():
            got(R_HR, g, rhalf(g, 3, 1))
            add_half(g, xl, 3, 1)
            message(R_ZM, g).start()
            got(R_HL, g, rhalf(g, 3, 0))
            add_half(g, xr, 3, 0)
            message(R_ZP, g).start()
            got(R_HO, g, rhalf(g, 6, 1))
            add_half(g, x, 6, 1)
            message(R_Z0, g).start()

            @when(middle)
            def _():
                got(R_FR, g, rbuf.at[g, 2])
                add(g, 4 + xl, 2)

            @when(x > 0)
            def _():
                message(R_R, g).start()

    def back3(g):
        @when(z0)
        def _():
            @when(middle)
            def _():
                got(R_FR, g, rbuf.at[g, 2])
                add(g, xl, 2)

            got(R_ZM, g, rbuf.at[g, 5])
            add(g, xl, 5)
            message(R_R, g).start()
            got(R_ZP, g, rhalf(g, 6, 0))
            add_half(g, xr, 6, 0)
            message(R_L, g).start()

    def back4(g):
        def finish(*whole):
            total = obuf[g, pl.ds(2 * c, 2)].astype(F32)
            for slot in whole:
                total += rbuf[g, slot].astype(F32)
            fin[:, :, :, pl.ds(pl.multiple_of(g * D, D), D)] = total[:, :, 0].astype(BF16)

        @when(z0)
        def _():
            got(R_Z0, g, rbuf.at[g, 4])
            got(R_R, g, rbuf.at[g, 0])
            got(R_L, g, rhalf(g, 1, 0))

            @when(x > 0)
            def _():
                add_half(g, c, 1, 0)
                finish(4, 0)

            @when(x == 0)
            def _():
                got(R_L2, g, rhalf(g, 1, 1))
                finish(4, 0, 1)

        @when(z1)
        def _():
            @when(x < 3)
            def _():
                got(R_R, g, rbuf.at[g, 0])

            @when(x == 0)
            def _():
                got(R_L, g, rhalf(g, 1, 0))
                got(R_L2, g, rhalf(g, 1, 1))
                finish(0, 1)

            @when(middle)
            def _():
                finish(0)

            @when(x == 3)
            def _():
                finish()

        head_message(OUT, g).start()

    odd = lax.rem(x, 2)
    pairs = (
        across,
        at_chip(z * 4 + x + 1 - 2 * odd),
        at_chip(z * 4 + lax.rem(x + 3 + 2 * odd, 4)),
    )

    def gate_step(i):
        return pltpu.make_async_remote_copy(
            src_ref=gsum.at[i], dst_ref=gall.at[i], send_sem=gsend.at[i], recv_sem=grecv.at[i],
            device_id=pairs[i], device_id_type=MESH,
        )

    gate_local = pltpu.make_async_copy(gsum.at[3], gg_ref.at[k], glast.at[0])
    gate_remote = pltpu.make_async_remote_copy(
        src_ref=gsum.at[3], dst_ref=gate_in, send_sem=glast.at[1], recv_sem=glast.at[2],
        device_id=partner, device_id_type=MESH,
    )
    landed = [
        pltpu.make_async_copy(dq_in, qg_ref.at[:, their_cols], lland.at[0]),
        pltpu.make_async_copy(fin_in.at[0], kg_ref.at[:, their_cols], lland.at[1]),
        pltpu.make_async_copy(fin_in.at[1], vg_ref.at[:, their_cols], lland.at[2]),
        pltpu.make_async_copy(gate_in, gg_ref.at[1 - k], lland.at[3]),
    ]

    def iteration(t):
        fixed = isinstance(t, int)

        def stage(offset, run, first=0):
            if fixed:
                if offset + first <= t < CHUNKS + offset:
                    run(t - offset)
                return
            conditions = []
            if offset + first > COMPUTE:
                conditions.append(t >= offset + first)
            if offset < COMPUTE:
                conditions.append(t < CHUNKS + offset)
            if not conditions:
                run(t - offset)
            else:
                pl.when(functools.reduce(jnp.logical_and, conditions))(lambda: run(t - offset))

        def fetch(g):
            for copy in own_copies(g):
                copy.start()
            for idx in (IN_K, IN_V, IN_Q, IN_C):
                head_message(idx, g).start()

        stage(BACK2, back2)
        stage(-AHEAD, lambda g: fetch(g))
        stage(0, gather1, 1)
        stage(GATHER2, gather2)
        stage(0, gather_own, 1)
        stage(GATHER2, gather_forward)
        stage(BACK3, back3)
        stage(LAST, back4)
        if not fixed:
            gather4(t - COMPUTE)
            swapped_queries(t - COMPUTE)
            span_work(t - COMPUTE)
        stage(GATHER3, gather3)
        if not fixed:
            head_message(DQ, t - COMPUTE).start()
            products(t - COMPUTE)
            back1(t - COMPUTE)

    for t in range(COMPUTE - 1):
        iteration(t)
    prepare()
    iteration(COMPUTE - 1)
    swapped(0)

    @pl.loop(COMPUTE, COMPUTE + CHUNKS)
    def _(t):
        iteration(t)

    query_copy().start()
    gsum[0] = gpart[...]
    gate_step(0).start()
    for i in range(LAST - COMPUTE):
        iteration(COMPUTE + CHUNKS + i)
        if i < 3:
            gate_step(i).wait_recv()
            gsum[i + 1] = gsum[i] + gall[i]
            if i < 2:
                gate_step(i + 1).start()
            else:
                gate_local.start()
                gate_remote.start()

    for copy in result_copies():
        copy.start()
    swap_all(DQ, dqs.at[their_rows], dq_in).wait_recv()
    landed[0].start()
    gate_remote.wait_recv()
    landed[3].start()
    swap_all(OUT, fin.at[1 - k], fin_in).wait_recv()
    landed[1].start()
    landed[2].start()

    for i in range(3):
        gate_step(i).wait_send()

    def done(*kinds):
        for idx in kinds:
            sent = kv.at[:, pl.ds(0, 1 if idx in HALVES else 2)]
            pltpu.make_async_remote_copy(
                src_ref=sent, dst_ref=sent, send_sem=ssem.at[idx], recv_sem=rsem.at[0, idx],
                device_id=partner, device_id_type=MESH,
            ).wait_send()

    @when(z0)
    def _():
        done(A_Z0, A_ZM, A_ZP)

    @when(z1)
    def _():
        done(A_HR, A_HL, R_HR, R_HL, R_HO, R_Z0, R_ZM, R_ZP)

    @when(jnp.logical_or(z0, x < 3))
    def _():
        done(A_R)

    @when(jnp.logical_or(z0, x == 0))
    def _():
        done(A_L)

    @when(jnp.logical_or(x == 1, jnp.logical_and(z1, x == 2)))
    def _():
        done(A_FR)

    @when(jnp.logical_and(z0, x == 0))
    def _():
        done(A_FL)

    @when(x >= 2)
    def _():
        done(R_FR)

    @when(x == 3)
    def _():
        done(R_L2)

    @when(jnp.logical_or(z0, x == 3))
    def _():
        done(R_L)

    @when(jnp.logical_or(z0, x > 0))
    def _():
        done(R_R)

    swap_all(DQ, dqs.at[their_rows], dq_in).wait_send()
    swap_all(OUT, fin.at[1 - k], fin_in).wait_send()
    for idx, sent in ((IN_K, kvt.at[0]), (IN_V, kvt.at[1]), (IN_Q, qct.at[0]), (IN_C, qct.at[1])):
        pltpu.make_async_remote_copy(
            src_ref=sent, dst_ref=sent, send_sem=hsend.at[idx], recv_sem=hout.at[0],
            device_id=partner, device_id_type=MESH,
        ).wait_send()
    for copy in landed:
        copy.wait()
    pltpu.make_async_copy(qg_ref.at[:, half_cols], qg_ref.at[:, half_cols], lout.at[0]).wait()
    pltpu.make_async_copy(kg_ref.at[:, half_cols], kg_ref.at[:, half_cols], lout.at[1]).wait()
    pltpu.make_async_copy(vg_ref.at[:, half_cols], vg_ref.at[:, half_cols], lout.at[2]).wait()

    gate_local.wait()
    gate_remote.wait_send()


def place(a0, a1, a2, a3, b0, b1, b2, b3, m0, m1, m2, m3, sem):
    pieces = [(a0.at[r], m0.at[r], b0.at[r]) for r in (pl.ds(64 * i, 64) for i in range(4))]
    pieces += [(a1, m1, b1), (a2, m2, b2), (a3, m3, b3)]
    into = [pltpu.make_async_copy(a, m, sem.at[0, i]) for i, (a, m, _) in enumerate(pieces)]
    out = [pltpu.make_async_copy(m, b, sem.at[1, i]) for i, (_, m, b) in enumerate(pieces)]
    for copy in into:
        copy.start()
    for copy, after in zip(into, out):
        copy.wait()
        after.start()
    for copy in out:
        copy.wait()


def shards(queries, keys, values, cotangent, gate, visible):
    tokens, width = queries.shape
    half = width // 2
    any_spec = pl.BlockSpec(memory_space=pl.ANY)
    hbm_spec = pl.BlockSpec(memory_space=pltpu.HBM)
    dma = pltpu.SemaphoreType.DMA
    out_shape = (
        jax.ShapeDtypeStruct((tokens, width), BF16),
        jax.ShapeDtypeStruct((LAT, width), BF16),
        jax.ShapeDtypeStruct((LAT, width), BF16),
        jax.ShapeDtypeStruct((2, CORE_HEADS, D), F32),
    )
    results = pl.pallas_call(
        kernel,
        out_shape=out_shape,
        in_specs=[hbm_spec] * 6,
        out_specs=(any_spec,) * 4,
        scratch_shapes=[
            pltpu.VMEM((2 * tokens, half), BF16),
            pltpu.VMEM((2 * tokens, half), BF16),
            pltpu.VMEM((CHUNKS, IMAGES, 2, N, LAT, D), BF16),
            pltpu.VMEM((CHUNKS, IMAGES, 2, N, LAT, D), BF16),
            pltpu.VMEM((CHUNKS, 7, 2, 2, N, LAT, D), BF16),
            pltpu.VMEM((IMAGES, 2, LAT, D), BF16),
            pltpu.VMEM((4, VIS + 1, LAT, SPAN), BF16),
            pltpu.VMEM((4, VIS + 1, LAT, SPAN), BF16),
            pltpu.VMEM((2 * tokens, 2 * D), BF16),
            pltpu.VMEM((2 * tokens, half), BF16),
            pltpu.VMEM((2, 2, LAT, half), BF16),
            pltpu.VMEM((CORE_HEADS, D), F32),
            pltpu.VMEM((3, CORE_HEADS, D), F32),
            pltpu.VMEM((4, CORE_HEADS, D), F32),
            pltpu.VMEM((1, 2, N, LAT, D), BF16),
            pltpu.VMEM((2 * CORE_HEADS, D), F32),
            pltpu.VMEM((2, tokens, half), BF16),
            pltpu.VMEM((2, LAT, half), BF16),
            pltpu.VMEM((tokens, half), BF16),
            pltpu.VMEM((2, LAT, half), BF16),
            pltpu.VMEM((CORE_HEADS, D), F32),
            pltpu.SMEM((2, 2, VIS), jnp.int32),
            pltpu.SMEM((4, IMAGES), jnp.int32),
            dma((MESSAGES,)),
            dma((CHUNKS, MESSAGES)),
            dma((6,)),
            dma((CORE_HEADS, 4)),
            dma((2,)),
            dma((CORE_HEADS, 2)),
            dma((3,)),
            dma((2,)),
            dma((4,)),
            dma((4,)),
            dma((3,)),
            dma((3,)),
            dma((4,)),
            dma((3,)),
            dma((3,)),
            dma((3,)),
        ],
        compiler_params=pltpu.CompilerParams(
            collective_id=0, has_side_effects=True, vmem_limit_bytes=63 * 1024 * 1024
        ),
        name="cross_attention_backward",
    )(queries, keys, values, cotangent, gate.reshape(2 * CORE_HEADS, D), visible)
    query_grad, key_grad, value_grad, gate_grad = pl.pallas_call(
        place,
        out_shape=out_shape,
        in_specs=[any_spec] * 4,
        out_specs=(hbm_spec,) * 4,
        scratch_shapes=[pltpu.VMEM(o.shape, o.dtype) for o in out_shape] + [dma((2, 7))],
        compiler_params=pltpu.CompilerParams(vmem_limit_bytes=63 * 1024 * 1024),
        name="place_results",
    )(*results)
    return query_grad, key_grad, value_grad, gate_grad.reshape(width)


def solution(mesh):
    placed = (
        P(("dp", "seq"), "tensor"),
        P(("dp", "seq"), "tensor"),
        P(("dp", "seq"), "tensor"),
        P(("dp", "seq"), "tensor"),
        P("tensor"),
        P(("dp", "seq"), None),
    )
    return jax.shard_map(
        shards,
        mesh=mesh,
        in_specs=placed,
        out_specs=(
            P(("dp", "seq"), "tensor"),
            P(("dp", "seq"), "tensor"),
            P(("dp", "seq"), "tensor"),
            P(("dp", "tensor")),
        ),
        check_vma=False,
    )
```

```python
import functools

import jax
import jax.numpy as jnp
from jax import lax
from jax.experimental import pallas as pl
from jax.experimental.pallas import tpu as pltpu
from jax.sharding import PartitionSpec as P

MESH = pl.DeviceIdType.MESH
D = 128
LAT = 64
SPAN = 128
VIS = 4
CORE_HEADS = 8
N = 1
CHUNKS = CORE_HEADS // N
AHEAD = 2
IMAGES = 16
GATHER2, GATHER3, COMPUTE, BACK2, BACK3, LAST = 1, 2, 3, 5, 7, 9
NEG = -1e30
EXP2_SCALE = D**-0.5 * 1.4426950408889634
F32, BF16 = jnp.float32, jnp.bfloat16

(
    A_R, A_L, A_FR, A_FL, A_Z0, A_ZM, A_ZP, A_HR, A_HL,
    R_R, R_L, R_L2, R_FR, R_Z0, R_ZM, R_ZP, R_HR, R_HL, R_HO,
) = range(19)
MESSAGES = 19
HALVES = (A_HR, A_HL, R_L, R_L2, R_ZP, R_HR, R_HL, R_HO)
DQ, OUT, IN_K, IN_V, IN_Q, IN_C = range(6)


def dot(a, b, ca, cb):
    return lax.dot_general(a, b, (((ca,), (cb,)), ((), ())), preferred_element_type=F32)


def kernel(
    q_ref, k_ref, v_ref, ct_ref, gate_hbm, vis_ref,
    qg_ref, kg_ref, vg_ref, gg_ref,
    qw, cw, kv, obuf, rbuf, kvw, sg_ref, low_ref, both_ref, dqs, fin, gpart, gall, gsum, first, gate_ref, qct, kvt, dq_in, fin_in, gate_in, vis_s, slot_s,
    ssem, rsem, hsend, hrecv, hout, lsem, lout, lfirst, lstage, lland, esend, erecv, elocal, gsend, grecv, glast,
):
    seq = lax.axis_index("seq")
    c, k = lax.div(seq, 2), lax.rem(seq, 2)
    z, x = lax.div(c, 4), lax.rem(c, 4)
    xr, xl = lax.rem(x + 1, 4), lax.rem(x + 3, 4)
    xo = lax.rem(x + 2, 4)
    z0, z1 = z == 0, z == 1

    def at_chip(chip):
        return {"seq": chip * 2 + k}

    right_chip, left_chip, across_chip = z * 4 + xr, z * 4 + xl, (1 - z) * 4 + x
    right, left, across = at_chip(right_chip), at_chip(left_chip), at_chip(across_chip)
    partner = {"seq": c * 2 + (1 - k)}

    def send(idx, g, src, dst, dev):
        return pltpu.make_async_remote_copy(
            src_ref=src, dst_ref=dst, send_sem=ssem.at[idx], recv_sem=rsem.at[g, idx],
            device_id=dev, device_id_type=MESH,
        )

    def blk(buf, g, b):
        return buf.at[g, pl.ds(2 * b, 2)]

    def img(buf, g, b, half):
        return buf.at[g, pl.ds(2 * b + half, 1)]

    def rhalf(g, slot, half):
        return rbuf.at[g, slot, pl.ds(half, 1)]

    hi = z * 4

    def message(idx, g):
        own = blk(kv, g, c)
        if idx == A_R:
            return send(idx, g, own, own, right)
        if idx == A_L:
            return send(idx, g, own, own, left)
        if idx == A_FR:
            b = blk(kv, g, hi + xl)
            return send(idx, g, b, b, right)
        if idx == A_FL:
            b = blk(kv, g, hi + xr)
            return send(idx, g, b, b, left)
        if idx == A_Z0:
            return send(idx, g, own, own, across)
        if idx == A_ZM:
            b = blk(kv, g, xl)
            return send(idx, g, b, b, across)
        if idx == A_ZP:
            b = blk(kv, g, xr)
            return send(idx, g, b, b, across)
        if idx == A_HR:
            b = img(kv, g, xl, 0)
            return send(idx, g, b, b, right)
        if idx == A_HL:
            b = img(kv, g, xr, 1)
            return send(idx, g, b, b, left)
        if idx == R_R:
            return send(idx, g, blk(obuf, g, hi + xl), rbuf.at[g, 0], left)
        if idx == R_L:
            return send(idx, g, img(obuf, g, hi + xr, 0), rhalf(g, 1, 0), right)
        if idx == R_L2:
            return send(idx, g, img(obuf, g, hi + xr, 1), rhalf(g, 1, 1), right)
        if idx == R_FR:
            return send(idx, g, blk(obuf, g, hi + xo), rbuf.at[g, 2], left)
        if idx == R_Z0:
            return send(idx, g, blk(obuf, g, x), rbuf.at[g, 4], across)
        if idx == R_ZM:
            return send(idx, g, blk(obuf, g, xl), rbuf.at[g, 5], across)
        if idx == R_ZP:
            return send(idx, g, img(obuf, g, xr, 0), rhalf(g, 6, 0), across)
        if idx == R_HR:
            return send(idx, g, img(obuf, g, xo, 1), rhalf(g, 3, 1), left)
        if idx == R_HL:
            return send(idx, g, img(obuf, g, xo, 0), rhalf(g, 3, 0), right)
        if idx == R_HO:
            return send(idx, g, img(obuf, g, xr, 1), rhalf(g, 6, 1), right)
        raise ValueError(idx)

    def swap(idx, h, src, dst):
        return pltpu.make_async_remote_copy(
            src_ref=src, dst_ref=dst, send_sem=hsend.at[idx], recv_sem=hrecv.at[h, idx - IN_K],
            device_id=partner, device_id_type=MESH,
        )

    def swap_all(idx, src, dst):
        return pltpu.make_async_remote_copy(
            src_ref=src, dst_ref=dst, send_sem=hsend.at[idx], recv_sem=hout.at[idx],
            device_id=partner, device_id_type=MESH,
        )

    def head_message(idx, h):
        g, n = h, 0
        theirs = head_cols(0, h)
        if idx == DQ:
            return swap_all(DQ, dqs.at[their_rows, theirs], dq_in.at[:, theirs])
        if idx == OUT:
            return swap_all(OUT, fin.at[1 - k, :, :, theirs], fin_in.at[:, :, theirs])
        if idx == IN_Q:
            return swap(idx, h, qct.at[0, :, theirs], qw.at[my_rows, theirs])
        if idx == IN_C:
            return swap(idx, h, qct.at[1, :, theirs], cw.at[my_rows, theirs])
        return swap(idx, h, kvt.at[idx - IN_K, :, theirs], kv.at[g, seq, idx - IN_K, n])

    def head_got(idx, h, dst):
        swap(idx, h, dst, dst).wait_recv()

    def head_cols(core, h):
        return pl.ds(pl.multiple_of((core * CORE_HEADS + h) * D, D), D)

    def got(idx, g, dst):
        send(idx, g, dst, dst, partner).wait_recv()

    def own_copies(h):
        g, n = h, 0
        mine = head_cols(k, h)
        return (
            pltpu.make_async_copy(k_ref.at[:, mine], kv.at[g, seq, 0, n], lsem.at[h, 0]),
            pltpu.make_async_copy(v_ref.at[:, mine], kv.at[g, seq, 1, n], lsem.at[h, 1]),
        )

    half_width = CORE_HEADS * D
    half_cols = pl.ds(pl.multiple_of(k * half_width, half_width), half_width)
    their_cols = pl.ds(pl.multiple_of((1 - k) * half_width, half_width), half_width)
    my_rows, their_rows = pl.ds(k * 256, 256), pl.ds((1 - k) * 256, 256)

    def result_copies():
        results = ((1, fin.at[k, 0], kg_ref), (2, fin.at[k, 1], vg_ref))
        return [
            pltpu.make_async_copy(src, ref.at[:, half_cols], lout.at[i]) for i, src, ref in results
        ]

    def query_copy():
        return pltpu.make_async_copy(dqs.at[my_rows], qg_ref.at[:, half_cols], lout.at[0])

    def early(i, src, dst):
        return pltpu.make_async_remote_copy(
            src_ref=src, dst_ref=dst, send_sem=esend.at[i], recv_sem=erecv.at[i],
            device_id=partner, device_id_type=MESH,
        )

    swaps = [
        early(0, vis_ref, vis_s.at[k]),
    ]
    theirs_staged = [
        pltpu.make_async_copy(k_ref.at[:, their_cols], kvt.at[0], lstage.at[0]),
        pltpu.make_async_copy(v_ref.at[:, their_cols], kvt.at[1], lstage.at[1]),
        pltpu.make_async_copy(q_ref.at[:, their_cols], qct.at[0], lstage.at[2]),
        pltpu.make_async_copy(ct_ref.at[:, their_cols], qct.at[1], lstage.at[3]),
    ]
    keeps = [
        pltpu.make_async_copy(vis_ref, vis_s.at[k], elocal.at[0]),
        pltpu.make_async_copy(q_ref.at[:, half_cols], qw.at[my_rows], elocal.at[1]),
        pltpu.make_async_copy(ct_ref.at[:, half_cols], cw.at[my_rows], elocal.at[2]),
        pltpu.make_async_copy(gate_hbm, gate_ref, elocal.at[3]),
    ]

    first_cols = head_cols(1 - k, 0)
    first_copies = [
        pltpu.make_async_copy(k_ref.at[:, first_cols], first.at[0, 0, 0], lfirst.at[0]),
        pltpu.make_async_copy(v_ref.at[:, first_cols], first.at[0, 1, 0], lfirst.at[1]),
    ]

    def first_messages(idx, chip):
        mine = kv.at[0, pl.ds(seq, 1)]
        return [
            pltpu.make_async_remote_copy(
                src_ref=src, dst_ref=mine, send_sem=ssem.at[idx], recv_sem=rsem.at[0, idx],
                device_id={"seq": chip * 2 + core}, device_id_type=MESH,
            )
            for src, core in ((mine, k), (first, 1 - k))
        ]

    def send_first():
        for copy in (*own_copies(0), *first_copies):
            copy.wait()

        @pl.when(jnp.logical_or(z0, x < 3))
        def _():
            for copy in first_messages(A_R, right_chip):
                copy.start()

        @pl.when(jnp.logical_or(z0, x == 0))
        def _():
            for copy in first_messages(A_L, left_chip):
                copy.start()

        @pl.when(z0)
        def _():
            for copy in first_messages(A_Z0, across_chip):
                copy.start()

    for copy in first_copies:
        copy.start()
    for h in range(AHEAD):
        for copy in own_copies(h):
            copy.start()

    for copy in theirs_staged + keeps:
        copy.start()

    barrier = pltpu.get_barrier_semaphore()
    greeted = [{"seq": chip * 2 + m} for chip in (right_chip, left_chip, across_chip) for m in (0, 1)]
    for device in greeted + [partner]:
        pl.semaphore_signal(barrier, inc=1, device_id=device, device_id_type=MESH)
    pl.semaphore_wait(barrier, 7)

    send_first()

    for copy in theirs_staged:
        copy.wait()
    for h in range(AHEAD):
        for idx in (IN_K, IN_V, IN_Q, IN_C):
            head_message(idx, h).start()

    for copy in swaps:
        copy.start()

    sg_ref[:, VIS] = jnp.zeros((4, LAT, SPAN), BF16)
    low_ref[:, VIS] = jnp.zeros((4, LAT, SPAN), BF16)

    def prepare():
        for copy in keeps:
            copy.wait()
        for copy in swaps:
            copy.wait()

        @pl.loop(0, IMAGES)
        def _(i):
            for s in range(4):
                slot = jnp.int32(VIS)
                for v in range(VIS):
                    slot = jnp.where(vis_s[s // 2, s % 2, v] == i, v, slot)
                slot_s[s, i] = slot

    def when(cond):
        return pl.when(cond)

    def span_work(h):
        cols = pl.ds(pl.multiple_of(h * D, D), D)
        kvw[...] = kv[h, :, :, 0]
        tanh_gate = jnp.tanh(gate_ref[pl.ds(k * CORE_HEADS + h, 1), :])
        q_all = qw[:, cols]
        ct_all = cw[:, cols]
        go_all = (tanh_gate * ct_all.astype(F32)).astype(BF16)
        both_ref[:, :D] = go_all
        both_ref[:, D:] = ct_all
        spans = range(4)
        listed = [[vis_s[s // 2, s % 2, v] for v in range(VIS)] for s in spans]
        ids = [[jnp.maximum(i, 0) for i in row] for row in listed]
        q = [q_all[s * SPAN : (s + 1) * SPAN] for s in spans]
        go = [go_all[s * SPAN : (s + 1) * SPAN] for s in spans]
        kl = [jnp.concatenate([kvw[i, 0] for i in ids[s]], axis=0) for s in spans]
        vl = [jnp.concatenate([kvw[i, 1] for i in ids[s]], axis=0) for s in spans]
        raw = [dot(kl[s], q[s], 1, 1) for s in spans]
        wg = [dot(vl[s], go[s], 1, 1) for s in spans]
        p, low, sg = [], [], []
        for s in spans:
            rows = [raw[s][:LAT] * EXP2_SCALE]
            for v in range(1, VIS):
                bias = jnp.where(listed[s][v] >= 0, 0.0, NEG).astype(F32)
                rows.append(raw[s][v * LAT : (v + 1) * LAT] * EXP2_SCALE + bias)
            sc = jnp.concatenate(rows, axis=0)
            e = jnp.exp2(sc - jnp.max(sc, axis=0, keepdims=True))
            p.append(e * (1.0 / jnp.sum(e, axis=0, keepdims=True)))
            low.append(p[s].astype(BF16))
        for s in spans:
            dots = jnp.sum(low[s].astype(F32) * wg[s], axis=0, keepdims=True)
            sg.append((p[s] * (wg[s] - dots)).astype(BF16))
        for s in spans:
            low_ref[s, pl.ds(0, VIS)] = low[s].reshape(VIS, LAT, SPAN)
            sg_ref[s, pl.ds(0, VIS)] = sg[s].reshape(VIS, LAT, SPAN)
        dq = [dot(sg[s], kl[s], 0, 0) * (D**-0.5) for s in spans]
        for s in spans:
            dqs[pl.ds(s * SPAN, SPAN), cols] = dq[s].astype(BF16)

    def products(g):
        tanh_gate = jnp.tanh(gate_ref[pl.ds(k * CORE_HEADS + g, 1), :])
        q_all = qw[:, pl.ds(pl.multiple_of(g * D, D), D)]
        both = both_ref[...]

        def images(count):
            left, low_left, vals = [], [], []
            for i in range(count):
                slots = [slot_s[s, i] for s in range(4)]
                left.append(jnp.concatenate([sg_ref[s, slots[s]] for s in range(4)], axis=1))
                low_left.append(jnp.concatenate([low_ref[s, slots[s]] for s in range(4)], axis=1))
                vals.append(jnp.where(i < 2 * (c + 1), kvw[i, 1].astype(F32), 0.0))
            dk = dot(jnp.concatenate(left, axis=0), q_all, 1, 0) * (D**-0.5)
            obuf[g, pl.ds(0, count), 0, 0] = dk.reshape(count, LAT, D).astype(BF16)
            vw = dot(jnp.concatenate(low_left, axis=0), both, 1, 0)
            obuf[g, pl.ds(0, count), 1, 0] = vw[:, :D].reshape(count, LAT, D).astype(BF16)
            vals = jnp.concatenate(vals, axis=0)
            gate_sum = jnp.sum(vals * vw[:, D:], axis=0, keepdims=True)
            gpart[pl.ds(g, 1), :] = gate_sum * (1.0 - tanh_gate * tanh_gate)

        @when(z0)
        def _():
            images(8)

        @when(z1)
        def _():
            images(16)

    def add(g, b, slot):
        rows = pl.ds(2 * b, 2)
        obuf[g, rows] = (obuf[g, rows].astype(F32) + rbuf[g, slot].astype(F32)).astype(BF16)

    def swapped(g):
        other = c * 2 + (1 - k)
        head_got(IN_K, g, kv.at[g, other, 0, 0])
        head_got(IN_V, g, kv.at[g, other, 1, 0])

    def swapped_queries(g):
        theirs = head_cols(0, g)
        head_got(IN_Q, g, qw.at[their_rows, theirs])
        head_got(IN_C, g, cw.at[their_rows, theirs])

    def gather1(g):
        for copy in own_copies(g):
            copy.wait()
        swapped(g)

        @when(jnp.logical_or(z0, x < 3))
        def _():
            message(A_R, g).start()

        @when(jnp.logical_or(z0, x == 0))
        def _():
            message(A_L, g).start()

    def gather2(g):
        @when(jnp.logical_or(z0, x > 0))
        def _():
            got(A_R, g, blk(kv, g, hi + xl))

        @when(z0)
        def _():
            message(A_ZM, g).start()
            got(A_L, g, blk(kv, g, hi + xr))
            message(A_ZP, g).start()

    def gather_own(g):
        @when(z0)
        def _():
            message(A_Z0, g).start()

    def gather_forward(g):
        @when(jnp.logical_or(x == 1, jnp.logical_and(z1, x == 2)))
        def _():
            message(A_FR, g).start()

        @when(jnp.logical_and(z0, x == 0))
        def _():
            message(A_FL, g).start()

    def gather3(g):
        @when(z1)
        def _():
            got(A_ZM, g, blk(kv, g, xl))
            message(A_HR, g).start()
            got(A_ZP, g, blk(kv, g, xr))
            message(A_HL, g).start()

    def gather4(g):
        @when(z1)
        def _():
            got(A_Z0, g, blk(kv, g, x))
            got(A_HR, g, img(kv, g, xo, 0))
            got(A_HL, g, img(kv, g, xo, 1))

        @when(jnp.logical_or(x == 2, jnp.logical_and(z1, x == 3)))
        def _():
            got(A_FR, g, blk(kv, g, hi + xo))

        @when(jnp.logical_and(z0, x == 3))
        def _():
            got(A_FL, g, blk(kv, g, xo))

        @when(jnp.logical_and(z1, x == 3))
        def _():
            got(A_L, g, blk(kv, g, 4))

    def add_half(g, b, slot, half):
        row = 2 * b + half
        obuf[g, row] = (obuf[g, row].astype(F32) + rbuf[g, slot, half].astype(F32)).astype(BF16)

    middle = jnp.logical_or(x == 1, x == 2)

    def back1(g):
        @when(z1)
        def _():
            message(R_HO, g).start()
            message(R_HR, g).start()
            message(R_HL, g).start()

        @when(x >= 2)
        def _():
            message(R_FR, g).start()

        @when(x == 3)
        def _():
            message(R_L2, g).start()

        @when(jnp.logical_and(z1, x == 3))
        def _():
            message(R_L, g).start()

    def back2(g):
        @when(z1)
        def _():
            got(R_HR, g, rhalf(g, 3, 1))
            add_half(g, xl, 3, 1)
            message(R_ZM, g).start()
            got(R_HL, g, rhalf(g, 3, 0))
            add_half(g, xr, 3, 0)
            message(R_ZP, g).start()
            got(R_HO, g, rhalf(g, 6, 1))
            add_half(g, x, 6, 1)
            message(R_Z0, g).start()

            @when(middle)
            def _():
                got(R_FR, g, rbuf.at[g, 2])
                add(g, 4 + xl, 2)

            @when(x > 0)
            def _():
                message(R_R, g).start()

    def back3(g):
        @when(z0)
        def _():
            @when(middle)
            def _():
                got(R_FR, g, rbuf.at[g, 2])
                add(g, xl, 2)

            got(R_ZM, g, rbuf.at[g, 5])
            add(g, xl, 5)
            message(R_R, g).start()
            got(R_ZP, g, rhalf(g, 6, 0))
            add_half(g, xr, 6, 0)
            message(R_L, g).start()

    def back4(g):
        def finish(*whole):
            total = obuf[g, pl.ds(2 * c, 2)].astype(F32)
            for slot in whole:
                total += rbuf[g, slot].astype(F32)
            fin[:, :, :, pl.ds(pl.multiple_of(g * D, D), D)] = total[:, :, 0].astype(BF16)

        @when(z0)
        def _():
            got(R_Z0, g, rbuf.at[g, 4])
            got(R_R, g, rbuf.at[g, 0])
            got(R_L, g, rhalf(g, 1, 0))

            @when(x > 0)
            def _():
                add_half(g, c, 1, 0)
                finish(4, 0)

            @when(x == 0)
            def _():
                got(R_L2, g, rhalf(g, 1, 1))
                finish(4, 0, 1)

        @when(z1)
        def _():
            @when(x < 3)
            def _():
                got(R_R, g, rbuf.at[g, 0])

            @when(x == 0)
            def _():
                got(R_L, g, rhalf(g, 1, 0))
                got(R_L2, g, rhalf(g, 1, 1))
                finish(0, 1)

            @when(middle)
            def _():
                finish(0)

            @when(x == 3)
            def _():
                finish()

        head_message(OUT, g).start()

    odd = lax.rem(x, 2)
    pairs = (
        across,
        at_chip(z * 4 + x + 1 - 2 * odd),
        at_chip(z * 4 + lax.rem(x + 3 + 2 * odd, 4)),
    )

    def gate_step(i):
        return pltpu.make_async_remote_copy(
            src_ref=gsum.at[i], dst_ref=gall.at[i], send_sem=gsend.at[i], recv_sem=grecv.at[i],
            device_id=pairs[i], device_id_type=MESH,
        )

    gate_local = pltpu.make_async_copy(gsum.at[3], gg_ref.at[k], glast.at[0])
    gate_remote = pltpu.make_async_remote_copy(
        src_ref=gsum.at[3], dst_ref=gate_in, send_sem=glast.at[1], recv_sem=glast.at[2],
        device_id=partner, device_id_type=MESH,
    )
    landed = [
        pltpu.make_async_copy(dq_in, qg_ref.at[:, their_cols], lland.at[0]),
        pltpu.make_async_copy(fin_in.at[0], kg_ref.at[:, their_cols], lland.at[1]),
        pltpu.make_async_copy(fin_in.at[1], vg_ref.at[:, their_cols], lland.at[2]),
        pltpu.make_async_copy(gate_in, gg_ref.at[1 - k], lland.at[3]),
    ]

    def iteration(t):
        fixed = isinstance(t, int)

        def stage(offset, run, first=0):
            if fixed:
                if offset + first <= t < CHUNKS + offset:
                    run(t - offset)
                return
            conditions = []
            if offset + first > COMPUTE:
                conditions.append(t >= offset + first)
            if offset < COMPUTE:
                conditions.append(t < CHUNKS + offset)
            if not conditions:
                run(t - offset)
            else:
                pl.when(functools.reduce(jnp.logical_and, conditions))(lambda: run(t - offset))

        def fetch(g):
            for copy in own_copies(g):
                copy.start()
            for idx in (IN_K, IN_V, IN_Q, IN_C):
                head_message(idx, g).start()

        stage(BACK2, back2)
        stage(BACK3, back3)
        stage(-AHEAD, lambda g: fetch(g))
        stage(0, gather1, 1)
        stage(GATHER2, gather2)
        stage(0, gather_own, 1)
        stage(GATHER2, gather_forward)
        stage(LAST, back4)
        if not fixed:
            gather4(t - COMPUTE)
            swapped_queries(t - COMPUTE)
            span_work(t - COMPUTE)
        stage(GATHER3, gather3)
        if not fixed:
            head_message(DQ, t - COMPUTE).start()
            products(t - COMPUTE)
            back1(t - COMPUTE)

    for t in range(COMPUTE - 1):
        iteration(t)
    prepare()
    iteration(COMPUTE - 1)
    swapped(0)

    @pl.loop(COMPUTE, COMPUTE + CHUNKS)
    def _(t):
        iteration(t)

    query_copy().start()
    gsum[0] = gpart[...]
    gate_step(0).start()
    for i in range(LAST - COMPUTE):
        iteration(COMPUTE + CHUNKS + i)
        if i == 4:
            swap_all(DQ, dqs.at[their_rows], dq_in).wait_recv()
            landed[0].start()
            gate_remote.wait_recv()
            landed[3].start()
        if i < 3:
            gate_step(i).wait_recv()
            gsum[i + 1] = gsum[i] + gall[i]
            if i < 2:
                gate_step(i + 1).start()
            else:
                gate_local.start()
                gate_remote.start()

    for copy in result_copies():
        copy.start()
    swap_all(OUT, fin.at[1 - k], fin_in).wait_recv()
    landed[1].start()
    landed[2].start()

    for i in range(3):
        gate_step(i).wait_send()

    def done(*kinds):
        for idx in kinds:
            sent = kv.at[:, pl.ds(0, 1 if idx in HALVES else 2)]
            pltpu.make_async_remote_copy(
                src_ref=sent, dst_ref=sent, send_sem=ssem.at[idx], recv_sem=rsem.at[0, idx],
                device_id=partner, device_id_type=MESH,
            ).wait_send()

    @when(z0)
    def _():
        done(A_Z0, A_ZM, A_ZP)

    @when(z1)
    def _():
        done(A_HR, A_HL, R_HR, R_HL, R_HO, R_Z0, R_ZM, R_ZP)

    @when(jnp.logical_or(z0, x < 3))
    def _():
        done(A_R)

    @when(jnp.logical_or(z0, x == 0))
    def _():
        done(A_L)

    @when(jnp.logical_or(x == 1, jnp.logical_and(z1, x == 2)))
    def _():
        done(A_FR)

    @when(jnp.logical_and(z0, x == 0))
    def _():
        done(A_FL)

    @when(x >= 2)
    def _():
        done(R_FR)

    @when(x == 3)
    def _():
        done(R_L2)

    @when(jnp.logical_or(z0, x == 3))
    def _():
        done(R_L)

    @when(jnp.logical_or(z0, x > 0))
    def _():
        done(R_R)

    swap_all(DQ, dqs.at[their_rows], dq_in).wait_send()
    swap_all(OUT, fin.at[1 - k], fin_in).wait_send()
    for idx, sent in ((IN_K, kvt.at[0]), (IN_V, kvt.at[1]), (IN_Q, qct.at[0]), (IN_C, qct.at[1])):
        pltpu.make_async_remote_copy(
            src_ref=sent, dst_ref=sent, send_sem=hsend.at[idx], recv_sem=hout.at[0],
            device_id=partner, device_id_type=MESH,
        ).wait_send()
    for copy in landed:
        copy.wait()
    pltpu.make_async_copy(qg_ref.at[:, half_cols], qg_ref.at[:, half_cols], lout.at[0]).wait()
    pltpu.make_async_copy(kg_ref.at[:, half_cols], kg_ref.at[:, half_cols], lout.at[1]).wait()
    pltpu.make_async_copy(vg_ref.at[:, half_cols], vg_ref.at[:, half_cols], lout.at[2]).wait()

    gate_local.wait()
    gate_remote.wait_send()


def place(a0, a1, a2, a3, b0, b1, b2, b3, m0, m1, m2, m3, sem):
    pieces = [(a0.at[r], m0.at[r], b0.at[r]) for r in (pl.ds(64 * i, 64) for i in range(4))]
    pieces += [(a1, m1, b1), (a2, m2, b2), (a3, m3, b3)]
    into = [pltpu.make_async_copy(a, m, sem.at[0, i]) for i, (a, m, _) in enumerate(pieces)]
    out = [pltpu.make_async_copy(m, b, sem.at[1, i]) for i, (_, m, b) in enumerate(pieces)]
    for copy in into:
        copy.start()
    for copy, after in zip(into, out):
        copy.wait()
        after.start()
    for copy in out:
        copy.wait()


def shards(queries, keys, values, cotangent, gate, visible):
    tokens, width = queries.shape
    half = width // 2
    any_spec = pl.BlockSpec(memory_space=pl.ANY)
    hbm_spec = pl.BlockSpec(memory_space=pltpu.HBM)
    dma = pltpu.SemaphoreType.DMA
    out_shape = (
        jax.ShapeDtypeStruct((tokens, width), BF16),
        jax.ShapeDtypeStruct((LAT, width), BF16),
        jax.ShapeDtypeStruct((LAT, width), BF16),
        jax.ShapeDtypeStruct((2, CORE_HEADS, D), F32),
    )
    results = pl.pallas_call(
        kernel,
        out_shape=out_shape,
        in_specs=[hbm_spec] * 6,
        out_specs=(any_spec,) * 4,
        scratch_shapes=[
            pltpu.VMEM((2 * tokens, half), BF16),
            pltpu.VMEM((2 * tokens, half), BF16),
            pltpu.VMEM((CHUNKS, IMAGES, 2, N, LAT, D), BF16),
            pltpu.VMEM((CHUNKS, IMAGES, 2, N, LAT, D), BF16),
            pltpu.VMEM((CHUNKS, 7, 2, 2, N, LAT, D), BF16),
            pltpu.VMEM((IMAGES, 2, LAT, D), BF16),
            pltpu.VMEM((4, VIS + 1, LAT, SPAN), BF16),
            pltpu.VMEM((4, VIS + 1, LAT, SPAN), BF16),
            pltpu.VMEM((2 * tokens, 2 * D), BF16),
            pltpu.VMEM((2 * tokens, half), BF16),
            pltpu.VMEM((2, 2, LAT, half), BF16),
            pltpu.VMEM((CORE_HEADS, D), F32),
            pltpu.VMEM((3, CORE_HEADS, D), F32),
            pltpu.VMEM((4, CORE_HEADS, D), F32),
            pltpu.VMEM((1, 2, N, LAT, D), BF16),
            pltpu.VMEM((2 * CORE_HEADS, D), F32),
            pltpu.VMEM((2, tokens, half), BF16),
            pltpu.VMEM((2, LAT, half), BF16),
            pltpu.VMEM((tokens, half), BF16),
            pltpu.VMEM((2, LAT, half), BF16),
            pltpu.VMEM((CORE_HEADS, D), F32),
            pltpu.SMEM((2, 2, VIS), jnp.int32),
            pltpu.SMEM((4, IMAGES), jnp.int32),
            dma((MESSAGES,)),
            dma((CHUNKS, MESSAGES)),
            dma((6,)),
            dma((CORE_HEADS, 4)),
            dma((2,)),
            dma((CORE_HEADS, 2)),
            dma((3,)),
            dma((2,)),
            dma((4,)),
            dma((4,)),
            dma((3,)),
            dma((3,)),
            dma((4,)),
            dma((3,)),
            dma((3,)),
            dma((3,)),
        ],
        compiler_params=pltpu.CompilerParams(
            collective_id=0, has_side_effects=True, vmem_limit_bytes=63 * 1024 * 1024
        ),
        name="cross_attention_backward",
    )(queries, keys, values, cotangent, gate.reshape(2 * CORE_HEADS, D), visible)
    query_grad, key_grad, value_grad, gate_grad = pl.pallas_call(
        place,
        out_shape=out_shape,
        in_specs=[any_spec] * 4,
        out_specs=(hbm_spec,) * 4,
        scratch_shapes=[pltpu.VMEM(o.shape, o.dtype) for o in out_shape] + [dma((2, 7))],
        compiler_params=pltpu.CompilerParams(vmem_limit_bytes=63 * 1024 * 1024),
        name="place_results",
    )(*results)
    return query_grad, key_grad, value_grad, gate_grad.reshape(width)


def solution(mesh):
    placed = (
        P(("dp", "seq"), "tensor"),
        P(("dp", "seq"), "tensor"),
        P(("dp", "seq"), "tensor"),
        P(("dp", "seq"), "tensor"),
        P("tensor"),
        P(("dp", "seq"), None),
    )
    return jax.shard_map(
        shards,
        mesh=mesh,
        in_specs=placed,
        out_specs=(
            P(("dp", "seq"), "tensor"),
            P(("dp", "seq"), "tensor"),
            P(("dp", "seq"), "tensor"),
            P(("dp", "tensor")),
        ),
        check_vma=False,
    )
```

```python
import functools

import jax
import jax.numpy as jnp
from jax import lax
from jax.experimental import pallas as pl
from jax.experimental.pallas import tpu as pltpu
from jax.sharding import PartitionSpec as P

MESH = pl.DeviceIdType.MESH
D = 128
LAT = 64
SPAN = 128
VIS = 4
CORE_HEADS = 8
N = 1
CHUNKS = CORE_HEADS // N
AHEAD = 8
IMAGES = 16
GATHER2, GATHER3, COMPUTE, BACK2, BACK3, LAST = 1, 2, 3, 5, 7, 9
NEG = -1e30
EXP2_SCALE = D**-0.5 * 1.4426950408889634
F32, BF16 = jnp.float32, jnp.bfloat16

(
    A_R, A_L, A_FR, A_FL, A_Z0, A_ZM, A_ZP, A_HR, A_HL,
    R_R, R_L, R_L2, R_FR, R_Z0, R_ZM, R_ZP, R_HR, R_HL, R_HO,
) = range(19)
MESSAGES = 19
HALVES = (A_HR, A_HL, R_L, R_L2, R_ZP, R_HR, R_HL, R_HO)
DQ, OUT, IN_K, IN_V, IN_Q, IN_C = range(6)


def dot(a, b, ca, cb):
    return lax.dot_general(a, b, (((ca,), (cb,)), ((), ())), preferred_element_type=F32)


def kernel(
    q_ref, k_ref, v_ref, ct_ref, gate_hbm, vis_ref,
    qg_ref, kg_ref, vg_ref, gg_ref,
    qw, cw, kv, obuf, rbuf, kvw, sg_ref, low_ref, both_ref, dqs, fin, gpart, gall, gsum, first, gate_ref, qct, kvt, dq_in, fin_in, gate_in, vis_s, slot_s,
    ssem, rsem, hsend, hrecv, hout, lsem, lout, lfirst, lstage, lland, esend, erecv, elocal, gsend, grecv, glast,
):
    seq = lax.axis_index("seq")
    c, k = lax.div(seq, 2), lax.rem(seq, 2)
    z, x = lax.div(c, 4), lax.rem(c, 4)
    xr, xl = lax.rem(x + 1, 4), lax.rem(x + 3, 4)
    xo = lax.rem(x + 2, 4)
    z0, z1 = z == 0, z == 1

    def at_chip(chip):
        return {"seq": chip * 2 + k}

    right_chip, left_chip, across_chip = z * 4 + xr, z * 4 + xl, (1 - z) * 4 + x
    right, left, across = at_chip(right_chip), at_chip(left_chip), at_chip(across_chip)
    partner = {"seq": c * 2 + (1 - k)}

    def send(idx, g, src, dst, dev):
        return pltpu.make_async_remote_copy(
            src_ref=src, dst_ref=dst, send_sem=ssem.at[idx], recv_sem=rsem.at[g, idx],
            device_id=dev, device_id_type=MESH,
        )

    def blk(buf, g, b):
        return buf.at[g, pl.ds(2 * b, 2)]

    def img(buf, g, b, half):
        return buf.at[g, pl.ds(2 * b + half, 1)]

    def rhalf(g, slot, half):
        return rbuf.at[g, slot, pl.ds(half, 1)]

    hi = z * 4

    def message(idx, g):
        own = blk(kv, g, c)
        if idx == A_R:
            return send(idx, g, own, own, right)
        if idx == A_L:
            return send(idx, g, own, own, left)
        if idx == A_FR:
            b = blk(kv, g, hi + xl)
            return send(idx, g, b, b, right)
        if idx == A_FL:
            b = blk(kv, g, hi + xr)
            return send(idx, g, b, b, left)
        if idx == A_Z0:
            return send(idx, g, own, own, across)
        if idx == A_ZM:
            b = blk(kv, g, xl)
            return send(idx, g, b, b, across)
        if idx == A_ZP:
            b = blk(kv, g, xr)
            return send(idx, g, b, b, across)
        if idx == A_HR:
            b = img(kv, g, xl, 0)
            return send(idx, g, b, b, right)
        if idx == A_HL:
            b = img(kv, g, xr, 1)
            return send(idx, g, b, b, left)
        if idx == R_R:
            return send(idx, g, blk(obuf, g, hi + xl), rbuf.at[g, 0], left)
        if idx == R_L:
            return send(idx, g, img(obuf, g, hi + xr, 0), rhalf(g, 1, 0), right)
        if idx == R_L2:
            return send(idx, g, img(obuf, g, hi + xr, 1), rhalf(g, 1, 1), right)
        if idx == R_FR:
            return send(idx, g, blk(obuf, g, hi + xo), rbuf.at[g, 2], left)
        if idx == R_Z0:
            return send(idx, g, blk(obuf, g, x), rbuf.at[g, 4], across)
        if idx == R_ZM:
            return send(idx, g, blk(obuf, g, xl), rbuf.at[g, 5], across)
        if idx == R_ZP:
            return send(idx, g, img(obuf, g, xr, 0), rhalf(g, 6, 0), across)
        if idx == R_HR:
            return send(idx, g, img(obuf, g, xo, 1), rhalf(g, 3, 1), left)
        if idx == R_HL:
            return send(idx, g, img(obuf, g, xo, 0), rhalf(g, 3, 0), right)
        if idx == R_HO:
            return send(idx, g, img(obuf, g, xr, 1), rhalf(g, 6, 1), right)
        raise ValueError(idx)

    def swap(idx, h, src, dst):
        return pltpu.make_async_remote_copy(
            src_ref=src, dst_ref=dst, send_sem=hsend.at[idx], recv_sem=hrecv.at[h, idx - IN_K],
            device_id=partner, device_id_type=MESH,
        )

    def swap_all(idx, src, dst):
        return pltpu.make_async_remote_copy(
            src_ref=src, dst_ref=dst, send_sem=hsend.at[idx], recv_sem=hout.at[idx],
            device_id=partner, device_id_type=MESH,
        )

    def head_message(idx, h):
        g, n = h, 0
        theirs = head_cols(0, h)
        if idx == DQ:
            return swap_all(DQ, dqs.at[their_rows, theirs], dq_in.at[:, theirs])
        if idx == OUT:
            return swap_all(OUT, fin.at[1 - k, :, :, theirs], fin_in.at[:, :, theirs])
        if idx == IN_Q:
            return swap(idx, h, qct.at[0, :, theirs], qw.at[my_rows, theirs])
        if idx == IN_C:
            return swap(idx, h, qct.at[1, :, theirs], cw.at[my_rows, theirs])
        return swap(idx, h, kvt.at[idx - IN_K, :, theirs], kv.at[g, seq, idx - IN_K, n])

    def head_got(idx, h, dst):
        swap(idx, h, dst, dst).wait_recv()

    def head_cols(core, h):
        return pl.ds(pl.multiple_of((core * CORE_HEADS + h) * D, D), D)

    def got(idx, g, dst):
        send(idx, g, dst, dst, partner).wait_recv()

    def own_copies(h):
        g, n = h, 0
        mine = head_cols(k, h)
        return (
            pltpu.make_async_copy(k_ref.at[:, mine], kv.at[g, seq, 0, n], lsem.at[h, 0]),
            pltpu.make_async_copy(v_ref.at[:, mine], kv.at[g, seq, 1, n], lsem.at[h, 1]),
        )

    half_width = CORE_HEADS * D
    half_cols = pl.ds(pl.multiple_of(k * half_width, half_width), half_width)
    their_cols = pl.ds(pl.multiple_of((1 - k) * half_width, half_width), half_width)
    my_rows, their_rows = pl.ds(k * 256, 256), pl.ds((1 - k) * 256, 256)

    def result_copies():
        results = ((1, fin.at[k, 0], kg_ref), (2, fin.at[k, 1], vg_ref))
        return [
            pltpu.make_async_copy(src, ref.at[:, half_cols], lout.at[i]) for i, src, ref in results
        ]

    def query_copy():
        return pltpu.make_async_copy(dqs.at[my_rows], qg_ref.at[:, half_cols], lout.at[0])

    def early(i, src, dst):
        return pltpu.make_async_remote_copy(
            src_ref=src, dst_ref=dst, send_sem=esend.at[i], recv_sem=erecv.at[i],
            device_id=partner, device_id_type=MESH,
        )

    swaps = [
        early(0, vis_ref, vis_s.at[k]),
    ]
    theirs_staged = [
        pltpu.make_async_copy(k_ref.at[:, their_cols], kvt.at[0], lstage.at[0]),
        pltpu.make_async_copy(v_ref.at[:, their_cols], kvt.at[1], lstage.at[1]),
        pltpu.make_async_copy(q_ref.at[:, their_cols], qct.at[0], lstage.at[2]),
        pltpu.make_async_copy(ct_ref.at[:, their_cols], qct.at[1], lstage.at[3]),
    ]
    keeps = [
        pltpu.make_async_copy(vis_ref, vis_s.at[k], elocal.at[0]),
        pltpu.make_async_copy(q_ref.at[:, half_cols], qw.at[my_rows], elocal.at[1]),
        pltpu.make_async_copy(ct_ref.at[:, half_cols], cw.at[my_rows], elocal.at[2]),
        pltpu.make_async_copy(gate_hbm, gate_ref, elocal.at[3]),
    ]

    first_cols = head_cols(1 - k, 0)
    first_copies = [
        pltpu.make_async_copy(k_ref.at[:, first_cols], first.at[0, 0, 0], lfirst.at[0]),
        pltpu.make_async_copy(v_ref.at[:, first_cols], first.at[0, 1, 0], lfirst.at[1]),
    ]

    def first_messages(idx, chip):
        mine = kv.at[0, pl.ds(seq, 1)]
        return [
            pltpu.make_async_remote_copy(
                src_ref=src, dst_ref=mine, send_sem=ssem.at[idx], recv_sem=rsem.at[0, idx],
                device_id={"seq": chip * 2 + core}, device_id_type=MESH,
            )
            for src, core in ((mine, k), (first, 1 - k))
        ]

    def send_first():
        for copy in (*own_copies(0), *first_copies):
            copy.wait()

        @pl.when(jnp.logical_or(z0, x < 3))
        def _():
            for copy in first_messages(A_R, right_chip):
                copy.start()

        @pl.when(jnp.logical_or(z0, x == 0))
        def _():
            for copy in first_messages(A_L, left_chip):
                copy.start()

        @pl.when(z0)
        def _():
            for copy in first_messages(A_Z0, across_chip):
                copy.start()

    for copy in first_copies:
        copy.start()
    for h in range(AHEAD):
        for copy in own_copies(h):
            copy.start()

    for copy in theirs_staged + keeps:
        copy.start()

    barrier = pltpu.get_barrier_semaphore()
    greeted = [{"seq": chip * 2 + m} for chip in (right_chip, left_chip, across_chip) for m in (0, 1)]
    for device in greeted + [partner]:
        pl.semaphore_signal(barrier, inc=1, device_id=device, device_id_type=MESH)
    pl.semaphore_wait(barrier, 7)

    send_first()

    for copy in theirs_staged:
        copy.wait()
    for h in range(AHEAD):
        for idx in (IN_K, IN_V, IN_Q, IN_C):
            head_message(idx, h).start()

    for copy in swaps:
        copy.start()

    sg_ref[:, VIS] = jnp.zeros((4, LAT, SPAN), BF16)
    low_ref[:, VIS] = jnp.zeros((4, LAT, SPAN), BF16)

    def prepare():
        for copy in keeps:
            copy.wait()
        for copy in swaps:
            copy.wait()

        @pl.loop(0, IMAGES)
        def _(i):
            for s in range(4):
                slot = jnp.int32(VIS)
                for v in range(VIS):
                    slot = jnp.where(vis_s[s // 2, s % 2, v] == i, v, slot)
                slot_s[s, i] = slot

    def when(cond):
        return pl.when(cond)

    def span_work(h):
        cols = pl.ds(pl.multiple_of(h * D, D), D)
        kvw[...] = kv[h, :, :, 0]
        tanh_gate = jnp.tanh(gate_ref[pl.ds(k * CORE_HEADS + h, 1), :])
        q_all = qw[:, cols]
        ct_all = cw[:, cols]
        go_all = (tanh_gate * ct_all.astype(F32)).astype(BF16)
        both_ref[:, :D] = go_all
        both_ref[:, D:] = ct_all
        spans = range(4)
        listed = [[vis_s[s // 2, s % 2, v] for v in range(VIS)] for s in spans]
        ids = [[jnp.maximum(i, 0) for i in row] for row in listed]
        q = [q_all[s * SPAN : (s + 1) * SPAN] for s in spans]
        go = [go_all[s * SPAN : (s + 1) * SPAN] for s in spans]
        kl = [jnp.concatenate([kvw[i, 0] for i in ids[s]], axis=0) for s in spans]
        vl = [jnp.concatenate([kvw[i, 1] for i in ids[s]], axis=0) for s in spans]
        raw = [dot(kl[s], q[s], 1, 1) for s in spans]
        wg = [dot(vl[s], go[s], 1, 1) for s in spans]
        p, low, sg = [], [], []
        for s in spans:
            rows = [raw[s][:LAT] * EXP2_SCALE]
            for v in range(1, VIS):
                bias = jnp.where(listed[s][v] >= 0, 0.0, NEG).astype(F32)
                rows.append(raw[s][v * LAT : (v + 1) * LAT] * EXP2_SCALE + bias)
            sc = jnp.concatenate(rows, axis=0)
            e = jnp.exp2(sc - jnp.max(sc, axis=0, keepdims=True))
            p.append(e * (1.0 / jnp.sum(e, axis=0, keepdims=True)))
            low.append(p[s].astype(BF16))
        for s in spans:
            dots = jnp.sum(low[s].astype(F32) * wg[s], axis=0, keepdims=True)
            sg.append((p[s] * (wg[s] - dots)).astype(BF16))
        for s in spans:
            low_ref[s, pl.ds(0, VIS)] = low[s].reshape(VIS, LAT, SPAN)
            sg_ref[s, pl.ds(0, VIS)] = sg[s].reshape(VIS, LAT, SPAN)
        dq = [dot(sg[s], kl[s], 0, 0) * (D**-0.5) for s in spans]
        for s in spans:
            dqs[pl.ds(s * SPAN, SPAN), cols] = dq[s].astype(BF16)

    def products(g):
        tanh_gate = jnp.tanh(gate_ref[pl.ds(k * CORE_HEADS + g, 1), :])
        q_all = qw[:, pl.ds(pl.multiple_of(g * D, D), D)]
        both = both_ref[...]

        def images(count):
            left, low_left, vals = [], [], []
            for i in range(count):
                slots = [slot_s[s, i] for s in range(4)]
                left.append(jnp.concatenate([sg_ref[s, slots[s]] for s in range(4)], axis=1))
                low_left.append(jnp.concatenate([low_ref[s, slots[s]] for s in range(4)], axis=1))
                vals.append(jnp.where(i < 2 * (c + 1), kvw[i, 1].astype(F32), 0.0))
            dk = dot(jnp.concatenate(left, axis=0), q_all, 1, 0) * (D**-0.5)
            obuf[g, pl.ds(0, count), 0, 0] = dk.reshape(count, LAT, D).astype(BF16)
            vw = dot(jnp.concatenate(low_left, axis=0), both, 1, 0)
            obuf[g, pl.ds(0, count), 1, 0] = vw[:, :D].reshape(count, LAT, D).astype(BF16)
            vals = jnp.concatenate(vals, axis=0)
            gate_sum = jnp.sum(vals * vw[:, D:], axis=0, keepdims=True)
            gpart[pl.ds(g, 1), :] = gate_sum * (1.0 - tanh_gate * tanh_gate)

        @when(z0)
        def _():
            images(8)

        @when(z1)
        def _():
            images(16)

    def add(g, b, slot):
        rows = pl.ds(2 * b, 2)
        obuf[g, rows] = (obuf[g, rows].astype(F32) + rbuf[g, slot].astype(F32)).astype(BF16)

    def swapped(g):
        other = c * 2 + (1 - k)
        head_got(IN_K, g, kv.at[g, other, 0, 0])
        head_got(IN_V, g, kv.at[g, other, 1, 0])

    def swapped_queries(g):
        theirs = head_cols(0, g)
        head_got(IN_Q, g, qw.at[their_rows, theirs])
        head_got(IN_C, g, cw.at[their_rows, theirs])

    def gather1(g):
        for copy in own_copies(g):
            copy.wait()
        swapped(g)

        @when(jnp.logical_or(z0, x < 3))
        def _():
            message(A_R, g).start()

        @when(jnp.logical_or(z0, x == 0))
        def _():
            message(A_L, g).start()

    def gather2(g):
        @when(jnp.logical_or(z0, x > 0))
        def _():
            got(A_R, g, blk(kv, g, hi + xl))

        @when(z0)
        def _():
            message(A_ZM, g).start()
            got(A_L, g, blk(kv, g, hi + xr))
            message(A_ZP, g).start()

    def gather_own(g):
        @when(z0)
        def _():
            message(A_Z0, g).start()

    def gather_forward(g):
        @when(jnp.logical_or(x == 1, jnp.logical_and(z1, x == 2)))
        def _():
            message(A_FR, g).start()

        @when(jnp.logical_and(z0, x == 0))
        def _():
            message(A_FL, g).start()

    def gather3(g):
        @when(z1)
        def _():
            got(A_ZM, g, blk(kv, g, xl))
            message(A_HR, g).start()
            got(A_ZP, g, blk(kv, g, xr))
            message(A_HL, g).start()

    def gather4(g):
        @when(z1)
        def _():
            got(A_Z0, g, blk(kv, g, x))
            got(A_HR, g, img(kv, g, xo, 0))
            got(A_HL, g, img(kv, g, xo, 1))

        @when(jnp.logical_or(x == 2, jnp.logical_and(z1, x == 3)))
        def _():
            got(A_FR, g, blk(kv, g, hi + xo))

        @when(jnp.logical_and(z0, x == 3))
        def _():
            got(A_FL, g, blk(kv, g, xo))

        @when(jnp.logical_and(z1, x == 3))
        def _():
            got(A_L, g, blk(kv, g, 4))

    def add_half(g, b, slot, half):
        row = 2 * b + half
        obuf[g, row] = (obuf[g, row].astype(F32) + rbuf[g, slot, half].astype(F32)).astype(BF16)

    middle = jnp.logical_or(x == 1, x == 2)

    def back1(g):
        @when(z1)
        def _():
            message(R_HO, g).start()
            message(R_HR, g).start()
            message(R_HL, g).start()

        @when(x >= 2)
        def _():
            message(R_FR, g).start()

        @when(x == 3)
        def _():
            message(R_L2, g).start()

        @when(jnp.logical_and(z1, x == 3))
        def _():
            message(R_L, g).start()

    def back2(g):
        @when(z1)
        def _():
            got(R_HR, g, rhalf(g, 3, 1))
            add_half(g, xl, 3, 1)
            message(R_ZM, g).start()
            got(R_HL, g, rhalf(g, 3, 0))
            add_half(g, xr, 3, 0)
            message(R_ZP, g).start()
            got(R_HO, g, rhalf(g, 6, 1))
            add_half(g, x, 6, 1)
            message(R_Z0, g).start()

            @when(middle)
            def _():
                got(R_FR, g, rbuf.at[g, 2])
                add(g, 4 + xl, 2)

            @when(x > 0)
            def _():
                message(R_R, g).start()

    def back3(g):
        @when(z0)
        def _():
            @when(middle)
            def _():
                got(R_FR, g, rbuf.at[g, 2])
                add(g, xl, 2)

            got(R_ZM, g, rbuf.at[g, 5])
            add(g, xl, 5)
            message(R_R, g).start()
            got(R_ZP, g, rhalf(g, 6, 0))
            add_half(g, xr, 6, 0)
            message(R_L, g).start()

    def back4(g):
        def finish(*whole):
            total = obuf[g, pl.ds(2 * c, 2)].astype(F32)
            for slot in whole:
                total += rbuf[g, slot].astype(F32)
            fin[:, :, :, pl.ds(pl.multiple_of(g * D, D), D)] = total[:, :, 0].astype(BF16)

        @when(z0)
        def _():
            got(R_Z0, g, rbuf.at[g, 4])
            got(R_R, g, rbuf.at[g, 0])
            got(R_L, g, rhalf(g, 1, 0))

            @when(x > 0)
            def _():
                add_half(g, c, 1, 0)
                finish(4, 0)

            @when(x == 0)
            def _():
                got(R_L2, g, rhalf(g, 1, 1))
                finish(4, 0, 1)

        @when(z1)
        def _():
            @when(x < 3)
            def _():
                got(R_R, g, rbuf.at[g, 0])

            @when(x == 0)
            def _():
                got(R_L, g, rhalf(g, 1, 0))
                got(R_L2, g, rhalf(g, 1, 1))
                finish(0, 1)

            @when(middle)
            def _():
                finish(0)

            @when(x == 3)
            def _():
                finish()

        head_message(OUT, g).start()

    odd = lax.rem(x, 2)
    pairs = (
        across,
        at_chip(z * 4 + x + 1 - 2 * odd),
        at_chip(z * 4 + lax.rem(x + 3 + 2 * odd, 4)),
    )

    def gate_step(i):
        return pltpu.make_async_remote_copy(
            src_ref=gsum.at[i], dst_ref=gall.at[i], send_sem=gsend.at[i], recv_sem=grecv.at[i],
            device_id=pairs[i], device_id_type=MESH,
        )

    gate_local = pltpu.make_async_copy(gsum.at[3], gg_ref.at[k], glast.at[0])
    gate_remote = pltpu.make_async_remote_copy(
        src_ref=gsum.at[3], dst_ref=gate_in, send_sem=glast.at[1], recv_sem=glast.at[2],
        device_id=partner, device_id_type=MESH,
    )
    landed = [
        pltpu.make_async_copy(dq_in, qg_ref.at[:, their_cols], lland.at[0]),
        pltpu.make_async_copy(fin_in.at[0], kg_ref.at[:, their_cols], lland.at[1]),
        pltpu.make_async_copy(fin_in.at[1], vg_ref.at[:, their_cols], lland.at[2]),
        pltpu.make_async_copy(gate_in, gg_ref.at[1 - k], lland.at[3]),
    ]

    def iteration(t):
        fixed = isinstance(t, int)

        def stage(offset, run, first=0):
            if fixed:
                if offset + first <= t < CHUNKS + offset:
                    run(t - offset)
                return
            conditions = []
            if offset + first > COMPUTE:
                conditions.append(t >= offset + first)
            if offset < COMPUTE:
                conditions.append(t < CHUNKS + offset)
            if not conditions:
                run(t - offset)
            else:
                pl.when(functools.reduce(jnp.logical_and, conditions))(lambda: run(t - offset))

        def fetch(g):
            for copy in own_copies(g):
                copy.start()
            for idx in (IN_K, IN_V, IN_Q, IN_C):
                head_message(idx, g).start()

        stage(BACK2, back2)
        stage(-AHEAD, lambda g: fetch(g))
        stage(0, gather1, 1)
        stage(GATHER2, gather2)
        stage(0, gather_own, 1)
        stage(GATHER2, gather_forward)
        stage(BACK3, back3)
        stage(LAST, back4)
        if not fixed:
            gather4(t - COMPUTE)
            swapped_queries(t - COMPUTE)
            span_work(t - COMPUTE)
        stage(GATHER3, gather3)
        if not fixed:
            head_message(DQ, t - COMPUTE).start()
            products(t - COMPUTE)
            back1(t - COMPUTE)

    for t in range(COMPUTE - 1):
        iteration(t)
    prepare()
    iteration(COMPUTE - 1)
    swapped(0)

    @pl.loop(COMPUTE, COMPUTE + CHUNKS)
    def _(t):
        iteration(t)

    query_copy().start()
    gsum[0] = gpart[...]
    gate_step(0).start()
    for i in range(LAST - COMPUTE):
        iteration(COMPUTE + CHUNKS + i)
        if i < 3:
            gate_step(i).wait_recv()
            gsum[i + 1] = gsum[i] + gall[i]
            if i < 2:
                gate_step(i + 1).start()
            else:
                gate_local.start()
                gate_remote.start()

    for copy in result_copies():
        copy.start()
    swap_all(DQ, dqs.at[their_rows], dq_in).wait_recv()
    landed[0].start()
    gate_remote.wait_recv()
    landed[3].start()
    swap_all(OUT, fin.at[1 - k], fin_in).wait_recv()
    landed[1].start()
    landed[2].start()

    for i in range(3):
        gate_step(i).wait_send()

    def done(*kinds):
        for idx in kinds:
            sent = kv.at[:, pl.ds(0, 1 if idx in HALVES else 2)]
            pltpu.make_async_remote_copy(
                src_ref=sent, dst_ref=sent, send_sem=ssem.at[idx], recv_sem=rsem.at[0, idx],
                device_id=partner, device_id_type=MESH,
            ).wait_send()

    @when(z0)
    def _():
        done(A_Z0, A_ZM, A_ZP)

    @when(z1)
    def _():
        done(A_HR, A_HL, R_HR, R_HL, R_HO, R_Z0, R_ZM, R_ZP)

    @when(jnp.logical_or(z0, x < 3))
    def _():
        done(A_R)

    @when(jnp.logical_or(z0, x == 0))
    def _():
        done(A_L)

    @when(jnp.logical_or(x == 1, jnp.logical_and(z1, x == 2)))
    def _():
        done(A_FR)

    @when(jnp.logical_and(z0, x == 0))
    def _():
        done(A_FL)

    @when(x >= 2)
    def _():
        done(R_FR)

    @when(x == 3)
    def _():
        done(R_L2)

    @when(jnp.logical_or(z0, x == 3))
    def _():
        done(R_L)

    @when(jnp.logical_or(z0, x > 0))
    def _():
        done(R_R)

    swap_all(DQ, dqs.at[their_rows], dq_in).wait_send()
    swap_all(OUT, fin.at[1 - k], fin_in).wait_send()
    for idx, sent in ((IN_K, kvt.at[0]), (IN_V, kvt.at[1]), (IN_Q, qct.at[0]), (IN_C, qct.at[1])):
        pltpu.make_async_remote_copy(
            src_ref=sent, dst_ref=sent, send_sem=hsend.at[idx], recv_sem=hout.at[0],
            device_id=partner, device_id_type=MESH,
        ).wait_send()
    for copy in landed:
        copy.wait()
    pltpu.make_async_copy(qg_ref.at[:, half_cols], qg_ref.at[:, half_cols], lout.at[0]).wait()
    pltpu.make_async_copy(kg_ref.at[:, half_cols], kg_ref.at[:, half_cols], lout.at[1]).wait()
    pltpu.make_async_copy(vg_ref.at[:, half_cols], vg_ref.at[:, half_cols], lout.at[2]).wait()

    gate_local.wait()
    gate_remote.wait_send()


def place(a0, a1, a2, a3, b0, b1, b2, b3, m0, m1, m2, m3, sem):
    pieces = [(a0.at[r], m0.at[r], b0.at[r]) for r in (pl.ds(64 * i, 64) for i in range(4))]
    pieces += [(a1, m1, b1), (a2, m2, b2), (a3, m3, b3)]
    into = [pltpu.make_async_copy(a, m, sem.at[0, i]) for i, (a, m, _) in enumerate(pieces)]
    out = [pltpu.make_async_copy(m, b, sem.at[1, i]) for i, (_, m, b) in enumerate(pieces)]
    for copy in into:
        copy.start()
    for copy, after in zip(into, out):
        copy.wait()
        after.start()
    for copy in out:
        copy.wait()


def shards(queries, keys, values, cotangent, gate, visible):
    tokens, width = queries.shape
    half = width // 2
    any_spec = pl.BlockSpec(memory_space=pl.ANY)
    hbm_spec = pl.BlockSpec(memory_space=pltpu.HBM)
    dma = pltpu.SemaphoreType.DMA
    out_shape = (
        jax.ShapeDtypeStruct((tokens, width), BF16),
        jax.ShapeDtypeStruct((LAT, width), BF16),
        jax.ShapeDtypeStruct((LAT, width), BF16),
        jax.ShapeDtypeStruct((2, CORE_HEADS, D), F32),
    )
    results = pl.pallas_call(
        kernel,
        out_shape=out_shape,
        in_specs=[hbm_spec] * 6,
        out_specs=(any_spec,) * 4,
        scratch_shapes=[
            pltpu.VMEM((2 * tokens, half), BF16),
            pltpu.VMEM((2 * tokens, half), BF16),
            pltpu.VMEM((CHUNKS, IMAGES, 2, N, LAT, D), BF16),
            pltpu.VMEM((CHUNKS, IMAGES, 2, N, LAT, D), BF16),
            pltpu.VMEM((CHUNKS, 7, 2, 2, N, LAT, D), BF16),
            pltpu.VMEM((IMAGES, 2, LAT, D), BF16),
            pltpu.VMEM((4, VIS + 1, LAT, SPAN), BF16),
            pltpu.VMEM((4, VIS + 1, LAT, SPAN), BF16),
            pltpu.VMEM((2 * tokens, 2 * D), BF16),
            pltpu.VMEM((2 * tokens, half), BF16),
            pltpu.VMEM((2, 2, LAT, half), BF16),
            pltpu.VMEM((CORE_HEADS, D), F32),
            pltpu.VMEM((3, CORE_HEADS, D), F32),
            pltpu.VMEM((4, CORE_HEADS, D), F32),
            pltpu.VMEM((1, 2, N, LAT, D), BF16),
            pltpu.VMEM((2 * CORE_HEADS, D), F32),
            pltpu.VMEM((2, tokens, half), BF16),
            pltpu.VMEM((2, LAT, half), BF16),
            pltpu.VMEM((tokens, half), BF16),
            pltpu.VMEM((2, LAT, half), BF16),
            pltpu.VMEM((CORE_HEADS, D), F32),
            pltpu.SMEM((2, 2, VIS), jnp.int32),
            pltpu.SMEM((4, IMAGES), jnp.int32),
            dma((MESSAGES,)),
            dma((CHUNKS, MESSAGES)),
            dma((6,)),
            dma((CORE_HEADS, 4)),
            dma((2,)),
            dma((CORE_HEADS, 2)),
            dma((3,)),
            dma((2,)),
            dma((4,)),
            dma((4,)),
            dma((3,)),
            dma((3,)),
            dma((4,)),
            dma((3,)),
            dma((3,)),
            dma((3,)),
        ],
        compiler_params=pltpu.CompilerParams(
            collective_id=0, has_side_effects=True, vmem_limit_bytes=63 * 1024 * 1024
        ),
        name="cross_attention_backward",
    )(queries, keys, values, cotangent, gate.reshape(2 * CORE_HEADS, D), visible)
    query_grad, key_grad, value_grad, gate_grad = pl.pallas_call(
        place,
        out_shape=out_shape,
        in_specs=[any_spec] * 4,
        out_specs=(hbm_spec,) * 4,
        scratch_shapes=[pltpu.VMEM(o.shape, o.dtype) for o in out_shape] + [dma((2, 7))],
        compiler_params=pltpu.CompilerParams(vmem_limit_bytes=63 * 1024 * 1024),
        name="place_results",
    )(*results)
    return query_grad, key_grad, value_grad, gate_grad.reshape(width)


def solution(mesh):
    placed = (
        P(("dp", "seq"), "tensor"),
        P(("dp", "seq"), "tensor"),
        P(("dp", "seq"), "tensor"),
        P(("dp", "seq"), "tensor"),
        P("tensor"),
        P(("dp", "seq"), None),
    )
    return jax.shard_map(
        shards,
        mesh=mesh,
        in_specs=placed,
        out_specs=(
            P(("dp", "seq"), "tensor"),
            P(("dp", "seq"), "tensor"),
            P(("dp", "seq"), "tensor"),
            P(("dp", "tensor")),
        ),
        check_vma=False,
    )
```
